32 devices in a mesh: seq: 4 (over z), fsdp: 8 (over y, x, core).
Axes of the slice: x: 2, y: 2, z: 4, core: 2. Of those that a mesh axis runs over, the one named last changes fastest.
Arguments:
- tokens: bfloat16 [8, 4096, 1024], P('fsdp', 'seq'), may hold values from -6 to 6
- norm_gain: float32 [1024], replicated, may hold values from 0.25 to 1.75
- in_weight: bfloat16 [1024, 4384], P('fsdp'), may hold values from -0.1875 to 0.1875
- conv_weight: float32 [4, 2304], replicated, may hold values from -3 to 3
- conv_bias: float32 [2304], replicated, may hold values from -3 to 3
- dt_bias: float32 [32], replicated, may hold values from -7 to -2
- a_log: float32 [32], replicated, may hold values from -0.5 to 2.8
- skip_gain: float32 [32], replicated, may hold values from 0.5 to 1.5
- gate_gain: float32 [2048], replicated, may hold values from 0.25 to 1.75
- out_weight: bfloat16 [2048, 1024], P('fsdp'), may hold values from -0.125 to 0.125
- cotangent: bfloat16 [8, 4096, 1024], P('fsdp', 'seq'), may hold values from -6 to 6
Outputs:
- mixed: bfloat16 [8, 4096, 1024], P('fsdp', 'seq')
- grad_tokens: float32 [8, 4096, 1024], P('fsdp', 'seq')
- grad_in_weight: float32 [1024, 4384], P(('seq', 'fsdp'))
- grad_out_weight: float32 [2048, 1024], P(('seq', 'fsdp'))
- grad_norm_gain: float32 [1024], replicated
- grad_conv_weight: float32 [4, 2304], replicated
- grad_conv_bias: float32 [2304], replicated
- grad_dt_bias: float32 [32], replicated
- grad_a_log: float32 [32], replicated
- grad_skip_gain: float32 [32], replicated
- grad_gate_gain: float32 [2048], replicated
The draws below stay inside these ranges and needn't reach their ends.
All inputs are finite; a program needn't handle non-finite values.
Results may differ from the reference program's by a relative error of at most 0.0088.
Values may be sent and summed in bfloat16 or wider, within the bound.
No kernel may reach another device: no remote copies, remote signals or barrier semaphores. Data moves between devices by JAX's collectives and lax.ppermute only.
A program may use at most 448 MiB of HBM per device.

```python
import jax
import jax.numpy as jnp
from jax import lax

D = 1024
HEADS = 32
HEAD_DIM = 64
STATE = 128
CONV = 4
BLOCK = 256
INNER = 2048
XBC = 2304
PROJ = 4384
LEN = 4096
SEQS = 8


def block_levels(rng, dims, shards, smallest, top_value):
    loudness, own = 1.0, jax.random.fold_in(rng, 6)
    for axis_at, blocks in shards:
        heights = jnp.exp(jax.random.uniform(jax.random.fold_in(own, axis_at), (blocks,), jnp.float32, smallest / len(shards), top_value / len(shards)))
        loudness = loudness * jnp.repeat(heights, dims[axis_at] // blocks).reshape([-1 if axis == axis_at else 1 for axis in range(len(dims))])
    return loudness


def centred(key, extent, scale, reach, split=(), kind=jnp.bfloat16):
    loudness = block_levels(key, extent, split, -0.22, 0.18) if split else 1.0
    values = jax.random.normal(key, extent, jnp.float32) * scale * loudness
    return jnp.minimum(jnp.maximum(values, -reach), reach).astype(kind)


def setup_inputs(seed: int = 0) -> dict:
    keys = jax.random.split(jax.random.key(seed), 12)
    tokens = centred(keys[0], (SEQS, LEN, D), 1.0, 6.0, ((0, 8), (1, 4)))
    norm_gain = jnp.clip(1.0 + 0.15 * jax.random.normal(keys[1], (D,), jnp.float32), 0.25, 1.75)
    in_weight = centred(keys[2], (D, PROJ), D ** -0.5, 0.1875, ((0, 8),))
    conv_weight = centred(keys[3], (CONV, XBC), CONV ** -0.5, 3.0, (), jnp.float32)
    conv_bias = centred(keys[4], (XBC,), 0.5, 3.0, (), jnp.float32)
    dt_bias = jnp.clip(jax.random.uniform(keys[5], (HEADS,), jnp.float32, -7.0, -2.0), -7.0, -2.0)
    a_log = jnp.clip(jax.random.uniform(keys[6], (HEADS,), jnp.float32, -0.5, 2.8), -0.5, 2.8)
    skip_gain = jnp.clip(jax.random.uniform(keys[7], (HEADS,), jnp.float32, 0.5, 1.5), 0.5, 1.5)
    gate_gain = jnp.clip(1.0 + 0.15 * jax.random.normal(keys[8], (INNER,), jnp.float32), 0.25, 1.75)
    out_weight = centred(keys[9], (INNER, D), INNER ** -0.5, 0.125, ((0, 8),))
    cotangent = centred(keys[10], (SEQS, LEN, D), 1.0, 6.0, ((0, 8), (1, 4)))
    return dict(tokens=tokens, norm_gain=norm_gain, in_weight=in_weight, conv_weight=conv_weight, conv_bias=conv_bias, dt_bias=dt_bias, a_log=a_log, skip_gain=skip_gain, gate_gain=gate_gain, out_weight=out_weight, cotangent=cotangent)


epsilon = 1e-05
highest = lax.Precision.HIGHEST

@jax.custom_vjp
def low(v):
    return lax.optimization_barrier(v.astype(jnp.bfloat16)).astype(jnp.float32)

@jax.custom_vjp
def low_back(v):
    return v

def low_keep(v):
    return (low(v), None)

def low_pass(kept, grad):
    return (grad,)

def back_keep(v):
    return (v, None)

def back_low(kept, grad):
    return (low(grad),)
low.defvjp(low_keep, low_pass)
low_back.defvjp(back_keep, back_low)

def block_mixer(values, step_sizes, decay_rates, inputs, outputs, skip_terms, start_state):
    row_count = step_sizes.shape[0]
    head_count = step_sizes.shape[1]
    head_width = values.shape[1] // head_count
    state_width = inputs.shape[1]
    blocks = row_count // BLOCK
    value_blocks = values.reshape(blocks, BLOCK, head_count, head_width)
    step_blocks = step_sizes.reshape(blocks, BLOCK, head_count)
    input_blocks = inputs.reshape(blocks, BLOCK, state_width)
    output_blocks = outputs.reshape(blocks, BLOCK, state_width)
    within = jnp.cumsum(step_blocks * decay_rates, axis=1)
    totals = within[:, -1, :]
    before = jnp.cumsum(totals, axis=0) - totals
    scores = jnp.einsum('cqn,csn->cqs', output_blocks, input_blocks, precision=highest)
    causal = lax.broadcasted_iota(jnp.int32, (BLOCK, BLOCK), 0) >= lax.broadcasted_iota(jnp.int32, (BLOCK, BLOCK), 1)
    spread = within[:, :, None, :] - within[:, None, :, :]
    decays = jnp.exp(jnp.where(causal[None, :, :, None], spread, -jnp.inf))
    weighted = scores[:, :, :, None] * decays * step_blocks[:, None, :, :]
    inside = jnp.einsum('cqsh,cshp->cqhp', weighted, value_blocks, precision=highest)
    tail_weight = jnp.exp(totals[:, None, :] - within) * step_blocks
    block_states = jnp.einsum('csh,csn,cshp->chpn', tail_weight, input_blocks, value_blocks, precision=highest)
    earlier_mask = lax.broadcasted_iota(jnp.int32, (blocks, blocks), 0) > lax.broadcasted_iota(jnp.int32, (blocks, blocks), 1)
    block_gap = before[:, None, :] - before[None, :, :] - totals[None, :, :]
    block_links = jnp.exp(jnp.where(earlier_mask[:, :, None], block_gap, -jnp.inf))
    entering = jnp.einsum('kjh,jhpn->khpn', block_links, block_states, precision=highest)
    entering = entering + jnp.exp(before)[:, :, None, None] * start_state[None]
    across = jnp.einsum('cqn,chpn->cqhp', output_blocks, entering, precision=highest) * jnp.exp(within)[:, :, :, None]
    result = inside + across + skip_terms[None, None, :, None] * value_blocks
    return result.reshape(row_count, head_count * head_width)

def all_heads(values, step_sizes, decay_rates, inputs, outputs, skip_terms):
    row_count = step_sizes.shape[0]
    per_head = values.reshape(row_count, HEADS, HEAD_DIM).transpose(1, 0, 2)

    def one_head(head_item):
        head_values, head_steps, head_rate, head_skip = head_item
        start_state = jnp.zeros((1, HEAD_DIM, STATE), jnp.float32)
        return block_mixer(head_values, head_steps[:, None], head_rate[None], inputs, outputs, head_skip[None], start_state)
    results = lax.map(jax.checkpoint(one_head), (per_head, step_sizes.T, decay_rates, skip_terms))
    return results.transpose(1, 0, 2).reshape(row_count, HEADS * HEAD_DIM)

def layer(seq_input, norm_gain, in_weight, conv_weight, conv_bias, dt_bias, a_log, skip_gain, gate_gain, out_weight):
    row_count = seq_input.shape[0]
    normed = low(seq_input * lax.rsqrt(lax.optimization_barrier(jnp.mean(seq_input * seq_input, axis=1, keepdims=True)) + epsilon) * norm_gain)
    projected = low_back(jnp.dot(normed, in_weight, precision=highest, preferred_element_type=jnp.float32))
    gate_in = projected[:, :INNER]
    conv_in = low(projected[:, INNER:INNER + XBC])
    raw_steps = projected[:, INNER + XBC:]
    padded = jnp.concatenate([jnp.zeros((CONV - 1, XBC), jnp.float32), conv_in], axis=0)
    conv_out = conv_bias + jnp.zeros((row_count, XBC), jnp.float32)
    for offset in range(CONV):
        conv_out = conv_out + conv_weight[offset] * padded[offset:offset + row_count]
    activated = jax.nn.silu(conv_out)
    values = low_back(low(activated[:, :INNER]))
    shared = low(activated[:, INNER:])
    step_sizes = low_back(low(jax.nn.softplus(raw_steps + dt_bias)))
    decay_rates = -jnp.exp(a_log)
    mixer_out = all_heads(values, step_sizes, decay_rates, shared[:, :STATE], shared[:, STATE:], skip_gain)
    mixer_out = low_back(low(mixer_out))
    gated_out = mixer_out * jax.nn.silu(gate_in)
    out_in = low(gated_out * lax.rsqrt(lax.optimization_barrier(jnp.mean(gated_out * gated_out, axis=1, keepdims=True)) + epsilon) * gate_gain)
    return seq_input + jnp.dot(out_in, out_weight, precision=highest, preferred_element_type=jnp.float32)

def reference(tokens, norm_gain, in_weight, conv_weight, conv_bias, dt_bias, a_log, skip_gain, gate_gain, out_weight, cotangent):
    params = (norm_gain, in_weight.astype(jnp.float32), conv_weight, conv_bias, dt_bias, a_log, skip_gain, gate_gain, out_weight.astype(jnp.float32))

    def one_sequence(running, seq_item):
        seq_input, seq_cot = seq_item
        output, pull_back = jax.vjp(layer, seq_input.astype(jnp.float32), *params)
        grads = pull_back(seq_cot.astype(jnp.float32))
        running = jax.tree.map(jnp.add, running, tuple(grads[1:]))
        return (running, (output.astype(jnp.bfloat16), grads[0]))
    zero_grads = jax.tree.map(jnp.zeros_like, params)
    totals, (mixed, grad_tokens) = lax.scan(one_sequence, zero_grads, (tokens, cotangent))
    return (mixed, grad_tokens, totals[1], totals[8], totals[0], totals[2], totals[3], totals[4], totals[5], totals[6], totals[7])
```

```python
import functools

import jax
import jax.numpy as jnp
from jax import lax
from jax.experimental import pallas as pl
from jax.experimental.pallas import tpu as pltpu
from jax.sharding import PartitionSpec as P

ROWS = 128
LANES = 128
HALO = 16
VMEM = 48 * 1024 * 1024
LOG2E = 1.4426950408889634
epsilon = 1e-05
bf16 = jnp.bfloat16
f32 = jnp.float32
highest = lax.Precision.HIGHEST


def shifted(block, axis, distance):
    size = lax.axis_size(axis)
    route = [(i - distance, i) for i in range(size) if 0 <= i - distance < size]
    return lax.ppermute(block, axis, route)


def exchanged(block, axis, bit):
    return lax.ppermute(block, axis, [(i, i ^ bit) for i in range(lax.axis_size(axis))])


def pick(block, at, axis):
    return lax.dynamic_index_in_dim(block, at, axis, keepdims=False)


def line_sum(part):
    pieces = lax.axis_size("seq")
    me = lax.axis_index("seq")
    up = jnp.zeros_like(part[0])
    down = up
    for t in range(1, pieces):
        ahead = pick(part, jnp.clip(pieces - t + me, 0, pieces - 1), 0)
        behind = pick(part, jnp.clip(t - pieces + me, 0, pieces - 1), 0)
        up = lax.ppermute(up + ahead, "seq", [(i, i + 1) for i in range(t)])
        down = lax.ppermute(down + behind, "seq", [(pieces - 1 - i, pieces - 2 - i) for i in range(t)])
    return pick(part, me, 0).astype(f32) + up.astype(f32) + down.astype(f32)


def sum_all(vector):
    for axis in ("fsdp", "seq"):
        size = lax.axis_size(axis)
        if size & (size - 1):
            vector = lax.psum(vector, axis)
            continue
        for bit in range(size.bit_length() - 1):
            vector = vector + exchanged(vector, axis, 1 << bit)
    return vector


def sum_scatter(part, rows):
    pieces, group = lax.axis_size("seq"), lax.axis_size("fsdp")
    bits = group.bit_length() - 1
    columns = part.shape[1]
    if group != 1 << bits or bits < 1 or pieces > 8 or rows % 2:
        return lax.psum_scatter(part.astype(f32), ("seq", "fsdp"), scatter_dimension=0, tiled=True)
    me = lax.axis_index("fsdp")

    def halve(block, bit, axis):
        mine = (me >> bit) & 1
        got = exchanged(pick(block, 1 - mine, axis), "fsdp", 1 << bit)
        return pick(block, mine, axis) + got

    block = halve(part.reshape(pieces, group // 2, 2, rows, columns), 0, 2)
    halves = []
    for way in (0, 1):
        half = block[:, :, way * (rows // 2) : (way + 1) * (rows // 2)]
        half = half.reshape((pieces,) + (2,) * (bits - 1) + half.shape[2:])
        left = list(range(bits - 1, 0, -1))
        for bit in list(left) if way else left[::-1]:
            half = halve(half, bit, 1 + left.index(bit))
            left.remove(bit)
        halves.append(half)
    return line_sum(jnp.concatenate(halves, axis=1))


def mm(a, b):
    return lax.dot_general(a, b, (((1,), (0,)), ((), ())), preferred_element_type=f32)


def mm_nt(a, b):
    return lax.dot_general(a, b, (((1,), (1,)), ((), ())), preferred_element_type=f32)


def mm_tn(a, b):
    return lax.dot_general(a, b, (((0,), (0,)), ((), ())), preferred_element_type=f32)


def sigmoid(v):
    return 0.5 + 0.5 * jnp.tanh(0.5 * v)


def rows_at():
    return lax.broadcasted_iota(jnp.int32, (ROWS, LANES), 0)


def lanes_at():
    return lax.broadcasted_iota(jnp.int32, (ROWS, LANES), 1)


def slab(i):
    return slice(i * LANES, (i + 1) * LANES)


def wide(i):
    return slice(i * 2 * LANES, (i + 1) * 2 * LANES)


def halves(columns, heads):
    lane = lanes_at()
    high = columns.astype(bf16).astype(f32)
    rest = pltpu.roll(columns - high, heads, 1)
    return jnp.where(lane < heads, high, jnp.where(lane < 2 * heads, rest, 0.0)).astype(bf16)


def low_lanes():
    return (lanes_at() < LANES // 2).astype(f32).astype(bf16), (lanes_at() >= LANES // 2).astype(f32).astype(bf16)


def diagonal(block, low, high):
    return jnp.concatenate([block * low, block * high], axis=0)


def params(**more):
    return pltpu.CompilerParams(vmem_limit_bytes=VMEM, **more)


def cost(microseconds):
    return pl.CostEstimate(flops=int(microseconds * 1e9), bytes_accessed=4 * 1024 * 1024, transcendentals=0)


def whole(shape):
    return pl.BlockSpec(shape, lambda i: (0,) * len(shape))


def by_rows(width, rows=ROWS):
    return pl.BlockSpec((rows, width), lambda i: (i, 0))


def conv_kernel(span, rows, normed_ref, weight_ref, taps_ref, bias_ref, act_ref, cin_ref, held):
    part = 256
    bounds = [(0, HALO)] + [(HALO + at, part) for at in range(0, rows, part)]
    for start, size in bounds:
        block = mm(normed_ref[start : start + size, :], weight_ref[...]).astype(bf16)
        cin_ref[start : start + size, :] = block
        held[start : start + size, :] = block.astype(f32)
    for at in range(0, rows, part):
        total = jnp.broadcast_to(bias_ref[0:1, :], (part, bias_ref.shape[1]))
        for k in range(span):
            start = HALO + at - (span - 1) + k
            total = total + taps_ref[k : k + 1, :] * held[start : start + part, :]
        act_ref[at : at + part, :] = (total * sigmoid(total)).astype(bf16)


def conv_forward(normed, weight, taps, bias):
    rows, width = normed.shape[0] - HALO, normed.shape[1]
    channels = taps.shape[1]
    cols = 256
    return pl.pallas_call(
        functools.partial(conv_kernel, taps.shape[0], rows),
        grid=(channels // cols,),
        in_specs=[
            whole((rows + HALO, width)),
            pl.BlockSpec((width, cols), lambda i: (0, i)),
            pl.BlockSpec((taps.shape[0], cols), lambda i: (0, i)),
            pl.BlockSpec((1, cols), lambda i: (0, i)),
        ],
        out_specs=[
            pl.BlockSpec((rows, cols), lambda i: (0, i)),
            pl.BlockSpec((rows + HALO, cols), lambda i: (0, i)),
        ],
        out_shape=[
            jax.ShapeDtypeStruct((rows, channels), bf16),
            jax.ShapeDtypeStruct((rows + HALO, channels), bf16),
        ],
        scratch_shapes=[pltpu.VMEM((rows + HALO, cols), f32)],
        compiler_params=params(),
        name="conv_forward",
        cost_estimate=cost(14),
    )(normed, weight, taps, bias)


def steps_kernel(blocks, heads, raw_ref, bias_ref, alog_ref, step_ref, cum_ref, left_ref, right_ref, rows3):
    lane = lanes_at()
    lower = (rows_at() >= lane).astype(f32)
    rates = -jnp.exp(alog_ref[...])
    rows3[...] = jnp.zeros_like(rows3)
    for b in range(blocks):
        rows = slice(b * ROWS, (b + 1) * ROWS)
        soft = raw_ref[rows, :] + bias_ref[...]
        soft = jnp.maximum(soft, 0.0) + jnp.log1p(jnp.exp(-jnp.abs(soft)))
        step = soft.astype(bf16).astype(f32)
        step_ref[rows, :] = step
        cum = jnp.dot(lower, step * rates, precision=highest, preferred_element_type=f32)
        cum_ref[rows, :] = cum
        cum = cum * LOG2E
        parts, rest = [], cum
        for _ in range(3):
            part = rest.astype(bf16).astype(f32)
            parts.append(part)
            rest = rest - part
        left = jnp.where(lane < 3 * heads + 3, 1.0, 0.0)
        for k in (2, 1, 0):
            left = jnp.where(lane < (k + 1) * heads, pltpu.roll(parts[k], k * heads, 1), left)
        left_ref[rows, :] = left.astype(bf16)
        for k in range(3):
            flipped = -parts[k].T
            for h in range(heads):
                rows3[k : k + 1, slab(h)] = flipped[h : h + 1, :]
        right_ref[b * HALO : (b + 1) * HALO, :] = rows3[...].astype(bf16)


def steps_forward(raw, bias, a_log, heads):
    rows = raw.shape[0]
    blocks = rows // ROWS
    shape = jax.ShapeDtypeStruct((rows, LANES), f32)
    return pl.pallas_call(
        functools.partial(steps_kernel, blocks, heads),
        out_shape=[
            shape,
            shape,
            jax.ShapeDtypeStruct((rows, LANES), bf16),
            jax.ShapeDtypeStruct((blocks * HALO, heads * LANES), bf16),
        ],
        scratch_shapes=[pltpu.VMEM((HALO, heads * LANES), f32)],
        compiler_params=params(),
        name="steps_forward",
        cost_estimate=cost(6),
    )(raw, bias, a_log)


def state_kernel(heads, v_ref, b_ref, step_ref, cum_ref, etot_ref, fan_ref, x_ref, f_ref, state, tails, both):
    at = pl.program_id(0)

    @pl.when(at == 0)
    def _():
        state[...] = jnp.zeros_like(state)

    cum, step = cum_ref[...], step_ref[...]
    tail = jnp.exp(cum[ROWS - 1 :, :] - cum) * step
    both[...] = mm(jnp.concatenate([halves(step, heads), halves(tail, heads)], axis=0), fan_ref[...])
    v = v_ref[...].astype(f32)
    x_ref[...] = (v * both[:ROWS, :]).astype(bf16)
    tails[...] = (v * both[ROWS:, :]).astype(bf16)
    state[...] = etot_ref[pl.ds(at, 1), :] * state[...] + mm_tn(b_ref[...], tails[...])

    @pl.when(at == pl.num_programs(0) - 1)
    def _():
        f_ref[...] = state[...].astype(bf16)


def piece_state(act, step, cum, etot, fan, heads, inner, width):
    rows = act.shape[0]
    inputs_at = inner // width
    return pl.pallas_call(
        functools.partial(state_kernel, heads),
        grid=(rows // ROWS,),
        in_specs=[
            by_rows(inner),
            pl.BlockSpec((ROWS, width), lambda i: (i, inputs_at)),
            by_rows(LANES),
            by_rows(LANES),
            whole(etot.shape),
            whole(fan.shape),
        ],
        out_specs=[by_rows(inner), whole((width, inner))],
        out_shape=[
            jax.ShapeDtypeStruct((rows, inner), bf16),
            jax.ShapeDtypeStruct((width, inner), bf16),
        ],
        scratch_shapes=[
            pltpu.VMEM((width, inner), f32),
            pltpu.VMEM((ROWS, inner), bf16),
            pltpu.VMEM((2 * ROWS, inner), f32),
        ],
        compiler_params=params(),
        name="piece_state",
        cost_estimate=cost(6),
    )(act, act, step, cum, etot, fan)


def inside_kernel(pairs, x_ref, b_ref, c_ref, left_ref, right_ref, still_ref, y_ref, right):
    fixed = left_rows(right, still_ref, right_ref)
    low, high = low_lanes()
    scores = jnp.where(rows_at() >= lanes_at(), mm_nt(c_ref[...], b_ref[...]), 0.0)
    scores = jnp.concatenate([scores, scores], axis=1)
    left = left_ref[...]
    for i in range(pairs):
        spread = mm(left, fixed[:, wide(i)])
        weights = (scores * jnp.exp2(jnp.minimum(spread, 0.0))).astype(bf16)
        y_ref[:, slab(i)] = mm(weights, diagonal(x_ref[:, slab(i)], low, high)).astype(bf16)


def left_rows(right, still_ref, right_ref):
    @pl.when(pl.program_id(0) == 0)
    def _():
        right[...] = still_ref[...]

    own = still_ref.shape[0] - 2 * HALO
    right[own : own + HALO, :] = right_ref[...]
    return right


def inside_forward(x, act, left, right, still, inner, width):
    rows = act.shape[0]
    inputs_at = inner // width
    return pl.pallas_call(
        functools.partial(inside_kernel, inner // LANES),
        grid=(rows // ROWS,),
        in_specs=[
            by_rows(inner),
            pl.BlockSpec((ROWS, width), lambda i: (i, inputs_at)),
            pl.BlockSpec((ROWS, width), lambda i: (i, inputs_at + 1)),
            by_rows(LANES),
            by_rows(right.shape[1], HALO),
            whole(still.shape),
        ],
        out_specs=by_rows(inner),
        out_shape=jax.ShapeDtypeStruct((rows, inner), bf16),
        scratch_shapes=[pltpu.VMEM(still.shape, bf16)],
        compiler_params=params(),
        name="inside_forward",
        cost_estimate=cost(10),
    )(x, act, act, left, right, still)


def gate_kernel(
    heads,
    pairs,
    y_ref,
    v_ref,
    b_ref,
    c_ref,
    z_ref,
    gn_ref,
    step_ref,
    cum_ref,
    etot_ref,
    ebef_ref,
    skip_ref,
    gain_ref,
    start_ref,
    ones_ref,
    fan_ref,
    out_ref,
    gm_ref,
    gz_ref,
    states_ref,
    pac_ref,
    back_ref,
    ggain_ref,
    gskip_ref,
    state,
    back,
    across,
    mixer,
    gated,
    early,
    tails,
    products,
    both,
):
    at = pl.program_id(0)
    width = pairs * LANES

    @pl.when(at == 0)
    def _():
        state[...] = start_ref[...]
        back[...] = jnp.zeros_like(back)
        ggain_ref[...] = jnp.zeros_like(ggain_ref)
        gskip_ref[...] = jnp.zeros_like(gskip_ref)

    entering = state[...].astype(bf16)
    states_ref[...] = entering
    across[...] = mm(c_ref[...], entering)
    cum = cum_ref[...]
    grow = jnp.exp(cum)
    tail = jnp.exp(cum[ROWS - 1 :, :] - cum) * step_ref[...]
    both[...] = mm(jnp.concatenate([halves(grow, heads), halves(tail, heads)], axis=0), fan_ref[...])
    squares = jnp.zeros((ROWS, LANES), f32)
    meets = jnp.zeros((ROWS, LANES), f32)
    for i in range(pairs):
        s = slab(i)
        v = v_ref[:, s].astype(f32)
        ya = across[:, s] * both[:ROWS, s]
        across[:, s] = ya
        m = (y_ref[:, s].astype(f32) + ya + skip_ref[:, s] * v).astype(bf16)
        mixer[:, s] = m
        z = z_ref[:, s].astype(f32)
        product = m.astype(f32) * (z * sigmoid(z))
        gated[:, s] = product
        squares = squares + product * product
        meets = meets + gn_ref[:, s].astype(f32) * gain_ref[:, s] * product
        tails[:, s] = (v * both[ROWS:, s]).astype(bf16)
    scale = lax.rsqrt(jnp.sum(squares, axis=1, keepdims=True) / width + epsilon)
    pull = scale * scale * scale * (jnp.sum(meets, axis=1, keepdims=True) / width)
    for i in range(pairs):
        s = slab(i)
        v = v_ref[:, s].astype(f32)
        product = gated[:, s]
        unit = product * scale
        gain = gain_ref[:, s]
        gn = gn_ref[:, s].astype(f32)
        out_ref[:, s] = (unit * gain).astype(bf16)
        ggain_ref[:, s] += jnp.sum(gn * unit, axis=0, keepdims=True)
        grad = gn * gain * scale - product * pull
        z = z_ref[:, s].astype(f32)
        sig = sigmoid(z)
        gm = (grad * (z * sig)).astype(bf16)
        gm_ref[:, s] = gm
        slope = sig * (1.0 + z * (1.0 - sig))
        gz_ref[:, s] = (grad * mixer[:, s].astype(f32) * slope).astype(bf16)
        g = gm.astype(f32)
        gskip_ref[:, s] += jnp.sum(g * v, axis=0, keepdims=True)
        products[:, s] = (g * across[:, s]).astype(bf16)
        early[:, s] = (g * both[:ROWS, s]).astype(bf16)
    pac_ref[...] = mm(products[...], ones_ref[...])
    back[...] += ebef_ref[pl.ds(at, 1), :] * mm_tn(c_ref[...], early[...])
    state[...] = etot_ref[pl.ds(at, 1), :] * state[...] + mm_tn(b_ref[...], tails[...])

    @pl.when(at == pl.num_programs(0) - 1)
    def _():
        back_ref[...] = back[...].astype(bf16)


def gate_both(y, act, z, gn, step, cum, etot, ebef, skip, gain, start, ones, fan, heads, inner, width):
    rows = act.shape[0]
    inputs_at = inner // width
    blocks = rows // ROWS
    return pl.pallas_call(
        functools.partial(gate_kernel, heads, inner // LANES),
        grid=(blocks,),
        in_specs=[
            by_rows(inner),
            by_rows(inner),
            pl.BlockSpec((ROWS, width), lambda i: (i, inputs_at)),
            pl.BlockSpec((ROWS, width), lambda i: (i, inputs_at + 1)),
            by_rows(inner),
            by_rows(inner),
            by_rows(LANES),
            by_rows(LANES),
            whole(etot.shape),
            whole(ebef.shape),
            whole((1, inner)),
            whole((1, inner)),
            whole((width, inner)),
            whole((inner, LANES)),
            whole(fan.shape),
        ],
        out_specs=[
            by_rows(inner),
            by_rows(inner),
            by_rows(inner),
            by_rows(inner, width),
            by_rows(LANES),
            whole((width, inner)),
            whole((1, inner)),
            whole((1, inner)),
        ],
        out_shape=[
            jax.ShapeDtypeStruct((rows, inner), bf16),
            jax.ShapeDtypeStruct((rows, inner), bf16),
            jax.ShapeDtypeStruct((rows, inner), bf16),
            jax.ShapeDtypeStruct((blocks * width, inner), bf16),
            jax.ShapeDtypeStruct((rows, LANES), f32),
            jax.ShapeDtypeStruct((width, inner), bf16),
            jax.ShapeDtypeStruct((1, inner), f32),
            jax.ShapeDtypeStruct((1, inner), f32),
        ],
        scratch_shapes=[
            pltpu.VMEM((width, inner), f32),
            pltpu.VMEM((width, inner), f32),
            pltpu.VMEM((ROWS, inner), f32),
            pltpu.VMEM((ROWS, inner), bf16),
            pltpu.VMEM((ROWS, inner), f32),
            pltpu.VMEM((ROWS, inner), bf16),
            pltpu.VMEM((ROWS, inner), bf16),
            pltpu.VMEM((ROWS, inner), bf16),
            pltpu.VMEM((2 * ROWS, inner), f32),
        ],
        compiler_params=params(),
        name="gate_both",
        cost_estimate=cost(18),
    )(y, act, act, act, z, gn, step, cum, etot, ebef, skip, gain, start, ones, fan)


def inside_back_kernel(
    pairs, x_ref, b_ref, c_ref, g_ref, left_ref, right_ref, still_ref, taken_ref,
    dx_ref, db_ref, dc_ref, pq_ref, right, moved, late,
):
    fixed = left_rows(right, still_ref, right_ref)
    lane = lanes_at()
    low, high = low_lanes()
    raw_scores = mm_nt(b_ref[...], c_ref[...])
    scores = jnp.where(rows_at() <= lane, raw_scores, 0.0)
    strict = jnp.where(rows_at() < lane, raw_scores, 0.0)
    scores = jnp.concatenate([scores, scores], axis=1)
    strict = jnp.concatenate([strict, strict], axis=1)
    left = -left_ref[...]
    gathered = jnp.zeros((ROWS, 2 * LANES), f32)
    for i in range(pairs):
        spread = mm(left, fixed[:, wide(i)])
        decay = jnp.exp2(jnp.minimum(spread, 0.0))
        stacked = diagonal(g_ref[:, slab(i)], low, high)
        grad = mm_nt(x_ref[:, slab(i)], stacked) * decay
        gathered = gathered + grad
        moved[:, wide(i)] = (grad * strict).astype(bf16)
        dx_ref[:, slab(i)] = mm((scores * decay).astype(bf16), stacked).astype(bf16)
    late[...] = jnp.zeros_like(late)
    ones = jnp.ones((16, ROWS), bf16)
    for i in range(pairs):
        sums = mm(ones, moved[:, wide(i)])
        late[2 * i : 2 * i + 1, :] = sums[0:1, :LANES]
        late[2 * i + 1 : 2 * i + 2, :] = sums[0:1, LANES:]
    pq_ref[...] = late[...].T - mm(moved[...], taken_ref[...])
    gathered = gathered[:, :LANES] + gathered[:, LANES:]
    gathered = jnp.where(rows_at() <= lane, gathered, 0.0).astype(bf16)
    db_ref[...] = mm(gathered, c_ref[...])
    dc_ref[...] = mm_tn(gathered, b_ref[...])


def inside_backward(x, act, gm, left, right, still, taken, inner, width):
    rows = act.shape[0]
    inputs_at = inner // width
    return pl.pallas_call(
        functools.partial(inside_back_kernel, inner // LANES),
        grid=(rows // ROWS,),
        in_specs=[
            by_rows(inner),
            pl.BlockSpec((ROWS, width), lambda i: (i, inputs_at)),
            pl.BlockSpec((ROWS, width), lambda i: (i, inputs_at + 1)),
            by_rows(inner),
            by_rows(LANES),
            by_rows(right.shape[1], HALO),
            whole(still.shape),
            whole(taken.shape),
        ],
        out_specs=[by_rows(inner), by_rows(width), by_rows(width), by_rows(LANES)],
        out_shape=[
            jax.ShapeDtypeStruct((rows, inner), bf16),
            jax.ShapeDtypeStruct((rows, width), f32),
            jax.ShapeDtypeStruct((rows, width), f32),
            jax.ShapeDtypeStruct((rows, LANES), f32),
        ],
        scratch_shapes=[
            pltpu.VMEM(still.shape, bf16),
            pltpu.VMEM((ROWS, 2 * inner), bf16),
            pltpu.VMEM((LANES, ROWS), f32),
        ],
        compiler_params=params(),
        name="inside_backward",
        cost_estimate=cost(20),
    )(x, act, act, gm, left, right, still, taken)


def finish_kernel(
    heads,
    pairs,
    blocks,
    v_ref,
    x_ref,
    b_ref,
    c_ref,
    g_ref,
    dx_ref,
    db_ref,
    dc_ref,
    pq_ref,
    pac_ref,
    states_ref,
    step_ref,
    cum_ref,
    raw_ref,
    bias_ref,
    alog_ref,
    etot_ref,
    skip_ref,
    start_ref,
    ones_ref,
    fan_ref,
    gact_ref,
    graw_ref,
    gbias_ref,
    grate_ref,
    state,
    tails,
    early,
    first,
    second,
    spread,
    three,
):
    at = pl.program_id(0)
    block = blocks - 1 - at
    inner = pairs * LANES
    width = state.shape[0]

    @pl.when(at == 0)
    def _():
        state[...] = start_ref[...]
        gbias_ref[...] = jnp.zeros_like(gbias_ref)
        grate_ref[...] = jnp.zeros_like(grate_ref)

    leaving = state[...]
    leaving_low = leaving.astype(bf16)
    entering = states_ref[...]
    etot = etot_ref[pl.ds(block, 1), :]
    held = jnp.sum(leaving * entering.astype(f32), axis=0, keepdims=True) * etot
    held = mm(jnp.broadcast_to(held, (8, inner)).astype(bf16), ones_ref[...])[0:1, :]
    spread[...] = mm(b_ref[...], leaving_low)
    cum, step = cum_ref[...], step_ref[...]
    grow = jnp.exp(cum)
    tail = jnp.exp(cum[ROWS - 1 :, :] - cum)
    three[...] = mm(
        jnp.concatenate([halves(step, heads), halves(tail, heads), halves(grow, heads)], axis=0), fan_ref[...]
    )
    for i in range(pairs):
        s = slab(i)
        v = v_ref[:, s].astype(f32)
        g = g_ref[:, s].astype(f32)
        steps = three[:ROWS, s]
        x = x_ref[:, s].astype(f32)
        part_tail = three[ROWS : 2 * ROWS, s]
        more = spread[:, s] * part_tail
        dx = dx_ref[:, s].astype(f32) + more
        first[:, s] = (x * more).astype(bf16)
        second[:, s] = (v * dx).astype(bf16)
        gact_ref[:, s] = (steps * dx + skip_ref[:, s] * g).astype(bf16)
        tails[:, s] = (x * part_tail).astype(bf16)
        early[:, s] = (g * three[2 * ROWS :, s]).astype(bf16)
    gact_ref[:, inner : inner + width] = (db_ref[...] + mm_nt(tails[...], leaving_low)).astype(bf16)
    gact_ref[:, inner + width :] = (dc_ref[...] + mm_nt(early[...], entering)).astype(bf16)
    later = (rows_at() <= lanes_at()).astype(f32)
    earlier = (rows_at() > lanes_at()).astype(f32)
    gdecay = (
        jnp.dot(later, pq_ref[...] + pac_ref[...], precision=highest, preferred_element_type=f32)
        + jnp.dot(
            earlier, mm(first[...], ones_ref[...]), precision=highest, preferred_element_type=f32
        )
        + held
    )
    gstep = mm(second[...], ones_ref[...]) - jnp.exp(alog_ref[...]) * gdecay
    graw = gstep.astype(bf16).astype(f32) * sigmoid(raw_ref[...] + bias_ref[...])
    graw_ref[...] = graw.astype(bf16)
    gbias_ref[...] += jnp.sum(graw, axis=0, keepdims=True)
    grate_ref[...] += jnp.sum(step * gdecay, axis=0, keepdims=True)
    state[...] = etot * leaving + mm_tn(c_ref[...], early[...])


def mixer_finish(
    act, x, gm, dx, db, dc, pq, pac, states, step, cum, raw, bias, a_log, etot, skip, start, ones, fan, heads, inner, width
):
    rows = act.shape[0]
    blocks = rows // ROWS
    inputs_at = inner // width
    channels = act.shape[1]

    def backwards(columns, height=ROWS, column_at=0):
        return pl.BlockSpec((height, columns), lambda i: (blocks - 1 - i, column_at))

    return pl.pallas_call(
        functools.partial(finish_kernel, heads, inner // LANES, blocks),
        grid=(blocks,),
        in_specs=[
            backwards(inner),
            backwards(inner),
            backwards(width, column_at=inputs_at),
            backwards(width, column_at=inputs_at + 1),
            backwards(inner),
            backwards(inner),
            backwards(width),
            backwards(width),
            backwards(LANES),
            backwards(LANES),
            backwards(inner, width),
            backwards(LANES),
            backwards(LANES),
            backwards(LANES),
            whole((1, LANES)),
            whole((1, LANES)),
            whole(etot.shape),
            whole((1, inner)),
            whole((width, inner)),
            whole((inner, LANES)),
            whole(fan.shape),
        ],
        out_specs=[backwards(channels), backwards(LANES), whole((1, LANES)), whole((1, LANES))],
        out_shape=[
            jax.ShapeDtypeStruct((rows, channels), bf16),
            jax.ShapeDtypeStruct((rows, LANES), bf16),
            jax.ShapeDtypeStruct((1, LANES), f32),
            jax.ShapeDtypeStruct((1, LANES), f32),
        ],
        scratch_shapes=[
            pltpu.VMEM((width, inner), f32),
            pltpu.VMEM((ROWS, inner), bf16),
            pltpu.VMEM((ROWS, inner), bf16),
            pltpu.VMEM((ROWS, inner), bf16),
            pltpu.VMEM((ROWS, inner), bf16),
            pltpu.VMEM((ROWS, inner), f32),
            pltpu.VMEM((3 * ROWS, inner), f32),
        ],
        compiler_params=params(),
        name="mixer_finish",
        cost_estimate=cost(16),
    )(act, x, act, act, gm, dx, db, dc, pq, pac, states, step, cum, raw, bias, a_log, etot, skip, start, ones, fan)


def conv_back_kernel(
    span, rows, blocks, cin_ref, gact_ref, graw_ref, taps_ref, bias_ref,
    gproj_ref, gtaps_ref, gbias_ref, top_ref, rest_ref, held, grads,
):
    part = 256
    at = pl.program_id(0)

    @pl.when(at == blocks)
    def _():
        gproj_ref[...] = graw_ref[...]

    @pl.when(at < blocks)
    def _():
        held[...] = cin_ref[...].astype(f32)
        grads[rows:, :] = jnp.zeros((HALO, LANES), f32)
        gbias = jnp.zeros((1, LANES), f32)
        gtaps = [jnp.zeros((1, LANES), f32)] * span
        for start in range(0, rows, part):
            total = jnp.broadcast_to(bias_ref[0:1, :], (part, LANES))
            seen = []
            for k in range(span):
                first = HALO + start - (span - 1) + k
                seen.append(held[first : first + part, :])
                total = total + taps_ref[k : k + 1, :] * seen[k]
            sig = sigmoid(total)
            grad = gact_ref[start : start + part, :].astype(f32) * (sig * (1.0 + total * (1.0 - sig)))
            grads[start : start + part, :] = grad
            gbias = gbias + jnp.sum(grad, axis=0, keepdims=True)
            for k in range(span):
                gtaps[k] = gtaps[k] + jnp.sum(seen[k] * grad, axis=0, keepdims=True)
        gbias_ref[...] = gbias
        for k in range(span):
            gtaps_ref[k : k + 1, :] = gtaps[k]
        top_ref[...] = grads[0:8, :]
        for start in range(0, rows, part):
            total = jnp.zeros((part, LANES), f32)
            for k in range(span):
                first = start + span - 1 - k
                total = total + taps_ref[k : k + 1, :] * grads[first : first + part, :]
            gproj_ref[start : start + part, :] = total.astype(bf16)
            if start + part == rows:
                rest_ref[...] = total[part - 8 :, :]


def conv_backward(cin, gact, graw, taps, bias):
    rows, channels = gact.shape
    blocks = channels // LANES
    span = taps.shape[0]

    def columns(height):
        return pl.BlockSpec((height, LANES), lambda i: (0, jnp.minimum(i, blocks - 1)))

    return pl.pallas_call(
        functools.partial(conv_back_kernel, span, rows, blocks),
        grid=(blocks + 1,),
        in_specs=[columns(rows + HALO), columns(rows), whole((rows, LANES)), columns(span), columns(1)],
        out_specs=[
            pl.BlockSpec((rows, LANES), lambda i: (0, i)),
            columns(span),
            columns(1),
            columns(8),
            columns(8),
        ],
        out_shape=[
            jax.ShapeDtypeStruct((rows, channels + LANES), bf16),
            jax.ShapeDtypeStruct((span, channels), f32),
            jax.ShapeDtypeStruct((1, channels), f32),
            jax.ShapeDtypeStruct((8, channels), f32),
            jax.ShapeDtypeStruct((8, channels), f32),
        ],
        scratch_shapes=[pltpu.VMEM((rows + HALO, LANES), f32), pltpu.VMEM((rows + HALO, LANES), f32)],
        compiler_params=params(),
        name="conv_backward",
        cost_estimate=cost(18),
    )(cin, gact, graw, taps, bias)


def local(
    tokens,
    norm_gain,
    in_weight,
    conv_weight,
    conv_bias,
    dt_bias,
    a_log,
    skip_gain,
    gate_gain,
    out_weight,
    cotangent,
):
    tokens, incoming = tokens[0], cotangent[0]
    rows, model = tokens.shape
    heads = a_log.shape[0]
    span, channels = conv_weight.shape
    inner = gate_gain.shape[0]
    width = (channels - inner) // 2
    head_width = inner // heads
    blocks = rows // ROWS
    pad = LANES - heads

    conv_part = jnp.pad(in_weight[:, inner:], ((0, 0), (0, pad)))
    w_conv = lax.all_gather(conv_part, "fsdp", axis=0, tiled=True)
    gate_part, w_conv = lax.optimization_barrier((in_weight[:, :inner], w_conv))
    w_gate = lax.all_gather(gate_part, "fsdp", axis=0, tiled=True)
    out_weight, w_gate = lax.optimization_barrier((out_weight, w_gate))
    w_out = lax.all_gather(out_weight, "fsdp", axis=0, tiled=True)

    before = shifted(tokens[rows - HALO :], "seq", 1)
    residual = jnp.concatenate([before, tokens], axis=0).astype(f32)
    scale = lax.rsqrt(jnp.mean(residual * residual, axis=1, keepdims=True) + epsilon)
    normed = (residual * scale * norm_gain).astype(bf16)
    act, cin = conv_forward(normed, w_conv, conv_weight, conv_bias[None])
    own = normed[HALO:]
    raw = mm(own, w_conv[:, channels:])
    bias_row = jnp.pad(dt_bias, (0, pad))[None]
    alog_row = jnp.pad(a_log, (0, pad))[None]
    step, cum, left, right = steps_forward(raw, bias_row, alog_row, heads)

    totals = cum.reshape(blocks, ROWS, LANES)[:, -1, :heads]
    befores = jnp.cumsum(totals, axis=0) - totals
    etot = jnp.repeat(jnp.exp(totals), head_width, axis=1)
    ebef = jnp.repeat(jnp.exp(befores), head_width, axis=1)
    skip = jnp.repeat(skip_gain, head_width)[None]
    ones = (
        lax.broadcasted_iota(jnp.int32, (inner, LANES), 0) // head_width
        == lax.broadcasted_iota(jnp.int32, (inner, LANES), 1)
    ).astype(bf16)

    def fanned(count, each):
        row = lax.broadcasted_iota(jnp.int32, (LANES, count), 0)
        column = lax.broadcasted_iota(jnp.int32, (LANES, count), 1)
        return ((row < 3 * heads) & (row % heads == column // each)).astype(bf16)

    fan = fanned(inner, head_width)
    still = fanned(heads * LANES, LANES)
    taken = (
        lax.broadcasted_iota(jnp.int32, (heads * LANES, LANES), 0) // LANES
        == lax.broadcasted_iota(jnp.int32, (heads * LANES, LANES), 1)
    ).astype(bf16)
    whole_decay = jnp.repeat(jnp.exp(jnp.sum(totals, axis=0)), head_width)[None]

    def handed_on(state, distance):
        entering = jnp.zeros(state.shape, f32)
        state = state.astype(f32)
        for _ in range(lax.axis_size("seq") - 1):
            leaving = (state + whole_decay * entering).astype(bf16)
            entering = shifted(leaving, "seq", distance).astype(f32)
        return entering

    x, leaves = piece_state(act, step, cum, etot, fan, heads, inner, width)
    start = handed_on(leaves, 1)
    y = inside_forward(x, act, left, right, still, inner, width)
    z = mm(own, w_gate).astype(bf16)
    gn = mm_nt(incoming, w_out).astype(bf16)
    out_in, gm, gz, states, pac, back, ggain, gskip = gate_both(
        y, act, z, gn, step, cum, etot, ebef, skip, gate_gain[None], start, ones, fan, heads, inner, width
    )
    back_start = handed_on(back, -1)
    mixed = (tokens.astype(f32) + mm(out_in, w_out)).astype(bf16)
    part_out = mm_tn(out_in, incoming).astype(bf16)
    part_gate = mm_tn(own, gz).astype(bf16)
    own_rows = model // (lax.axis_size("seq") * lax.axis_size("fsdp"))
    grad_out_weight = sum_scatter(part_out, own_rows * inner // model)
    grad_gate_weight = sum_scatter(part_gate, own_rows)
    grad_normed = mm_nt(gz, w_gate)

    dx, db, dc, pq = inside_backward(x, act, gm, left, right, still, taken, inner, width)
    gact, graw, gdt, grate = mixer_finish(
        act, x, gm, dx, db, dc, pq, pac, states, step, cum, raw, bias_row, alog_row, etot, skip,
        back_start, ones, fan, heads, inner, width,
    )
    gproj, gtaps, gcbias, top, rest = conv_backward(cin, gact, graw, conv_weight, conv_bias[None])
    nexts = shifted(top, "seq", -1)
    owed = jnp.zeros((8, channels), f32)
    for k in range(span - 1):
        reach = span - 1 - k
        owed = owed + jnp.pad(conv_weight[k] * nexts[:reach], ((8 - reach, 0), (0, 0)))
    gproj = lax.dynamic_update_slice(gproj, (rest + owed).astype(bf16), (rows - 8, 0))

    part_conv = mm_tn(own, gproj).astype(bf16)
    grad_conv_part = sum_scatter(part_conv, own_rows)
    grad_normed = grad_normed + mm_nt(gproj, w_conv)
    own_residual, own_scale = residual[HALO:], scale[HALO:]
    unit = own_residual * own_scale
    pulled = grad_normed * norm_gain
    mean_pull = jnp.mean(pulled * unit, axis=1, keepdims=True)
    grad_tokens = incoming.astype(f32) + own_scale * (pulled - unit * mean_pull)
    grad_norm_gain = jnp.sum(grad_normed * unit, axis=0)

    grad_in_weight = jnp.concatenate(
        [grad_gate_weight, grad_conv_part[:, : channels + heads]], axis=1
    )
    small = [
        gtaps.reshape(-1),
        gcbias[0],
        gdt[0, :heads],
        grate[0, :heads] * -jnp.exp(a_log),
        jnp.sum(gskip.reshape(heads, head_width), axis=1),
        ggain[0],
    ]
    sizes = [part.shape[0] for part in small]
    summed = sum_all(jnp.concatenate(small))
    grad_norm_gain = sum_all(grad_norm_gain)
    split, at = [], 0
    for size in sizes:
        split.append(summed[at : at + size])
        at += size
    return (
        mixed[None],
        grad_tokens[None],
        grad_in_weight,
        grad_out_weight,
        grad_norm_gain,
        split[0].reshape(span, channels),
        *split[1:],
    )


def solution(mesh):
    tokens = P("fsdp", "seq", None)
    sharded = P("fsdp", None)
    spread = P(("seq", "fsdp"), None)
    return jax.shard_map(
        local,
        mesh=mesh,
        in_specs=(tokens, P(), sharded, P(), P(), P(), P(), P(), P(), sharded, tokens),
        out_specs=(tokens, tokens, spread, spread, P(), P(), P(), P(), P(), P(), P()),
        check_vma=False,
    )
```

```python
import functools

import jax
import jax.numpy as jnp
import ml_dtypes
import numpy as np
from jax import lax
from jax.experimental import pallas as pl
from jax.experimental.pallas import tpu as pltpu
from jax.sharding import PartitionSpec as P

ROWS = 128
GROUP = 2
LANES = 128
HALO = 16
VMEM = 48 * 1024 * 1024
LOG2E = 1.4426950408889634
epsilon = 1e-05
bf16 = jnp.bfloat16
f32 = jnp.float32
highest = lax.Precision.HIGHEST


def shifted(block, axis, distance):
    size = lax.axis_size(axis)
    route = [(i - distance, i) for i in range(size) if 0 <= i - distance < size]
    return lax.ppermute(block, axis, route)


def exchanged(block, axis, bit):
    return lax.ppermute(block, axis, [(i, i ^ bit) for i in range(lax.axis_size(axis))])


def pick(block, at, axis):
    return lax.dynamic_index_in_dim(block, at, axis, keepdims=False)


class Flight:
    def __init__(self, steps):
        self.steps, self.value, self.flying = steps, None, None
        self.advance(None)

    def advance(self, arrived):
        try:
            self.flying = self.steps.send(arrived)
        except StopIteration as end:
            self.flying, self.value = None, end.value

    def step(self, *others):
        if self.flying is not None:
            count = len(self.flying)
            tied = lax.optimization_barrier((*self.flying, *others))
            others = tied[count:]
            self.advance(tuple(tied[:count]))
        return others[0] if len(others) == 1 else others

    def finish(self):
        while self.flying is not None:
            self.advance(self.flying)
        return self.value


def gather(weight):
    rows = weight.shape[0]
    if lax.axis_size("fsdp") != 8 or rows % 32:
        full = lax.all_gather(weight, "fsdp", axis=0, tiled=True)
        return full[: full.shape[0] // 2], full[full.shape[0] // 2 :]
    half = rows // 2
    first, last = weight[:half], weight[half:]
    first_y, last_x = yield exchanged(first, "fsdp", 4), exchanged(last, "fsdp", 2)
    first_x, last_y = yield (
        exchanged(jnp.concatenate([first, first_y]), "fsdp", 2),
        exchanged(jnp.concatenate([last, last_x]), "fsdp", 4),
    )
    near = jnp.concatenate(
        [weight, first_x[:half], last_x, first_y, last_y[:half], first_x[half:], last_y[half:]]
    )
    (far,) = yield (exchanged(near, "fsdp", 1),)
    return near, far


def gathered_order():
    group = lax.axis_size("fsdp")
    if group != 8:
        return list(range(group))
    me = lax.axis_index("fsdp")
    return [me ^ distance for distance in (0, 2, 4, 6, 1, 3, 5, 7)]


def in_order(block, order):
    size = block.shape[1] // len(order)
    return jnp.concatenate(
        [lax.dynamic_slice_in_dim(block, at * size, size, axis=1) for at in order], axis=1
    )


def handed_on(state, decay, distance):
    entering = jnp.zeros(state.shape, f32)
    state = state.astype(f32)
    for _ in range(lax.axis_size("seq") - 1):
        leaving = (state + decay * entering).astype(bf16)
        (arrived,) = yield (shifted(leaving, "seq", distance),)
        entering = arrived.astype(f32)
    return entering


def sum_all(vector):
    for axis in ("fsdp", "seq"):
        size = lax.axis_size(axis)
        if size & (size - 1):
            vector = lax.psum(vector, axis)
            continue
        for bit in range(size.bit_length() - 1):
            (other,) = yield (exchanged(vector, axis, 1 << bit),)
            vector = vector + other
    return vector


def sum_scatter(parts):
    pieces, group = lax.axis_size("seq"), lax.axis_size("fsdp")
    bits = group.bit_length() - 1
    columns = parts[0].shape[1]
    rows = [part.shape[0] // (pieces * group) for part in parts]
    total = sum(rows)
    if group != 1 << bits or bits < 1 or total % 2:
        return [
            lax.psum_scatter(part.astype(f32), ("seq", "fsdp"), scatter_dimension=0, tiled=True)
            for part in parts
        ]
    me = lax.axis_index("fsdp")
    parts = [part.reshape(pieces, group // 2, 2, -1, columns) for part in parts]
    mine = me & 1
    (got,) = yield (
        exchanged(jnp.concatenate([pick(part, 1 - mine, 2) for part in parts], axis=2), "fsdp", 1),
    )
    block = jnp.concatenate([pick(part, mine, 2) for part in parts], axis=2) + got
    ways = [list(range(bits - 1, 0, -1)), list(range(bits - 1, 0, -1))]
    halves = [
        part.reshape((pieces,) + (2,) * (bits - 1) + part.shape[2:])
        for part in (block[:, :, : total // 2], block[:, :, total // 2 :])
    ]
    for _ in range(bits - 1):
        taken = [ways[0][-1], ways[1][0]]
        places = [1 + ways[way].index(taken[way]) for way in (0, 1)]
        sides = [(me >> taken[way]) & 1 for way in (0, 1)]
        got = yield tuple(
            exchanged(pick(halves[way], 1 - sides[way], places[way]), "fsdp", 1 << taken[way])
            for way in (0, 1)
        )
        halves = [pick(halves[way], sides[way], places[way]) + got[way] for way in (0, 1)]
        for way in (0, 1):
            ways[way].remove(taken[way])
    part = jnp.concatenate(halves, axis=1)
    (got,) = yield (lax.all_to_all(part, "seq", split_axis=0, concat_axis=0, tiled=True),)
    own = jnp.sum(got.astype(f32), axis=0)
    results, at = [], 0
    for size in rows:
        results.append(own[at : at + size])
        at += size
    return results


def mm(a, b):
    return lax.dot_general(a, b, (((1,), (0,)), ((), ())), preferred_element_type=f32)


def mm_nt(a, b):
    return lax.dot_general(a, b, (((1,), (1,)), ((), ())), preferred_element_type=f32)


def mm_tn(a, b):
    return lax.dot_general(a, b, (((0,), (0,)), ((), ())), preferred_element_type=f32)


def sigmoid(v):
    return 0.5 + 0.5 * jnp.tanh(0.5 * v)


def rows_at():
    return lax.broadcasted_iota(jnp.int32, (ROWS, LANES), 0)


def lanes_at():
    return lax.broadcasted_iota(jnp.int32, (ROWS, LANES), 1)


def slab(i):
    return slice(i * LANES, (i + 1) * LANES)


def wide(i):
    return slice(i * 2 * LANES, (i + 1) * 2 * LANES)


def halves(columns, heads):
    lane = lanes_at()
    high = columns.astype(bf16).astype(f32)
    rest = pltpu.roll(columns - high, heads, 1)
    return jnp.where(lane < heads, high, jnp.where(lane < 2 * heads, rest, 0.0)).astype(bf16)


def low_lanes():
    return (lanes_at() < LANES // 2).astype(f32).astype(bf16), (lanes_at() >= LANES // 2).astype(f32).astype(bf16)


def diagonal(block, low, high):
    return jnp.concatenate([block * low, block * high], axis=0)


def parts_of_step():
    return [slice(part * ROWS, (part + 1) * ROWS) for part in range(GROUP)]


def params(**more):
    return pltpu.CompilerParams(vmem_limit_bytes=VMEM, **more)


def cost(microseconds):
    return pl.CostEstimate(flops=int(microseconds * 1e9), bytes_accessed=4 * 1024 * 1024, transcendentals=0)


def whole(shape):
    return pl.BlockSpec(shape, lambda i: (0,) * len(shape))


def by_rows(width, rows=GROUP * ROWS):
    return pl.BlockSpec((rows, width), lambda i: (i, 0))


def both_halves(block, near_ref, far_ref):
    half = near_ref.shape[0]
    return mm(block[:, :half], near_ref[...]) + mm(block[:, half:], far_ref[...])


def product_kernel(rows, block_ref, near_ref, far_ref, out_ref):
    part = 256
    for at in range(0, rows, part):
        out_ref[at : at + part, :] = both_halves(block_ref[at : at + part, :], near_ref, far_ref)


def product(block, near, far):
    rows, width = block.shape
    columns = near.shape[1]
    cols = 512
    return pl.pallas_call(
        functools.partial(product_kernel, rows),
        grid=(columns // cols,),
        in_specs=[
            whole((rows, width)),
            pl.BlockSpec((width // 2, cols), lambda i: (0, i)),
            pl.BlockSpec((width // 2, cols), lambda i: (0, i)),
        ],
        out_specs=pl.BlockSpec((rows, cols), lambda i: (0, i)),
        out_shape=jax.ShapeDtypeStruct((rows, columns), f32),
        compiler_params=params(),
        name="gate_product",
        cost_estimate=cost(8),
    )(block, near, far)


def conv_kernel(span, rows, normed_ref, near_ref, far_ref, taps_ref, bias_ref, act_ref, cin_ref, held):
    part = 256
    bounds = [(0, HALO)] + [(HALO + at, part) for at in range(0, rows, part)]
    for start, size in bounds:
        block = both_halves(normed_ref[start : start + size, :], near_ref, far_ref).astype(bf16)
        cin_ref[start : start + size, :] = block
        held[start : start + size, :] = block.astype(f32)
    for at in range(0, rows, part):
        total = jnp.broadcast_to(bias_ref[0:1, :], (part, bias_ref.shape[1]))
        for k in range(span):
            start = HALO + at - (span - 1) + k
            total = total + taps_ref[k : k + 1, :] * held[start : start + part, :]
        act_ref[at : at + part, :] = (total * sigmoid(total)).astype(bf16)


def conv_forward(normed, near, far, taps, bias):
    rows, width = normed.shape[0] - HALO, normed.shape[1]
    channels = taps.shape[1]
    cols = 256
    return pl.pallas_call(
        functools.partial(conv_kernel, taps.shape[0], rows),
        grid=(channels // cols,),
        in_specs=[
            whole((rows + HALO, width)),
            pl.BlockSpec((width // 2, cols), lambda i: (0, i)),
            pl.BlockSpec((width // 2, cols), lambda i: (0, i)),
            pl.BlockSpec((taps.shape[0], cols), lambda i: (0, i)),
            pl.BlockSpec((1, cols), lambda i: (0, i)),
        ],
        out_specs=[
            pl.BlockSpec((rows, cols), lambda i: (0, i)),
            pl.BlockSpec((rows + HALO, cols), lambda i: (0, i)),
        ],
        out_shape=[
            jax.ShapeDtypeStruct((rows, channels), bf16),
            jax.ShapeDtypeStruct((rows + HALO, channels), bf16),
        ],
        scratch_shapes=[pltpu.VMEM((rows + HALO, cols), f32)],
        compiler_params=params(),
        name="conv_forward",
        cost_estimate=cost(14),
    )(normed, near, far, taps, bias)


def steps_kernel(blocks, heads, raw_ref, bias_ref, alog_ref, step_ref, cum_ref, left_ref, right_ref, rows3):
    lane = lanes_at()
    lower = (rows_at() >= lane).astype(f32)
    rates = -jnp.exp(alog_ref[...])
    rows3[...] = jnp.zeros_like(rows3)
    for b in range(blocks):
        rows = slice(b * ROWS, (b + 1) * ROWS)
        soft = raw_ref[rows, :] + bias_ref[...]
        soft = jnp.maximum(soft, 0.0) + jnp.log1p(jnp.exp(-jnp.abs(soft)))
        step = soft.astype(bf16).astype(f32)
        step_ref[rows, :] = step
        cum = jnp.dot(lower, step * rates, precision=highest, preferred_element_type=f32)
        cum_ref[rows, :] = cum
        cum = cum * LOG2E
        parts, rest = [], cum
        for _ in range(3):
            part = rest.astype(bf16).astype(f32)
            parts.append(part)
            rest = rest - part
        left = jnp.where(lane < 3 * heads + 3, 1.0, 0.0)
        for k in (2, 1, 0):
            left = jnp.where(lane < (k + 1) * heads, pltpu.roll(parts[k], k * heads, 1), left)
        left_ref[rows, :] = left.astype(bf16)
        for k in range(3):
            flipped = -parts[k].T
            for h in range(heads):
                rows3[k : k + 1, slab(h)] = flipped[h : h + 1, :]
        right_ref[b * HALO : (b + 1) * HALO, :] = rows3[...].astype(bf16)


def steps_forward(raw, bias, a_log, heads):
    rows = raw.shape[0]
    blocks = rows // ROWS
    shape = jax.ShapeDtypeStruct((rows, LANES), f32)
    return pl.pallas_call(
        functools.partial(steps_kernel, blocks, heads),
        out_shape=[
            shape,
            shape,
            jax.ShapeDtypeStruct((rows, LANES), bf16),
            jax.ShapeDtypeStruct((blocks * HALO, heads * LANES), bf16),
        ],
        scratch_shapes=[pltpu.VMEM((HALO, heads * LANES), f32)],
        compiler_params=params(),
        name="steps_forward",
        cost_estimate=cost(6),
    )(raw, bias, a_log)


def state_kernel(heads, v_ref, b_ref, step_ref, cum_ref, etot_ref, fan_ref, x_ref, f_ref, state, tails, both):
    at = pl.program_id(0)

    @pl.when(at == 0)
    def _():
        state[...] = jnp.zeros_like(state)

    for part, r in enumerate(parts_of_step()):
        cum, step = cum_ref[r, :], step_ref[r, :]
        tail = jnp.exp(cum[ROWS - 1 :, :] - cum) * step
        both[...] = mm(jnp.concatenate([halves(step, heads), halves(tail, heads)], axis=0), fan_ref[...])
        v = v_ref[r, :].astype(f32)
        x_ref[r, :] = (v * both[:ROWS, :]).astype(bf16)
        tails[...] = (v * both[ROWS:, :]).astype(bf16)
        etot = etot_ref[pl.ds(at * GROUP + part, 1), :]
        state[...] = etot * state[...] + mm_tn(b_ref[r, :], tails[...])

    @pl.when(at == pl.num_programs(0) - 1)
    def _():
        f_ref[...] = state[...].astype(bf16)


def piece_state(act, step, cum, etot, fan, heads, inner, width):
    rows = act.shape[0]
    inputs_at = inner // width
    return pl.pallas_call(
        functools.partial(state_kernel, heads),
        grid=(rows // (GROUP * ROWS),),
        in_specs=[
            by_rows(inner),
            pl.BlockSpec((GROUP * ROWS, width), lambda i: (i, inputs_at)),
            by_rows(LANES),
            by_rows(LANES),
            whole(etot.shape),
            whole(fan.shape),
        ],
        out_specs=[by_rows(inner), whole((width, inner))],
        out_shape=[
            jax.ShapeDtypeStruct((rows, inner), bf16),
            jax.ShapeDtypeStruct((width, inner), bf16),
        ],
        scratch_shapes=[
            pltpu.VMEM((width, inner), f32),
            pltpu.VMEM((ROWS, inner), bf16),
            pltpu.VMEM((2 * ROWS, inner), f32),
        ],
        compiler_params=params(),
        name="piece_state",
        cost_estimate=cost(6),
    )(act, act, step, cum, etot, fan)


def inside_kernel(pairs, x_ref, b_ref, c_ref, left_ref, right_ref, still_ref, y_ref, right):
    fixed = left_rows(right, still_ref, right_ref)
    low, high = low_lanes()
    for part, r in enumerate(parts_of_step()):
        scores = jnp.where(rows_at() >= lanes_at(), mm_nt(c_ref[r, :], b_ref[r, :]), 0.0)
        scores = jnp.concatenate([scores, scores], axis=1)
        left = left_ref[r, :]
        for i in range(pairs):
            spread = mm(left, fixed[part, :, wide(i)])
            weights = (scores * jnp.exp2(jnp.minimum(spread, 0.0))).astype(bf16)
            y_ref[r, slab(i)] = mm(weights, diagonal(x_ref[r, slab(i)], low, high))


def left_rows(right, still_ref, right_ref):
    @pl.when(pl.program_id(0) == 0)
    def _():
        for part in range(GROUP):
            right[part, :, :] = still_ref[...]

    own = still_ref.shape[0] - 2 * HALO
    for part in range(GROUP):
        right[part, own : own + HALO, :] = right_ref[part * HALO : (part + 1) * HALO, :]
    return right


def inside_forward(x, act, left, right, still, inner, width):
    rows = act.shape[0]
    inputs_at = inner // width
    return pl.pallas_call(
        functools.partial(inside_kernel, inner // LANES),
        grid=(rows // (GROUP * ROWS),),
        in_specs=[
            by_rows(inner),
            pl.BlockSpec((GROUP * ROWS, width), lambda i: (i, inputs_at)),
            pl.BlockSpec((GROUP * ROWS, width), lambda i: (i, inputs_at + 1)),
            by_rows(LANES),
            by_rows(right.shape[1], GROUP * HALO),
            whole(still.shape),
        ],
        out_specs=by_rows(inner),
        out_shape=jax.ShapeDtypeStruct((rows, inner), f32),
        scratch_shapes=[pltpu.VMEM((GROUP,) + still.shape, bf16)],
        compiler_params=params(),
        name="inside_forward",
        cost_estimate=cost(10),
    )(x, act, act, left, right, still)


def gate_kernel(
    heads,
    pairs,
    y_ref,
    v_ref,
    b_ref,
    c_ref,
    z_ref,
    gn_ref,
    step_ref,
    cum_ref,
    etot_ref,
    ebef_ref,
    skip_ref,
    gain_ref,
    start_ref,
    ones_ref,
    fan_ref,
    out_ref,
    gm_ref,
    gz_ref,
    states_ref,
    pac_ref,
    back_ref,
    ggain_ref,
    gskip_ref,
    state,
    back,
    across,
    mixer,
    gated,
    early,
    tails,
    products,
    both,
):
    at = pl.program_id(0)
    width = pairs * LANES

    @pl.when(at == 0)
    def _():
        state[...] = start_ref[...]
        back[...] = jnp.zeros_like(back)
        ggain_ref[...] = jnp.zeros_like(ggain_ref)
        gskip_ref[...] = jnp.zeros_like(gskip_ref)

    for part, r in enumerate(parts_of_step()):
        outputs = c_ref[r, :]
        entering = state[...].astype(bf16)
        states_ref[part * state.shape[0] : (part + 1) * state.shape[0], :] = entering
        across[...] = mm(outputs, entering)
        cum = cum_ref[r, :]
        grow = jnp.exp(cum)
        tail = jnp.exp(cum[ROWS - 1 :, :] - cum) * step_ref[r, :]
        both[...] = mm(jnp.concatenate([halves(grow, heads), halves(tail, heads)], axis=0), fan_ref[...])
        squares = jnp.zeros((ROWS, LANES), f32)
        meets = jnp.zeros((ROWS, LANES), f32)
        for i in range(pairs):
            s = slab(i)
            v = v_ref[r, s].astype(f32)
            ya = across[:, s] * both[:ROWS, s]
            across[:, s] = ya
            m = (y_ref[r, s] + ya + skip_ref[:, s] * v).astype(bf16)
            mixer[:, s] = m
            z = z_ref[r, s]
            product = m.astype(f32) * (z * sigmoid(z))
            gated[:, s] = product
            squares = squares + product * product
            meets = meets + gn_ref[r, s] * gain_ref[:, s] * product
            tails[:, s] = (v * both[ROWS:, s]).astype(bf16)
        scale = lax.rsqrt(jnp.sum(squares, axis=1, keepdims=True) / width + epsilon)
        pull = scale * scale * scale * (jnp.sum(meets, axis=1, keepdims=True) / width)
        for i in range(pairs):
            s = slab(i)
            v = v_ref[r, s].astype(f32)
            product = gated[:, s]
            unit = product * scale
            gain = gain_ref[:, s]
            gn = gn_ref[r, s]
            out_ref[r, s] = (unit * gain).astype(bf16)
            ggain_ref[:, s] += jnp.sum(gn * unit, axis=0, keepdims=True)
            grad = gn * gain * scale - product * pull
            z = z_ref[r, s]
            sig = sigmoid(z)
            swish = z * sig
            gm = (grad * swish).astype(bf16)
            gm_ref[r, s] = gm
            slope = sig + swish * (1.0 - sig)
            gz_ref[r, s] = (grad * mixer[:, s].astype(f32) * slope).astype(bf16)
            g = gm.astype(f32)
            gskip_ref[:, s] += jnp.sum(g * v, axis=0, keepdims=True)
            products[:, s] = (g * across[:, s]).astype(bf16)
            early[:, s] = (g * both[:ROWS, s]).astype(bf16)
        pac_ref[r, :] = mm(products[...], ones_ref[...])
        block = at * GROUP + part
        back[...] += ebef_ref[pl.ds(block, 1), :] * mm_tn(outputs, early[...])
        state[...] = etot_ref[pl.ds(block, 1), :] * state[...] + mm_tn(b_ref[r, :], tails[...])

    @pl.when(at == pl.num_programs(0) - 1)
    def _():
        back_ref[...] = back[...].astype(bf16)


def gate_both(y, act, z, gn, step, cum, etot, ebef, skip, gain, start, ones, fan, heads, inner, width):
    rows = act.shape[0]
    inputs_at = inner // width
    blocks = rows // ROWS
    return pl.pallas_call(
        functools.partial(gate_kernel, heads, inner // LANES),
        grid=(blocks // GROUP,),
        in_specs=[
            by_rows(inner),
            by_rows(inner),
            pl.BlockSpec((GROUP * ROWS, width), lambda i: (i, inputs_at)),
            pl.BlockSpec((GROUP * ROWS, width), lambda i: (i, inputs_at + 1)),
            by_rows(inner),
            by_rows(inner),
            by_rows(LANES),
            by_rows(LANES),
            whole(etot.shape),
            whole(ebef.shape),
            whole((1, inner)),
            whole((1, inner)),
            whole((width, inner)),
            whole((inner, LANES)),
            whole(fan.shape),
        ],
        out_specs=[
            by_rows(inner),
            by_rows(inner),
            by_rows(inner),
            by_rows(inner, GROUP * width),
            by_rows(LANES),
            whole((width, inner)),
            whole((1, inner)),
            whole((1, inner)),
        ],
        out_shape=[
            jax.ShapeDtypeStruct((rows, inner), bf16),
            jax.ShapeDtypeStruct((rows, inner), bf16),
            jax.ShapeDtypeStruct((rows, inner), bf16),
            jax.ShapeDtypeStruct((blocks * width, inner), bf16),
            jax.ShapeDtypeStruct((rows, LANES), f32),
            jax.ShapeDtypeStruct((width, inner), bf16),
            jax.ShapeDtypeStruct((1, inner), f32),
            jax.ShapeDtypeStruct((1, inner), f32),
        ],
        scratch_shapes=[
            pltpu.VMEM((width, inner), f32),
            pltpu.VMEM((width, inner), f32),
            pltpu.VMEM((ROWS, inner), f32),
            pltpu.VMEM((ROWS, inner), bf16),
            pltpu.VMEM((ROWS, inner), f32),
            pltpu.VMEM((ROWS, inner), bf16),
            pltpu.VMEM((ROWS, inner), bf16),
            pltpu.VMEM((ROWS, inner), bf16),
            pltpu.VMEM((2 * ROWS, inner), f32),
        ],
        compiler_params=params(),
        name="gate_both",
        cost_estimate=cost(18),
    )(y, act, act, act, z, gn, step, cum, etot, ebef, skip, gain, start, ones, fan)


def inside_back_kernel(
    pairs, x_ref, b_ref, c_ref, g_ref, left_ref, right_ref, still_ref, taken_ref,
    dx_ref, db_ref, dc_ref, pq_ref, right, moved, late,
):
    fixed = left_rows(right, still_ref, right_ref)
    lane = lanes_at()
    low, high = low_lanes()
    ones = jnp.ones((16, ROWS), bf16)
    for part, r in enumerate(parts_of_step()):
        inputs, outputs = b_ref[r, :], c_ref[r, :]
        raw_scores = mm_nt(inputs, outputs)
        scores = jnp.where(rows_at() <= lane, raw_scores, 0.0)
        strict = jnp.where(rows_at() < lane, raw_scores, 0.0)
        scores = jnp.concatenate([scores, scores], axis=1)
        strict = jnp.concatenate([strict, strict], axis=1)
        left = -left_ref[r, :]
        gathered = jnp.zeros((ROWS, 2 * LANES), f32)
        for i in range(pairs):
            spread = mm(left, fixed[part, :, wide(i)])
            decay = jnp.exp2(jnp.minimum(spread, 0.0))
            stacked = diagonal(g_ref[r, slab(i)], low, high)
            grad = mm_nt(x_ref[r, slab(i)], stacked) * decay
            gathered = gathered + grad
            moved[:, wide(i)] = (grad * strict).astype(bf16)
            dx_ref[r, slab(i)] = mm((scores * decay).astype(bf16), stacked)
        late[...] = jnp.zeros_like(late)
        for i in range(pairs):
            sums = mm(ones, moved[:, wide(i)])
            late[2 * i : 2 * i + 1, :] = sums[0:1, :LANES]
            late[2 * i + 1 : 2 * i + 2, :] = sums[0:1, LANES:]
        pq_ref[r, :] = late[...].T - mm(moved[...], taken_ref[...])
        gathered = gathered[:, :LANES] + gathered[:, LANES:]
        gathered = jnp.where(rows_at() <= lane, gathered, 0.0).astype(bf16)
        db_ref[r, :] = mm(gathered, outputs)
        dc_ref[r, :] = mm_tn(gathered, inputs)


def inside_backward(x, act, gm, left, right, still, taken, inner, width):
    rows = act.shape[0]
    inputs_at = inner // width
    return pl.pallas_call(
        functools.partial(inside_back_kernel, inner // LANES),
        grid=(rows // (GROUP * ROWS),),
        in_specs=[
            by_rows(inner),
            pl.BlockSpec((GROUP * ROWS, width), lambda i: (i, inputs_at)),
            pl.BlockSpec((GROUP * ROWS, width), lambda i: (i, inputs_at + 1)),
            by_rows(inner),
            by_rows(LANES),
            by_rows(right.shape[1], GROUP * HALO),
            whole(still.shape),
            whole(taken.shape),
        ],
        out_specs=[by_rows(inner), by_rows(width), by_rows(width), by_rows(LANES)],
        out_shape=[
            jax.ShapeDtypeStruct((rows, inner), f32),
            jax.ShapeDtypeStruct((rows, width), f32),
            jax.ShapeDtypeStruct((rows, width), f32),
            jax.ShapeDtypeStruct((rows, LANES), f32),
        ],
        scratch_shapes=[
            pltpu.VMEM((GROUP,) + still.shape, bf16),
            pltpu.VMEM((ROWS, 2 * inner), bf16),
            pltpu.VMEM((LANES, ROWS), f32),
        ],
        compiler_params=params(),
        name="inside_backward",
        cost_estimate=cost(20),
    )(x, act, act, gm, left, right, still, taken)


def finish_kernel(
    heads,
    pairs,
    blocks,
    v_ref,
    x_ref,
    b_ref,
    c_ref,
    g_ref,
    dx_ref,
    db_ref,
    dc_ref,
    pq_ref,
    pac_ref,
    states_ref,
    step_ref,
    cum_ref,
    raw_ref,
    bias_ref,
    alog_ref,
    etot_ref,
    skip_ref,
    start_ref,
    ones_ref,
    fan_ref,
    gact_ref,
    graw_ref,
    gbias_ref,
    grate_ref,
    state,
    tails,
    early,
    first,
    second,
    third,
    spread,
    three,
):
    at = pl.program_id(0)
    step_at = blocks // GROUP - 1 - at
    inner = pairs * LANES
    width = state.shape[0]

    @pl.when(at == 0)
    def _():
        state[...] = start_ref[...]
        gbias_ref[...] = jnp.zeros_like(gbias_ref)
        grate_ref[...] = jnp.zeros_like(grate_ref)

    later = (rows_at() <= lanes_at()).astype(f32)
    earlier = (rows_at() > lanes_at()).astype(f32)
    rates = jnp.exp(alog_ref[...])
    for part, r in reversed(list(enumerate(parts_of_step()))):
        inputs, outputs = b_ref[r, :], c_ref[r, :]
        leaving = state[...]
        leaving_low = leaving.astype(bf16)
        entering = states_ref[part * width : (part + 1) * width, :]
        etot = etot_ref[pl.ds(step_at * GROUP + part, 1), :]
        held = jnp.sum(leaving * entering.astype(f32), axis=0, keepdims=True) * etot
        held = mm(jnp.broadcast_to(held, (8, inner)).astype(bf16), ones_ref[...])[0:1, :]
        spread[...] = mm(inputs, leaving_low)
        cum, step = cum_ref[r, :], step_ref[r, :]
        grow = jnp.exp(cum)
        tail = jnp.exp(cum[ROWS - 1 :, :] - cum)
        three[...] = mm(
            jnp.concatenate([halves(step, heads), halves(tail, heads), halves(grow, heads)], axis=0),
            fan_ref[...],
        )
        for i in range(pairs):
            s = slab(i)
            v = v_ref[r, s].astype(f32)
            g = g_ref[r, s].astype(f32)
            steps = three[:ROWS, s]
            x = x_ref[r, s].astype(f32)
            part_tail = three[ROWS : 2 * ROWS, s]
            more = spread[:, s] * part_tail
            dx = dx_ref[r, s] + more
            first[:, s] = (x * more).astype(bf16)
            direct = v * dx
            high = direct.astype(bf16)
            second[:, s] = high
            third[:, s] = (direct - high.astype(f32)).astype(bf16)
            gact_ref[r, s] = (steps * dx + skip_ref[:, s] * g).astype(bf16)
            tails[:, s] = (x * part_tail).astype(bf16)
            early[:, s] = (g * three[2 * ROWS :, s]).astype(bf16)
        gact_ref[r, inner : inner + width] = (db_ref[r, :] + mm_nt(tails[...], leaving_low)).astype(bf16)
        gact_ref[r, inner + width :] = (dc_ref[r, :] + mm_nt(early[...], entering)).astype(bf16)
        gdecay = (
            jnp.dot(later, pq_ref[r, :] + pac_ref[r, :], precision=highest, preferred_element_type=f32)
            + jnp.dot(
                earlier, mm(first[...], ones_ref[...]), precision=highest, preferred_element_type=f32
            )
            + held
        )
        gstep = mm(second[...], ones_ref[...]) + mm(third[...], ones_ref[...]) - rates * gdecay
        graw = gstep.astype(bf16).astype(f32) * sigmoid(raw_ref[r, :] + bias_ref[...])
        graw_ref[r, :] = graw.astype(bf16)
        gbias_ref[...] += jnp.sum(graw, axis=0, keepdims=True)
        grate_ref[...] += jnp.sum(step * gdecay, axis=0, keepdims=True)
        state[...] = etot * leaving + mm_tn(outputs, early[...])


def mixer_finish(
    act, x, gm, dx, db, dc, pq, pac, states, step, cum, raw, bias, a_log, etot, skip, start, ones, fan, heads, inner, width
):
    rows = act.shape[0]
    blocks = rows // ROWS
    inputs_at = inner // width
    channels = act.shape[1]

    def backwards(columns, height=GROUP * ROWS, column_at=0):
        return pl.BlockSpec((height, columns), lambda i: (blocks // GROUP - 1 - i, column_at))

    return pl.pallas_call(
        functools.partial(finish_kernel, heads, inner // LANES, blocks),
        grid=(blocks // GROUP,),
        in_specs=[
            backwards(inner),
            backwards(inner),
            backwards(width, column_at=inputs_at),
            backwards(width, column_at=inputs_at + 1),
            backwards(inner),
            backwards(inner),
            backwards(width),
            backwards(width),
            backwards(LANES),
            backwards(LANES),
            backwards(inner, GROUP * width),
            backwards(LANES),
            backwards(LANES),
            backwards(LANES),
            whole((1, LANES)),
            whole((1, LANES)),
            whole(etot.shape),
            whole((1, inner)),
            whole((width, inner)),
            whole((inner, LANES)),
            whole(fan.shape),
        ],
        out_specs=[backwards(channels), backwards(LANES), whole((1, LANES)), whole((1, LANES))],
        out_shape=[
            jax.ShapeDtypeStruct((rows, channels), bf16),
            jax.ShapeDtypeStruct((rows, LANES), bf16),
            jax.ShapeDtypeStruct((1, LANES), f32),
            jax.ShapeDtypeStruct((1, LANES), f32),
        ],
        scratch_shapes=[
            pltpu.VMEM((width, inner), f32),
            pltpu.VMEM((ROWS, inner), bf16),
            pltpu.VMEM((ROWS, inner), bf16),
            pltpu.VMEM((ROWS, inner), bf16),
            pltpu.VMEM((ROWS, inner), bf16),
            pltpu.VMEM((ROWS, inner), bf16),
            pltpu.VMEM((ROWS, inner), f32),
            pltpu.VMEM((3 * ROWS, inner), f32),
        ],
        compiler_params=params(),
        name="mixer_finish",
        cost_estimate=cost(16),
    )(act, x, act, act, gm, dx, db, dc, pq, pac, states, step, cum, raw, bias, a_log, etot, skip, start, ones, fan)


def conv_back_kernel(
    span, rows, blocks, cin_ref, gact_ref, graw_ref, taps_ref, bias_ref,
    gproj_ref, gtaps_ref, gbias_ref, top_ref, rest_ref, held, grads,
):
    part = 256
    at = pl.program_id(0)

    @pl.when(at == blocks)
    def _():
        gproj_ref[...] = graw_ref[...]

    @pl.when(at < blocks)
    def _():
        held[...] = cin_ref[...].astype(f32)
        grads[rows:, :] = jnp.zeros((HALO, LANES), f32)
        gbias = jnp.zeros((1, LANES), f32)
        gtaps = [jnp.zeros((1, LANES), f32)] * span
        for start in range(0, rows, part):
            total = jnp.broadcast_to(bias_ref[0:1, :], (part, LANES))
            seen = []
            for k in range(span):
                first = HALO + start - (span - 1) + k
                seen.append(held[first : first + part, :])
                total = total + taps_ref[k : k + 1, :] * seen[k]
            sig = sigmoid(total)
            grad = gact_ref[start : start + part, :].astype(f32) * (sig * (1.0 + total * (1.0 - sig)))
            grads[start : start + part, :] = grad
            gbias = gbias + jnp.sum(grad, axis=0, keepdims=True)
            for k in range(span):
                gtaps[k] = gtaps[k] + jnp.sum(seen[k] * grad, axis=0, keepdims=True)
        gbias_ref[...] = gbias
        for k in range(span):
            gtaps_ref[k : k + 1, :] = gtaps[k]
        top_ref[...] = grads[0:8, :]
        for start in range(0, rows, part):
            total = jnp.zeros((part, LANES), f32)
            for k in range(span):
                first = start + span - 1 - k
                total = total + taps_ref[k : k + 1, :] * grads[first : first + part, :]
            gproj_ref[start : start + part, :] = total.astype(bf16)
            if start + part == rows:
                rest_ref[...] = total[part - 8 :, :]


def conv_backward(cin, gact, graw, taps, bias):
    rows, channels = gact.shape
    blocks = channels // LANES
    span = taps.shape[0]

    def columns(height):
        return pl.BlockSpec((height, LANES), lambda i: (0, jnp.minimum(i, blocks - 1)))

    return pl.pallas_call(
        functools.partial(conv_back_kernel, span, rows, blocks),
        grid=(blocks + 1,),
        in_specs=[columns(rows + HALO), columns(rows), whole((rows, LANES)), columns(span), columns(1)],
        out_specs=[
            pl.BlockSpec((rows, LANES), lambda i: (0, i)),
            columns(span),
            columns(1),
            columns(8),
            columns(8),
        ],
        out_shape=[
            jax.ShapeDtypeStruct((rows, channels + LANES), bf16),
            jax.ShapeDtypeStruct((span, channels), f32),
            jax.ShapeDtypeStruct((1, channels), f32),
            jax.ShapeDtypeStruct((8, channels), f32),
            jax.ShapeDtypeStruct((8, channels), f32),
        ],
        scratch_shapes=[pltpu.VMEM((rows + HALO, LANES), f32), pltpu.VMEM((rows + HALO, LANES), f32)],
        compiler_params=params(),
        name="conv_backward",
        cost_estimate=cost(18),
    )(cin, gact, graw, taps, bias)


def local(
    tokens,
    norm_gain,
    in_weight,
    conv_weight,
    conv_bias,
    dt_bias,
    a_log,
    skip_gain,
    gate_gain,
    out_weight,
    cotangent,
):
    tokens, incoming = tokens[0], cotangent[0]
    rows, model = tokens.shape
    heads = a_log.shape[0]
    span, channels = conv_weight.shape
    inner = gate_gain.shape[0]
    width = (channels - inner) // 2
    head_width = inner // heads
    blocks = rows // ROWS
    pad = LANES - heads

    order = gathered_order()
    half = model // 2
    conv_flight = Flight(gather(jnp.pad(in_weight[:, inner:], ((0, 0), (0, pad)))))
    before = shifted(tokens[rows - HALO :], "seq", 1)

    def first_norm(block):
        block = block.astype(f32)
        scale = lax.rsqrt(jnp.mean(block * block, axis=1, keepdims=True) + epsilon)
        return (block * scale * norm_gain).astype(bf16), scale

    own, own_scale = first_norm(tokens)
    own = conv_flight.step(own)
    own_turned = in_order(own, order)
    turned = jnp.concatenate([in_order(first_norm(before)[0], order), own_turned], axis=0)
    turned, gate_part, out_weight = conv_flight.step(turned, in_weight[:, :inner], out_weight)
    gate_flight = Flight(gather(gate_part))
    w_out = lax.all_gather(out_weight, "fsdp", axis=0, tiled=True)
    conv_near, conv_far = conv_flight.finish()
    raw = mm(own_turned[:, :half], conv_near[:, channels:]) + mm(own_turned[:, half:], conv_far[:, channels:])
    act, cin = conv_forward(turned, conv_near, conv_far, conv_weight, conv_bias[None])
    act = gate_flight.step(act)
    bias_row = jnp.pad(dt_bias, (0, pad))[None]
    alog_row = jnp.pad(a_log, (0, pad))[None]
    step, cum, left, right = steps_forward(raw, bias_row, alog_row, heads)

    totals = cum.reshape(blocks, ROWS, LANES)[:, -1, :heads]
    befores = jnp.cumsum(totals, axis=0) - totals
    etot = jnp.repeat(jnp.exp(totals), head_width, axis=1)
    ebef = jnp.repeat(jnp.exp(befores), head_width, axis=1)
    skip = jnp.repeat(skip_gain, head_width)[None]
    def fanned(count, each):
        row, column = np.arange(LANES)[:, None], np.arange(count)[None]
        return ((row < 3 * heads) & (row % heads == column // each)).astype(ml_dtypes.bfloat16)

    def gathering(count, each):
        return (np.arange(count)[:, None] // each == np.arange(LANES)[None]).astype(ml_dtypes.bfloat16)

    fan = fanned(inner, head_width)
    still = fanned(heads * LANES, LANES)
    ones = gathering(inner, head_width)
    taken = gathering(heads * LANES, LANES)
    whole_decay = jnp.repeat(jnp.exp(jnp.sum(totals, axis=0)), head_width)[None]

    x, leaves = piece_state(act, step, cum, etot, fan, heads, inner, width)
    ahead = Flight(handed_on(leaves, whole_decay, 1))
    x = gate_flight.step(x)
    y = inside_forward(x, act, left, right, still, inner, width)
    y = ahead.step(y)
    gate_near, gate_far = gate_flight.finish()
    z = product(own_turned, gate_near, gate_far)
    z = ahead.step(z)
    gn = mm_nt(incoming, w_out)
    gn = ahead.step(gn)
    start = ahead.finish()
    out_in, gm, gz, states, pac, back, ggain, gskip = gate_both(
        y, act, z, gn, step, cum, etot, ebef, skip, gate_gain[None], start, ones, fan, heads, inner, width
    )

    behind = Flight(handed_on(back, whole_decay, -1))
    part_out = mm_tn(out_in, incoming).astype(bf16)
    part_gate = mm_tn(own, gz).astype(bf16)
    slices = inner // model
    sums = Flight(
        sum_scatter([part_out] + [part_gate[:, i * model : (i + 1) * model] for i in range(slices)])
    )
    mixed = (tokens.astype(f32) + mm(out_in, w_out)).astype(bf16)
    mixed = behind.step(mixed)
    mixed = sums.step(mixed)
    dx, db, dc, pq = inside_backward(x, act, gm, left, right, still, taken, inner, width)
    dx = behind.step(dx)
    dx = sums.step(dx)
    pulled_near, pulled_far = mm_nt(gz, gate_near), mm_nt(gz, gate_far)
    pulled_near, pulled_far = behind.step(pulled_near, pulled_far)
    back_start = behind.finish()
    gact, graw, gdt, grate = mixer_finish(
        act, x, gm, dx, db, dc, pq, pac, states, step, cum, raw, bias_row, alog_row, etot, skip,
        back_start, ones, fan, heads, inner, width,
    )
    gact = sums.step(gact)
    gproj, gtaps, gcbias, top, rest = conv_backward(cin, gact, graw, conv_weight, conv_bias[None])
    nexts = shifted(top, "seq", -1)
    owed = jnp.zeros((8, channels), f32)
    for k in range(span - 1):
        reach = span - 1 - k
        owed = owed + jnp.pad(conv_weight[k] * nexts[:reach], ((8 - reach, 0), (0, 0)))
    gproj = lax.dynamic_update_slice(gproj, (rest + owed).astype(bf16), (rows - 8, 0))

    part_conv = mm_tn(own, gproj).astype(bf16)
    conv_sums = Flight(sum_scatter([part_conv]))
    pulled_near = pulled_near + mm_nt(gproj, conv_near)
    pulled_far = pulled_far + mm_nt(gproj, conv_far)
    pulled_near, pulled_far = conv_sums.step(pulled_near, pulled_far)
    size = model // len(order)
    places = sum(jnp.arange(len(order)) * 0 + jnp.where(jnp.arange(len(order)) == at, i, 0) for i, at in enumerate(order))
    grad_normed = in_order(jnp.concatenate([pulled_near, pulled_far], axis=1), [places[i] for i in range(len(order))])
    unit = tokens.astype(f32) * own_scale
    pulled = grad_normed * norm_gain
    mean_pull = jnp.mean(pulled * unit, axis=1, keepdims=True)
    grad_tokens = incoming.astype(f32) + own_scale * (pulled - unit * mean_pull)
    grad_norm_gain = jnp.sum(grad_normed * unit, axis=0)
    small = [
        grad_norm_gain,
        gtaps.reshape(-1),
        gcbias[0],
        gdt[0, :heads],
        grate[0, :heads] * -jnp.exp(a_log),
        jnp.sum(gskip.reshape(heads, head_width), axis=1),
        ggain[0],
    ]
    small_sums = Flight(sum_all(jnp.concatenate(small)))
    conv_sums.step()
    summed_parts = sums.finish()
    grad_out_weight = summed_parts[0]
    (grad_conv_part,) = conv_sums.finish()
    summed = small_sums.finish()

    grad_in_weight = jnp.concatenate(
        summed_parts[1:] + [grad_conv_part[:, : channels + heads]], axis=1
    )
    sizes = [part.shape[0] for part in small]
    split, at = [], 0
    for size in sizes:
        split.append(summed[at : at + size])
        at += size
    return (
        mixed[None],
        grad_tokens[None],
        grad_in_weight,
        grad_out_weight,
        split[0],
        split[1].reshape(span, channels),
        *split[2:],
    )


def solution(mesh):
    tokens = P("fsdp", "seq", None)
    sharded = P("fsdp", None)
    spread = P(("seq", "fsdp"), None)
    return jax.shard_map(
        local,
        mesh=mesh,
        in_specs=(tokens, P(), sharded, P(), P(), P(), P(), P(), P(), sharded, tokens),
        out_specs=(tokens, tokens, spread, spread, P(), P(), P(), P(), P(), P(), P()),
        check_vma=False,
    )
```

```python
import functools

import jax
import jax.numpy as jnp
import ml_dtypes
import numpy as np
from jax import lax
from jax.experimental import pallas as pl
from jax.experimental.pallas import tpu as pltpu
from jax.sharding import PartitionSpec as P

ROWS = 128
GROUP = 2
LANES = 128
HALO = 16
VMEM = 48 * 1024 * 1024
LOG2E = 1.4426950408889634
epsilon = 1e-05
bf16 = jnp.bfloat16
f32 = jnp.float32
highest = lax.Precision.HIGHEST


def shifted(block, axis, distance):
    size = lax.axis_size(axis)
    route = [(i - distance, i) for i in range(size) if 0 <= i - distance < size]
    return lax.ppermute(block, axis, route)


def exchanged(block, axis, bit):
    return lax.ppermute(block, axis, [(i, i ^ bit) for i in range(lax.axis_size(axis))])


def pick(block, at, axis):
    return lax.dynamic_index_in_dim(block, at, axis, keepdims=False)


class Flight:
    def __init__(self, steps):
        self.steps, self.value, self.flying = steps, None, None
        self.advance(None)

    def advance(self, arrived):
        try:
            self.flying = self.steps.send(arrived)
        except StopIteration as end:
            self.flying, self.value = None, end.value

    def step(self, *others):
        if self.flying is not None:
            count = len(self.flying)
            tied = lax.optimization_barrier((*self.flying, *others))
            others = tied[count:]
            self.advance(tuple(tied[:count]))
        return others[0] if len(others) == 1 else others

    def finish(self):
        while self.flying is not None:
            self.advance(self.flying)
        return self.value


def gather(weight):
    rows = weight.shape[0]
    if lax.axis_size("fsdp") != 8 or rows % 32:
        full = lax.all_gather(weight, "fsdp", axis=0, tiled=True)
        return [full[: full.shape[0] // 2]], [full[full.shape[0] // 2 :]]
    first, last = weight[: rows // 2], weight[rows // 2 :]

    def crossed(block):
        return exchanged(block, "fsdp", 1)

    first_y, last_x = exchanged(first, "fsdp", 4), exchanged(last, "fsdp", 2)
    first_x, last_y = exchanged(first, "fsdp", 2), exchanged(last, "fsdp", 4)
    far = [crossed(weight)]
    first_y, last_x, first_x, last_y = yield first_y, last_x, first_x, last_y
    first_xy, last_xy = exchanged(first_y, "fsdp", 2), exchanged(last_x, "fsdp", 4)
    far += [crossed(block) for block in (first_x, last_x, first_y, last_y)]
    first_xy, last_xy, *far = yield first_xy, last_xy, *far
    far += [crossed(first_xy), crossed(last_xy)]
    far = yield tuple(far)
    return [weight, first_x, last_x, first_y, last_y, first_xy, last_xy], list(far)


def gathered_order():
    group = lax.axis_size("fsdp")
    if group != 8:
        return list(range(group))
    me = lax.axis_index("fsdp")
    return [me ^ distance for distance in (0, 2, 4, 6, 1, 3, 5, 7)]


def in_order(block, order):
    size = block.shape[1] // len(order)
    return jnp.concatenate(
        [lax.dynamic_slice_in_dim(block, at * size, size, axis=1) for at in order], axis=1
    )


def handed_on(state, decay, distance):
    entering = jnp.zeros(state.shape, f32)
    state = state.astype(f32)
    for _ in range(lax.axis_size("seq") - 1):
        leaving = (state + decay * entering).astype(bf16)
        (arrived,) = yield (shifted(leaving, "seq", distance),)
        entering = arrived.astype(f32)
    return entering


def sum_all(vector):
    for axis in ("fsdp", "seq"):
        size = lax.axis_size(axis)
        if size & (size - 1):
            vector = lax.psum(vector, axis)
            continue
        for bit in range(size.bit_length() - 1):
            (other,) = yield (exchanged(vector, axis, 1 << bit),)
            vector = vector + other
    return vector


def sum_scatter(parts):
    pieces, group = lax.axis_size("seq"), lax.axis_size("fsdp")
    bits = group.bit_length() - 1
    columns = parts[0].shape[1]
    rows = [part.shape[0] // (pieces * group) for part in parts]
    total = sum(rows)
    if group != 1 << bits or bits < 1 or total % 2:
        return [
            lax.psum_scatter(part.astype(f32), ("seq", "fsdp"), scatter_dimension=0, tiled=True)
            for part in parts
        ]
    me = lax.axis_index("fsdp")
    parts = [part.reshape(pieces, group // 2, 2, -1, columns) for part in parts]
    mine = me & 1
    (got,) = yield (
        exchanged(jnp.concatenate([pick(part, 1 - mine, 2) for part in parts], axis=2), "fsdp", 1),
    )
    block = jnp.concatenate([pick(part, mine, 2) for part in parts], axis=2) + got
    ways = [list(range(bits - 1, 0, -1)), list(range(bits - 1, 0, -1))]
    halves = [
        part.reshape((pieces,) + (2,) * (bits - 1) + part.shape[2:])
        for part in (block[:, :, : total // 2], block[:, :, total // 2 :])
    ]
    for _ in range(bits - 1):
        taken = [ways[0][-1], ways[1][0]]
        places = [1 + ways[way].index(taken[way]) for way in (0, 1)]
        sides = [(me >> taken[way]) & 1 for way in (0, 1)]
        got = yield tuple(
            exchanged(pick(halves[way], 1 - sides[way], places[way]), "fsdp", 1 << taken[way])
            for way in (0, 1)
        )
        halves = [pick(halves[way], sides[way], places[way]) + got[way] for way in (0, 1)]
        for way in (0, 1):
            ways[way].remove(taken[way])
    part = jnp.concatenate(halves, axis=1)
    (part,) = yield (part,)
    (got,) = yield (lax.all_to_all(part, "seq", split_axis=0, concat_axis=0, tiled=True),)
    own = jnp.sum(got.astype(f32), axis=0)
    results, at = [], 0
    for size in rows:
        results.append(own[at : at + size])
        at += size
    return results


def mm(a, b):
    return lax.dot_general(a, b, (((1,), (0,)), ((), ())), preferred_element_type=f32)


def mm_nt(a, b):
    return lax.dot_general(a, b, (((1,), (1,)), ((), ())), preferred_element_type=f32)


def mm_tn(a, b):
    return lax.dot_general(a, b, (((0,), (0,)), ((), ())), preferred_element_type=f32)


def sigmoid(v):
    return 0.5 + 0.5 * jnp.tanh(0.5 * v)


def rows_at():
    return lax.broadcasted_iota(jnp.int32, (ROWS, LANES), 0)


def lanes_at():
    return lax.broadcasted_iota(jnp.int32, (ROWS, LANES), 1)


def slab(i):
    return slice(i * LANES, (i + 1) * LANES)


def wide(i):
    return slice(i * 2 * LANES, (i + 1) * 2 * LANES)


def halves(columns, heads):
    lane = lanes_at()
    high = columns.astype(bf16).astype(f32)
    rest = pltpu.roll(columns - high, heads, 1)
    return jnp.where(lane < heads, high, jnp.where(lane < 2 * heads, rest, 0.0)).astype(bf16)


def low_lanes():
    return (lanes_at() < LANES // 2).astype(f32).astype(bf16), (lanes_at() >= LANES // 2).astype(f32).astype(bf16)


def diagonal(block, low, high):
    return jnp.concatenate([block * low, block * high], axis=0)


def parts_of_step():
    return [slice(part * ROWS, (part + 1) * ROWS) for part in range(GROUP)]


def params(**more):
    return pltpu.CompilerParams(vmem_limit_bytes=VMEM, **more)


def cost(microseconds):
    return pl.CostEstimate(flops=int(microseconds * 1e9), bytes_accessed=4 * 1024 * 1024, transcendentals=0)


def whole(shape):
    return pl.BlockSpec(shape, lambda i: (0,) * len(shape))


def by_rows(width, rows=GROUP * ROWS):
    return pl.BlockSpec((rows, width), lambda i: (i, 0))


def conv_kernel(span, rows, pieces, normed_ref, *refs):
    near_refs, far_refs = refs[:pieces], refs[pieces : 2 * pieces]
    taps_ref, bias_ref, act_ref, cin_ref, raw_ref, near_ref, far_ref, held = refs[2 * pieces :]
    at = pl.program_id(0)
    last = pl.num_programs(0) - 1
    near = jnp.concatenate([ref[...] for ref in near_refs], axis=0)
    far = jnp.concatenate([ref[...] for ref in far_refs], axis=0)
    near_ref[...] = near
    far_ref[...] = far
    half = near.shape[0]

    def projected(start, size):
        block = normed_ref[start : start + size, :]
        return mm(block[:, :half], near) + mm(block[:, half:], far)

    part = 256

    @pl.when(at == last)
    def _():
        for start in range(0, rows, part):
            raw_ref[start : start + part, :] = projected(HALO + start, part)[:, :LANES]

    @pl.when(at < last)
    def _():
        for start, size in [(0, HALO)] + [(HALO + at, part) for at in range(0, rows, part)]:
            block = projected(start, size).astype(bf16)
            cin_ref[start : start + size, :] = block
            held[start : start + size, :] = block.astype(f32)
        for start in range(0, rows, part):
            total = jnp.broadcast_to(bias_ref[0:1, :], (part, bias_ref.shape[1]))
            for k in range(span):
                first = HALO + start - (span - 1) + k
                total = total + taps_ref[k : k + 1, :] * held[first : first + part, :]
            act_ref[start : start + part, :] = (total * sigmoid(total)).astype(bf16)


def conv_forward(normed, near, far, taps, bias):
    rows, width = normed.shape[0] - HALO, normed.shape[1]
    channels = taps.shape[1]
    total = near[0].shape[1]
    cols = 2 * LANES
    blocks = channels // cols

    def columns(height, upto=blocks):
        return pl.BlockSpec((height, cols), lambda i: (0, jnp.minimum(i, upto)))

    return pl.pallas_call(
        functools.partial(conv_kernel, taps.shape[0], rows, len(near)),
        grid=(blocks + 1,),
        in_specs=[whole((rows + HALO, width))]
        + [columns(piece.shape[0]) for piece in near + far]
        + [columns(taps.shape[0], blocks - 1), columns(1, blocks - 1)],
        out_specs=[
            columns(rows, blocks - 1),
            columns(rows + HALO, blocks - 1),
            whole((rows, LANES)),
            columns(width // 2),
            columns(width // 2),
        ],
        out_shape=[
            jax.ShapeDtypeStruct((rows, channels), bf16),
            jax.ShapeDtypeStruct((rows + HALO, channels), bf16),
            jax.ShapeDtypeStruct((rows, LANES), f32),
            jax.ShapeDtypeStruct((width // 2, total), bf16),
            jax.ShapeDtypeStruct((width // 2, total), bf16),
        ],
        scratch_shapes=[pltpu.VMEM((rows + HALO, cols), f32)],
        compiler_params=params(),
        name="conv_forward",
        cost_estimate=cost(16),
    )(normed, *near, *far, taps, bias)


def steps_kernel(blocks, heads, raw_ref, bias_ref, alog_ref, step_ref, cum_ref, left_ref, right_ref, rows3):
    lane = lanes_at()
    lower = (rows_at() >= lane).astype(f32)
    rates = -jnp.exp(alog_ref[...])
    rows3[...] = jnp.zeros_like(rows3)
    for b in range(blocks):
        rows = slice(b * ROWS, (b + 1) * ROWS)
        soft = raw_ref[rows, :] + bias_ref[...]
        soft = jnp.maximum(soft, 0.0) + jnp.log1p(jnp.exp(-jnp.abs(soft)))
        step = soft.astype(bf16).astype(f32)
        step_ref[rows, :] = step
        cum = jnp.dot(lower, step * rates, precision=highest, preferred_element_type=f32)
        cum_ref[rows, :] = cum
        cum = cum * LOG2E
        parts, rest = [], cum
        for _ in range(3):
            part = rest.astype(bf16).astype(f32)
            parts.append(part)
            rest = rest - part
        left = jnp.where(lane < 3 * heads + 3, 1.0, 0.0)
        for k in (2, 1, 0):
            left = jnp.where(lane < (k + 1) * heads, pltpu.roll(parts[k], k * heads, 1), left)
        left_ref[rows, :] = left.astype(bf16)
        for k in range(3):
            flipped = -parts[k].T
            for h in range(heads):
                rows3[k : k + 1, slab(h)] = flipped[h : h + 1, :]
        right_ref[b * HALO : (b + 1) * HALO, :] = rows3[...].astype(bf16)


def steps_forward(raw, bias, a_log, heads):
    rows = raw.shape[0]
    blocks = rows // ROWS
    shape = jax.ShapeDtypeStruct((rows, LANES), f32)
    return pl.pallas_call(
        functools.partial(steps_kernel, blocks, heads),
        out_shape=[
            shape,
            shape,
            jax.ShapeDtypeStruct((rows, LANES), bf16),
            jax.ShapeDtypeStruct((blocks * HALO, heads * LANES), bf16),
        ],
        scratch_shapes=[pltpu.VMEM((HALO, heads * LANES), f32)],
        compiler_params=params(),
        name="steps_forward",
        cost_estimate=cost(6),
    )(raw, bias, a_log)


def state_kernel(heads, v_ref, b_ref, step_ref, cum_ref, etot_ref, fan_ref, x_ref, f_ref, state, tails, both):
    at = pl.program_id(0)

    @pl.when(at == 0)
    def _():
        state[...] = jnp.zeros_like(state)

    for part, r in enumerate(parts_of_step()):
        cum, step = cum_ref[r, :], step_ref[r, :]
        tail = jnp.exp(cum[ROWS - 1 :, :] - cum) * step
        both[...] = mm(jnp.concatenate([halves(step, heads), halves(tail, heads)], axis=0), fan_ref[...])
        v = v_ref[r, :].astype(f32)
        x_ref[r, :] = (v * both[:ROWS, :]).astype(bf16)
        tails[...] = (v * both[ROWS:, :]).astype(bf16)
        etot = etot_ref[pl.ds(at * GROUP + part, 1), :]
        state[...] = etot * state[...] + mm_tn(b_ref[r, :], tails[...])

    @pl.when(at == pl.num_programs(0) - 1)
    def _():
        f_ref[...] = state[...].astype(bf16)


def piece_state(act, step, cum, etot, fan, heads, inner, width):
    rows = act.shape[0]
    inputs_at = inner // width
    return pl.pallas_call(
        functools.partial(state_kernel, heads),
        grid=(rows // (GROUP * ROWS),),
        in_specs=[
            by_rows(inner),
            pl.BlockSpec((GROUP * ROWS, width), lambda i: (i, inputs_at)),
            by_rows(LANES),
            by_rows(LANES),
            whole(etot.shape),
            whole(fan.shape),
        ],
        out_specs=[by_rows(inner), whole((width, inner))],
        out_shape=[
            jax.ShapeDtypeStruct((rows, inner), bf16),
            jax.ShapeDtypeStruct((width, inner), bf16),
        ],
        scratch_shapes=[
            pltpu.VMEM((width, inner), f32),
            pltpu.VMEM((ROWS, inner), bf16),
            pltpu.VMEM((2 * ROWS, inner), f32),
        ],
        compiler_params=params(),
        name="piece_state",
        cost_estimate=cost(6),
    )(act, act, step, cum, etot, fan)


def inside_kernel(pairs, x_ref, b_ref, c_ref, left_ref, right_ref, still_ref, y_ref, right):
    fixed = left_rows(right, still_ref, right_ref)
    low, high = low_lanes()
    for part, r in enumerate(parts_of_step()):
        scores = jnp.where(rows_at() >= lanes_at(), mm_nt(c_ref[r, :], b_ref[r, :]), 0.0)
        scores = jnp.concatenate([scores, scores], axis=1)
        left = left_ref[r, :]
        for i in range(pairs):
            spread = mm(left, fixed[part, :, wide(i)])
            weights = (scores * jnp.exp2(jnp.minimum(spread, 0.0))).astype(bf16)
            y_ref[r, slab(i)] = mm(weights, diagonal(x_ref[r, slab(i)], low, high))


def left_rows(right, still_ref, right_ref):
    @pl.when(pl.program_id(0) == 0)
    def _():
        for part in range(GROUP):
            right[part, :, :] = still_ref[...]

    own = still_ref.shape[0] - 2 * HALO
    for part in range(GROUP):
        right[part, own : own + HALO, :] = right_ref[part * HALO : (part + 1) * HALO, :]
    return right


def inside_forward(x, act, left, right, still, inner, width):
    rows = act.shape[0]
    inputs_at = inner // width
    return pl.pallas_call(
        functools.partial(inside_kernel, inner // LANES),
        grid=(rows // (GROUP * ROWS),),
        in_specs=[
            by_rows(inner),
            pl.BlockSpec((GROUP * ROWS, width), lambda i: (i, inputs_at)),
            pl.BlockSpec((GROUP * ROWS, width), lambda i: (i, inputs_at + 1)),
            by_rows(LANES),
            by_rows(right.shape[1], GROUP * HALO),
            whole(still.shape),
        ],
        out_specs=by_rows(inner),
        out_shape=jax.ShapeDtypeStruct((rows, inner), f32),
        scratch_shapes=[pltpu.VMEM((GROUP,) + still.shape, bf16)],
        compiler_params=params(),
        name="inside_forward",
        cost_estimate=cost(10),
    )(x, act, act, left, right, still)


def gate_kernel(
    heads,
    pairs,
    y_ref,
    v_ref,
    b_ref,
    c_ref,
    z_ref,
    gn_ref,
    step_ref,
    cum_ref,
    etot_ref,
    ebef_ref,
    skip_ref,
    gain_ref,
    start_ref,
    ones_ref,
    fan_ref,
    out_ref,
    gm_ref,
    gz_ref,
    states_ref,
    pac_ref,
    back_ref,
    ggain_ref,
    gskip_ref,
    state,
    back,
    across,
    mixer,
    gated,
    early,
    tails,
    products,
    both,
):
    at = pl.program_id(0)
    width = pairs * LANES

    @pl.when(at == 0)
    def _():
        state[...] = start_ref[...]
        back[...] = jnp.zeros_like(back)
        ggain_ref[...] = jnp.zeros_like(ggain_ref)
        gskip_ref[...] = jnp.zeros_like(gskip_ref)

    for part, r in enumerate(parts_of_step()):
        outputs = c_ref[r, :]
        entering = state[...].astype(bf16)
        states_ref[part * state.shape[0] : (part + 1) * state.shape[0], :] = entering
        across[...] = mm(outputs, entering)
        cum = cum_ref[r, :]
        grow = jnp.exp(cum)
        tail = jnp.exp(cum[ROWS - 1 :, :] - cum) * step_ref[r, :]
        both[...] = mm(jnp.concatenate([halves(grow, heads), halves(tail, heads)], axis=0), fan_ref[...])
        squares = jnp.zeros((ROWS, LANES), f32)
        meets = jnp.zeros((ROWS, LANES), f32)
        for i in range(pairs):
            s = slab(i)
            v = v_ref[r, s].astype(f32)
            ya = across[:, s] * both[:ROWS, s]
            across[:, s] = ya
            m = (y_ref[r, s] + ya + skip_ref[:, s] * v).astype(bf16)
            mixer[:, s] = m
            z = z_ref[r, s]
            product = m.astype(f32) * (z * sigmoid(z))
            gated[:, s] = product
            squares = squares + product * product
            meets = meets + gn_ref[r, s] * gain_ref[:, s] * product
            tails[:, s] = (v * both[ROWS:, s]).astype(bf16)
        scale = lax.rsqrt(jnp.sum(squares, axis=1, keepdims=True) / width + epsilon)
        pull = scale * scale * scale * (jnp.sum(meets, axis=1, keepdims=True) / width)
        for i in range(pairs):
            s = slab(i)
            v = v_ref[r, s].astype(f32)
            product = gated[:, s]
            unit = product * scale
            gain = gain_ref[:, s]
            gn = gn_ref[r, s]
            out_ref[r, s] = (unit * gain).astype(bf16)
            ggain_ref[:, s] += jnp.sum(gn * unit, axis=0, keepdims=True)
            grad = gn * gain * scale - product * pull
            z = z_ref[r, s]
            sig = sigmoid(z)
            swish = z * sig
            gm = (grad * swish).astype(bf16)
            gm_ref[r, s] = gm
            slope = sig + swish * (1.0 - sig)
            gz_ref[r, s] = (grad * mixer[:, s].astype(f32) * slope).astype(bf16)
            g = gm.astype(f32)
            gskip_ref[:, s] += jnp.sum(g * v, axis=0, keepdims=True)
            products[:, s] = (g * across[:, s]).astype(bf16)
            early[:, s] = (g * both[:ROWS, s]).astype(bf16)
        pac_ref[r, :] = mm(products[...], ones_ref[...])
        block = at * GROUP + part
        back[...] += ebef_ref[pl.ds(block, 1), :] * mm_tn(outputs, early[...])
        state[...] = etot_ref[pl.ds(block, 1), :] * state[...] + mm_tn(b_ref[r, :], tails[...])

    @pl.when(at == pl.num_programs(0) - 1)
    def _():
        back_ref[...] = back[...].astype(bf16)


def gate_both(y, act, z, gn, step, cum, etot, ebef, skip, gain, start, ones, fan, heads, inner, width):
    rows = act.shape[0]
    inputs_at = inner // width
    blocks = rows // ROWS
    return pl.pallas_call(
        functools.partial(gate_kernel, heads, inner // LANES),
        grid=(blocks // GROUP,),
        in_specs=[
            by_rows(inner),
            by_rows(inner),
            pl.BlockSpec((GROUP * ROWS, width), lambda i: (i, inputs_at)),
            pl.BlockSpec((GROUP * ROWS, width), lambda i: (i, inputs_at + 1)),
            by_rows(inner),
            by_rows(inner),
            by_rows(LANES),
            by_rows(LANES),
            whole(etot.shape),
            whole(ebef.shape),
            whole((1, inner)),
            whole((1, inner)),
            whole((width, inner)),
            whole((inner, LANES)),
            whole(fan.shape),
        ],
        out_specs=[
            by_rows(inner),
            by_rows(inner),
            by_rows(inner),
            by_rows(inner, GROUP * width),
            by_rows(LANES),
            whole((width, inner)),
            whole((1, inner)),
            whole((1, inner)),
        ],
        out_shape=[
            jax.ShapeDtypeStruct((rows, inner), bf16),
            jax.ShapeDtypeStruct((rows, inner), bf16),
            jax.ShapeDtypeStruct((rows, inner), bf16),
            jax.ShapeDtypeStruct((blocks * width, inner), bf16),
            jax.ShapeDtypeStruct((rows, LANES), f32),
            jax.ShapeDtypeStruct((width, inner), bf16),
            jax.ShapeDtypeStruct((1, inner), f32),
            jax.ShapeDtypeStruct((1, inner), f32),
        ],
        scratch_shapes=[
            pltpu.VMEM((width, inner), f32),
            pltpu.VMEM((width, inner), f32),
            pltpu.VMEM((ROWS, inner), f32),
            pltpu.VMEM((ROWS, inner), bf16),
            pltpu.VMEM((ROWS, inner), f32),
            pltpu.VMEM((ROWS, inner), bf16),
            pltpu.VMEM((ROWS, inner), bf16),
            pltpu.VMEM((ROWS, inner), bf16),
            pltpu.VMEM((2 * ROWS, inner), f32),
        ],
        compiler_params=params(),
        name="gate_both",
        cost_estimate=cost(18),
    )(y, act, act, act, z, gn, step, cum, etot, ebef, skip, gain, start, ones, fan)


def inside_back_kernel(
    pairs, x_ref, b_ref, c_ref, g_ref, left_ref, right_ref, still_ref, taken_ref,
    dx_ref, db_ref, dc_ref, pq_ref, right, moved, late,
):
    fixed = left_rows(right, still_ref, right_ref)
    lane = lanes_at()
    low, high = low_lanes()
    ones = jnp.ones((16, ROWS), bf16)
    for part, r in enumerate(parts_of_step()):
        inputs, outputs = b_ref[r, :], c_ref[r, :]
        raw_scores = mm_nt(inputs, outputs)
        scores = jnp.where(rows_at() <= lane, raw_scores, 0.0)
        strict = jnp.where(rows_at() < lane, raw_scores, 0.0)
        scores = jnp.concatenate([scores, scores], axis=1)
        strict = jnp.concatenate([strict, strict], axis=1)
        left = -left_ref[r, :]
        gathered = jnp.zeros((ROWS, 2 * LANES), f32)
        for i in range(pairs):
            spread = mm(left, fixed[part, :, wide(i)])
            decay = jnp.exp2(jnp.minimum(spread, 0.0))
            stacked = diagonal(g_ref[r, slab(i)], low, high)
            grad = mm_nt(x_ref[r, slab(i)], stacked) * decay
            gathered = gathered + grad
            moved[:, wide(i)] = (grad * strict).astype(bf16)
            dx_ref[r, slab(i)] = mm((scores * decay).astype(bf16), stacked)
        late[...] = jnp.zeros_like(late)
        for i in range(pairs):
            sums = mm(ones, moved[:, wide(i)])
            late[2 * i : 2 * i + 1, :] = sums[0:1, :LANES]
            late[2 * i + 1 : 2 * i + 2, :] = sums[0:1, LANES:]
        pq_ref[r, :] = late[...].T - mm(moved[...], taken_ref[...])
        gathered = gathered[:, :LANES] + gathered[:, LANES:]
        gathered = jnp.where(rows_at() <= lane, gathered, 0.0).astype(bf16)
        db_ref[r, :] = mm(gathered, outputs)
        dc_ref[r, :] = mm_tn(gathered, inputs)


def inside_backward(x, act, gm, left, right, still, taken, inner, width):
    rows = act.shape[0]
    inputs_at = inner // width
    return pl.pallas_call(
        functools.partial(inside_back_kernel, inner // LANES),
        grid=(rows // (GROUP * ROWS),),
        in_specs=[
            by_rows(inner),
            pl.BlockSpec((GROUP * ROWS, width), lambda i: (i, inputs_at)),
            pl.BlockSpec((GROUP * ROWS, width), lambda i: (i, inputs_at + 1)),
            by_rows(inner),
            by_rows(LANES),
            by_rows(right.shape[1], GROUP * HALO),
            whole(still.shape),
            whole(taken.shape),
        ],
        out_specs=[by_rows(inner), by_rows(width), by_rows(width), by_rows(LANES)],
        out_shape=[
            jax.ShapeDtypeStruct((rows, inner), f32),
            jax.ShapeDtypeStruct((rows, width), f32),
            jax.ShapeDtypeStruct((rows, width), f32),
            jax.ShapeDtypeStruct((rows, LANES), f32),
        ],
        scratch_shapes=[
            pltpu.VMEM((GROUP,) + still.shape, bf16),
            pltpu.VMEM((ROWS, 2 * inner), bf16),
            pltpu.VMEM((LANES, ROWS), f32),
        ],
        compiler_params=params(),
        name="inside_backward",
        cost_estimate=cost(20),
    )(x, act, act, gm, left, right, still, taken)


def finish_kernel(
    heads,
    pairs,
    blocks,
    v_ref,
    x_ref,
    b_ref,
    c_ref,
    g_ref,
    dx_ref,
    db_ref,
    dc_ref,
    pq_ref,
    pac_ref,
    states_ref,
    step_ref,
    cum_ref,
    raw_ref,
    bias_ref,
    alog_ref,
    etot_ref,
    skip_ref,
    start_ref,
    ones_ref,
    fan_ref,
    gact_ref,
    graw_ref,
    gbias_ref,
    grate_ref,
    state,
    tails,
    early,
    first,
    second,
    third,
    spread,
    three,
):
    at = pl.program_id(0)
    step_at = blocks // GROUP - 1 - at
    inner = pairs * LANES
    width = state.shape[0]

    @pl.when(at == 0)
    def _():
        state[...] = start_ref[...]
        gbias_ref[...] = jnp.zeros_like(gbias_ref)
        grate_ref[...] = jnp.zeros_like(grate_ref)

    later = (rows_at() <= lanes_at()).astype(f32)
    earlier = (rows_at() > lanes_at()).astype(f32)
    rates = jnp.exp(alog_ref[...])
    for part, r in reversed(list(enumerate(parts_of_step()))):
        inputs, outputs = b_ref[r, :], c_ref[r, :]
        leaving = state[...]
        leaving_low = leaving.astype(bf16)
        entering = states_ref[part * width : (part + 1) * width, :]
        etot = etot_ref[pl.ds(step_at * GROUP + part, 1), :]
        held = jnp.sum(leaving * entering.astype(f32), axis=0, keepdims=True) * etot
        held = mm(jnp.broadcast_to(held, (8, inner)).astype(bf16), ones_ref[...])[0:1, :]
        spread[...] = mm(inputs, leaving_low)
        cum, step = cum_ref[r, :], step_ref[r, :]
        grow = jnp.exp(cum)
        tail = jnp.exp(cum[ROWS - 1 :, :] - cum)
        three[...] = mm(
            jnp.concatenate([halves(step, heads), halves(tail, heads), halves(grow, heads)], axis=0),
            fan_ref[...],
        )
        for i in range(pairs):
            s = slab(i)
            v = v_ref[r, s].astype(f32)
            g = g_ref[r, s].astype(f32)
            steps = three[:ROWS, s]
            x = x_ref[r, s].astype(f32)
            part_tail = three[ROWS : 2 * ROWS, s]
            more = spread[:, s] * part_tail
            dx = dx_ref[r, s] + more
            first[:, s] = (x * more).astype(bf16)
            direct = v * dx
            high = direct.astype(bf16)
            second[:, s] = high
            third[:, s] = (direct - high.astype(f32)).astype(bf16)
            gact_ref[r, s] = (steps * dx + skip_ref[:, s] * g).astype(bf16)
            tails[:, s] = (x * part_tail).astype(bf16)
            early[:, s] = (g * three[2 * ROWS :, s]).astype(bf16)
        gact_ref[r, inner : inner + width] = (db_ref[r, :] + mm_nt(tails[...], leaving_low)).astype(bf16)
        gact_ref[r, inner + width :] = (dc_ref[r, :] + mm_nt(early[...], entering)).astype(bf16)
        gdecay = (
            jnp.dot(later, pq_ref[r, :] + pac_ref[r, :], precision=highest, preferred_element_type=f32)
            + jnp.dot(
                earlier, mm(first[...], ones_ref[...]), precision=highest, preferred_element_type=f32
            )
            + held
        )
        gstep = mm(second[...], ones_ref[...]) + mm(third[...], ones_ref[...]) - rates * gdecay
        graw = gstep.astype(bf16).astype(f32) * sigmoid(raw_ref[r, :] + bias_ref[...])
        graw_ref[r, :] = graw.astype(bf16)
        gbias_ref[...] += jnp.sum(graw, axis=0, keepdims=True)
        grate_ref[...] += jnp.sum(step * gdecay, axis=0, keepdims=True)
        state[...] = etot * leaving + mm_tn(outputs, early[...])


def mixer_finish(
    act, x, gm, dx, db, dc, pq, pac, states, step, cum, raw, bias, a_log, etot, skip, start, ones, fan, heads, inner, width
):
    rows = act.shape[0]
    blocks = rows // ROWS
    inputs_at = inner // width
    channels = act.shape[1]

    def backwards(columns, height=GROUP * ROWS, column_at=0):
        return pl.BlockSpec((height, columns), lambda i: (blocks // GROUP - 1 - i, column_at))

    return pl.pallas_call(
        functools.partial(finish_kernel, heads, inner // LANES, blocks),
        grid=(blocks // GROUP,),
        in_specs=[
            backwards(inner),
            backwards(inner),
            backwards(width, column_at=inputs_at),
            backwards(width, column_at=inputs_at + 1),
            backwards(inner),
            backwards(inner),
            backwards(width),
            backwards(width),
            backwards(LANES),
            backwards(LANES),
            backwards(inner, GROUP * width),
            backwards(LANES),
            backwards(LANES),
            backwards(LANES),
            whole((1, LANES)),
            whole((1, LANES)),
            whole(etot.shape),
            whole((1, inner)),
            whole((width, inner)),
            whole((inner, LANES)),
            whole(fan.shape),
        ],
        out_specs=[backwards(channels), backwards(LANES), whole((1, LANES)), whole((1, LANES))],
        out_shape=[
            jax.ShapeDtypeStruct((rows, channels), bf16),
            jax.ShapeDtypeStruct((rows, LANES), bf16),
            jax.ShapeDtypeStruct((1, LANES), f32),
            jax.ShapeDtypeStruct((1, LANES), f32),
        ],
        scratch_shapes=[
            pltpu.VMEM((width, inner), f32),
            pltpu.VMEM((ROWS, inner), bf16),
            pltpu.VMEM((ROWS, inner), bf16),
            pltpu.VMEM((ROWS, inner), bf16),
            pltpu.VMEM((ROWS, inner), bf16),
            pltpu.VMEM((ROWS, inner), bf16),
            pltpu.VMEM((ROWS, inner), f32),
            pltpu.VMEM((3 * ROWS, inner), f32),
        ],
        compiler_params=params(),
        name="mixer_finish",
        cost_estimate=cost(16),
    )(act, x, act, act, gm, dx, db, dc, pq, pac, states, step, cum, raw, bias, a_log, etot, skip, start, ones, fan)


def conv_back_kernel(
    span, rows, blocks, cin_ref, gact_ref, graw_ref, taps_ref, bias_ref,
    gproj_ref, gtaps_ref, gbias_ref, top_ref, rest_ref, held, grads,
):
    part = 256
    at = pl.program_id(0)

    @pl.when(at == blocks)
    def _():
        gproj_ref[...] = graw_ref[...]

    @pl.when(at < blocks)
    def _():
        held[...] = cin_ref[...].astype(f32)
        grads[rows:, :] = jnp.zeros((HALO, LANES), f32)
        gbias = jnp.zeros((1, LANES), f32)
        gtaps = [jnp.zeros((1, LANES), f32)] * span
        for start in range(0, rows, part):
            total = jnp.broadcast_to(bias_ref[0:1, :], (part, LANES))
            seen = []
            for k in range(span):
                first = HALO + start - (span - 1) + k
                seen.append(held[first : first + part, :])
                total = total + taps_ref[k : k + 1, :] * seen[k]
            sig = sigmoid(total)
            grad = gact_ref[start : start + part, :].astype(f32) * (sig * (1.0 + total * (1.0 - sig)))
            grads[start : start + part, :] = grad
            gbias = gbias + jnp.sum(grad, axis=0, keepdims=True)
            for k in range(span):
                gtaps[k] = gtaps[k] + jnp.sum(seen[k] * grad, axis=0, keepdims=True)
        gbias_ref[...] = gbias
        for k in range(span):
            gtaps_ref[k : k + 1, :] = gtaps[k]
        top_ref[...] = grads[0:8, :]
        for start in range(0, rows, part):
            total = jnp.zeros((part, LANES), f32)
            for k in range(span):
                first = start + span - 1 - k
                total = total + taps_ref[k : k + 1, :] * grads[first : first + part, :]
            gproj_ref[start : start + part, :] = total.astype(bf16)
            if start + part == rows:
                rest_ref[...] = total[part - 8 :, :]


def conv_backward(cin, gact, graw, taps, bias):
    rows, channels = gact.shape
    blocks = channels // LANES
    span = taps.shape[0]

    def columns(height):
        return pl.BlockSpec((height, LANES), lambda i: (0, jnp.minimum(i, blocks - 1)))

    return pl.pallas_call(
        functools.partial(conv_back_kernel, span, rows, blocks),
        grid=(blocks + 1,),
        in_specs=[columns(rows + HALO), columns(rows), whole((rows, LANES)), columns(span), columns(1)],
        out_specs=[
            pl.BlockSpec((rows, LANES), lambda i: (0, i)),
            columns(span),
            columns(1),
            columns(8),
            columns(8),
        ],
        out_shape=[
            jax.ShapeDtypeStruct((rows, channels + LANES), bf16),
            jax.ShapeDtypeStruct((span, channels), f32),
            jax.ShapeDtypeStruct((1, channels), f32),
            jax.ShapeDtypeStruct((8, channels), f32),
            jax.ShapeDtypeStruct((8, channels), f32),
        ],
        scratch_shapes=[pltpu.VMEM((rows + HALO, LANES), f32), pltpu.VMEM((rows + HALO, LANES), f32)],
        compiler_params=params(),
        name="conv_backward",
        cost_estimate=cost(18),
    )(cin, gact, graw, taps, bias)


def local(
    tokens,
    norm_gain,
    in_weight,
    conv_weight,
    conv_bias,
    dt_bias,
    a_log,
    skip_gain,
    gate_gain,
    out_weight,
    cotangent,
):
    tokens, incoming = tokens[0], cotangent[0]
    rows, model = tokens.shape
    heads = a_log.shape[0]
    span, channels = conv_weight.shape
    inner = gate_gain.shape[0]
    width = (channels - inner) // 2
    head_width = inner // heads
    blocks = rows // ROWS
    pad = LANES - heads

    order = gathered_order()
    conv_flight = Flight(gather(jnp.pad(in_weight[:, inner:], ((0, 0), (0, pad)))))
    before = shifted(tokens[rows - HALO :], "seq", 1)

    def first_norm(block):
        block = block.astype(f32)
        scale = lax.rsqrt(jnp.mean(block * block, axis=1, keepdims=True) + epsilon)
        return (block * scale * norm_gain).astype(bf16), scale

    own, own_scale = first_norm(tokens)
    gate_part, out_weight, own = conv_flight.step(in_weight[:, :inner], out_weight, own)
    w_gate = lax.all_gather(gate_part, "fsdp", axis=0, tiled=True)
    w_out = lax.all_gather(out_weight, "fsdp", axis=0, tiled=True)
    own_turned = in_order(own, order)
    turned = jnp.concatenate([in_order(first_norm(before)[0], order), own_turned], axis=0)
    conv_near, conv_far = conv_flight.finish()
    act, cin, raw, conv_near, conv_far = conv_forward(turned, conv_near, conv_far, conv_weight, conv_bias[None])
    bias_row = jnp.pad(dt_bias, (0, pad))[None]
    alog_row = jnp.pad(a_log, (0, pad))[None]
    step, cum, left, right = steps_forward(raw, bias_row, alog_row, heads)

    totals = cum.reshape(blocks, ROWS, LANES)[:, -1, :heads]
    befores = jnp.cumsum(totals, axis=0) - totals
    etot = jnp.repeat(jnp.exp(totals), head_width, axis=1)
    ebef = jnp.repeat(jnp.exp(befores), head_width, axis=1)
    skip = jnp.repeat(skip_gain, head_width)[None]
    def fanned(count, each):
        row, column = np.arange(LANES)[:, None], np.arange(count)[None]
        return ((row < 3 * heads) & (row % heads == column // each)).astype(ml_dtypes.bfloat16)

    def gathering(count, each):
        return (np.arange(count)[:, None] // each == np.arange(LANES)[None]).astype(ml_dtypes.bfloat16)

    fan = fanned(inner, head_width)
    still = fanned(heads * LANES, LANES)
    ones = gathering(inner, head_width)
    taken = gathering(heads * LANES, LANES)
    whole_decay = jnp.repeat(jnp.exp(jnp.sum(totals, axis=0)), head_width)[None]

    x, leaves = piece_state(act, step, cum, etot, fan, heads, inner, width)
    ahead = Flight(handed_on(leaves, whole_decay, 1))
    y = inside_forward(x, act, left, right, still, inner, width)
    y = ahead.step(y)
    z = mm(own, w_gate)
    z = ahead.step(z)
    gn = mm_nt(incoming, w_out)
    gn = ahead.step(gn)
    start = ahead.finish()
    out_in, gm, gz, states, pac, back, ggain, gskip = gate_both(
        y, act, z, gn, step, cum, etot, ebef, skip, gate_gain[None], start, ones, fan, heads, inner, width
    )

    behind = Flight(handed_on(back, whole_decay, -1))
    part_out = mm_tn(out_in, incoming).astype(bf16)
    part_gate = mm_tn(own, gz).astype(bf16)
    part_out, part_gate = behind.step(part_out, part_gate)
    slices = inner // model
    sums = Flight(
        sum_scatter([part_out] + [part_gate[:, i * model : (i + 1) * model] for i in range(slices)])
    )
    pulled_gate = mm_nt(gz, w_gate)
    pulled_gate = behind.step(pulled_gate)
    pulled_gate, gm = sums.step(pulled_gate, gm)
    dx, db, dc, pq = inside_backward(x, act, gm, left, right, still, taken, inner, width)
    dx = behind.step(dx)
    dx = sums.step(dx)
    back_start = behind.finish()
    gact, graw, gdt, grate = mixer_finish(
        act, x, gm, dx, db, dc, pq, pac, states, step, cum, raw, bias_row, alog_row, etot, skip,
        back_start, ones, fan, heads, inner, width,
    )
    gact = sums.step(gact)
    cin = sums.step(cin)
    gproj, gtaps, gcbias, top, rest = conv_backward(cin, gact, graw, conv_weight, conv_bias[None])
    nexts = shifted(top, "seq", -1)
    mixed = (tokens.astype(f32) + mm(out_in, w_out)).astype(bf16)
    nexts, mixed = lax.optimization_barrier((nexts, mixed))
    gproj = sums.step(gproj)
    owed = jnp.zeros((8, channels), f32)
    for k in range(span - 1):
        reach = span - 1 - k
        owed = owed + jnp.pad(conv_weight[k] * nexts[:reach], ((8 - reach, 0), (0, 0)))
    gproj = lax.dynamic_update_slice(gproj, (rest + owed).astype(bf16), (rows - 8, 0))

    part_conv = mm_tn(own, gproj).astype(bf16)
    conv_sums = Flight(sum_scatter([part_conv]))
    pulled_conv = jnp.concatenate([mm_nt(gproj, conv_near), mm_nt(gproj, conv_far)], axis=1)
    pulled_conv = conv_sums.step(pulled_conv)
    places = [sum(jnp.where(at == block, i, 0) for i, at in enumerate(order)) for block in range(len(order))]
    grad_normed = pulled_gate + in_order(pulled_conv, places)
    unit = tokens.astype(f32) * own_scale
    pulled = grad_normed * norm_gain
    mean_pull = jnp.mean(pulled * unit, axis=1, keepdims=True)
    grad_tokens = incoming.astype(f32) + own_scale * (pulled - unit * mean_pull)
    grad_norm_gain = jnp.sum(grad_normed * unit, axis=0)
    small = [
        grad_norm_gain,
        gtaps.reshape(-1),
        gcbias[0],
        gdt[0, :heads],
        grate[0, :heads] * -jnp.exp(a_log),
        jnp.sum(gskip.reshape(heads, head_width), axis=1),
        ggain[0],
    ]
    small_sums = Flight(sum_all(jnp.concatenate(small)))
    small_sums.flying = conv_sums.step(*small_sums.flying, grad_tokens)[:1]
    small_sums.advance(small_sums.flying)
    summed_parts = sums.finish()
    grad_out_weight = summed_parts[0]
    (grad_conv_part,) = conv_sums.finish()
    summed = small_sums.finish()

    grad_in_weight = jnp.concatenate(
        summed_parts[1:] + [grad_conv_part[:, : channels + heads]], axis=1
    )
    sizes = [part.shape[0] for part in small]
    split, at = [], 0
    for size in sizes:
        split.append(summed[at : at + size])
        at += size
    return (
        mixed[None],
        grad_tokens[None],
        grad_in_weight,
        grad_out_weight,
        split[0],
        split[1].reshape(span, channels),
        *split[2:],
    )


def solution(mesh):
    tokens = P("fsdp", "seq", None)
    sharded = P("fsdp", None)
    spread = P(("seq", "fsdp"), None)
    return jax.shard_map(
        local,
        mesh=mesh,
        in_specs=(tokens, P(), sharded, P(), P(), P(), P(), P(), P(), sharded, tokens),
        out_specs=(tokens, tokens, spread, spread, P(), P(), P(), P(), P(), P(), P()),
        check_vma=False,
    )
```

```python
import functools

import jax
import jax.numpy as jnp
import ml_dtypes
import numpy as np
from jax import lax
from jax.experimental import pallas as pl
from jax.experimental.pallas import tpu as pltpu
from jax.sharding import PartitionSpec as P

ROWS = 128
GROUP = 2
LANES = 128
HALO = 16
VMEM = 48 * 1024 * 1024
LOG2E = 1.4426950408889634
epsilon = 1e-05
bf16 = jnp.bfloat16
f32 = jnp.float32
highest = lax.Precision.HIGHEST


def shifted(block, axis, distance):
    size = lax.axis_size(axis)
    route = [(i - distance, i) for i in range(size) if 0 <= i - distance < size]
    return lax.ppermute(block, axis, route)


def exchanged(block, axis, bit):
    return lax.ppermute(block, axis, [(i, i ^ bit) for i in range(lax.axis_size(axis))])


def pick(block, at, axis):
    return lax.dynamic_index_in_dim(block, at, axis, keepdims=False)


class Flight:
    def __init__(self, steps):
        self.steps, self.value, self.flying = steps, None, None
        self.advance(None)

    def advance(self, arrived):
        try:
            self.flying = self.steps.send(arrived)
        except StopIteration as end:
            self.flying, self.value = None, end.value

    def step(self, *others):
        if self.flying is not None:
            count = len(self.flying)
            tied = lax.optimization_barrier((*self.flying, *others))
            others = tied[count:]
            self.advance(tuple(tied[:count]))
        return others[0] if len(others) == 1 else others

    def finish(self):
        while self.flying is not None:
            self.advance(self.flying)
        return self.value


def gather(weight):
    rows = weight.shape[0]
    if lax.axis_size("fsdp") != 8 or rows % 32:
        full = lax.all_gather(weight, "fsdp", axis=0, tiled=True)
        return [full[: full.shape[0] // 2]], [full[full.shape[0] // 2 :]]
    first, last = weight[: rows // 2], weight[rows // 2 :]

    def crossed(block):
        return exchanged(block, "fsdp", 1)

    first_y, last_x = exchanged(first, "fsdp", 4), exchanged(last, "fsdp", 2)
    first_x, last_y = exchanged(first, "fsdp", 2), exchanged(last, "fsdp", 4)
    far = [crossed(weight)]
    first_y, last_x, first_x, last_y = yield first_y, last_x, first_x, last_y
    first_xy, last_xy = exchanged(first_y, "fsdp", 2), exchanged(last_x, "fsdp", 4)
    far += [crossed(block) for block in (first_x, last_x, first_y, last_y)]
    first_xy, last_xy, *far = yield first_xy, last_xy, *far
    far += [crossed(first_xy), crossed(last_xy)]
    far = yield tuple(far)
    return [weight, first_x, last_x, first_y, last_y, first_xy, last_xy], list(far)


def gathered_order():
    group = lax.axis_size("fsdp")
    if group != 8:
        return list(range(group))
    me = lax.axis_index("fsdp")
    return [me ^ distance for distance in (0, 2, 4, 6, 1, 3, 5, 7)]


def in_order(block, order):
    size = block.shape[1] // len(order)
    return jnp.concatenate(
        [lax.dynamic_slice_in_dim(block, at * size, size, axis=1) for at in order], axis=1
    )


def handed_on(state, decay, distance):
    entering = jnp.zeros(state.shape, f32)
    state = state.astype(f32)
    for _ in range(lax.axis_size("seq") - 1):
        leaving = (state + decay * entering).astype(bf16)
        (arrived,) = yield (shifted(leaving, "seq", distance),)
        entering = arrived.astype(f32)
    return entering


def sum_all(vector):
    for axis in ("fsdp", "seq"):
        size = lax.axis_size(axis)
        if size & (size - 1):
            vector = lax.psum(vector, axis)
            continue
        for bit in range(size.bit_length() - 1):
            (other,) = yield (exchanged(vector, axis, 1 << bit),)
            vector = vector + other
    return vector


def sum_scatter(parts):
    pieces, group = lax.axis_size("seq"), lax.axis_size("fsdp")
    bits = group.bit_length() - 1
    columns = parts[0].shape[1]
    rows = [part.shape[0] // (pieces * group) for part in parts]
    total = sum(rows)
    if group != 1 << bits or bits < 1 or total % 2:
        return [
            lax.psum_scatter(part.astype(f32), ("seq", "fsdp"), scatter_dimension=0, tiled=True)
            for part in parts
        ]
    me = lax.axis_index("fsdp")
    parts = [part.reshape(pieces, group // 2, 2, -1, columns) for part in parts]
    mine = me & 1
    (got,) = yield (
        exchanged(jnp.concatenate([pick(part, 1 - mine, 2) for part in parts], axis=2), "fsdp", 1),
    )
    block = jnp.concatenate([pick(part, mine, 2) for part in parts], axis=2) + got
    ways = [list(range(bits - 1, 0, -1)), list(range(bits - 1, 0, -1))]
    halves = [
        part.reshape((pieces,) + (2,) * (bits - 1) + part.shape[2:])
        for part in (block[:, :, : total // 2], block[:, :, total // 2 :])
    ]
    for _ in range(bits - 1):
        taken = [ways[0][-1], ways[1][0]]
        places = [1 + ways[way].index(taken[way]) for way in (0, 1)]
        sides = [(me >> taken[way]) & 1 for way in (0, 1)]
        got = yield tuple(
            exchanged(pick(halves[way], 1 - sides[way], places[way]), "fsdp", 1 << taken[way])
            for way in (0, 1)
        )
        halves = [pick(halves[way], sides[way], places[way]) + got[way] for way in (0, 1)]
        for way in (0, 1):
            ways[way].remove(taken[way])
    part = jnp.concatenate(halves, axis=1)
    (part,) = yield (part,)
    place = lax.axis_index("seq")
    got = yield tuple(
        lax.ppermute(
            pick(part, (place + ahead) % pieces, 0), "seq", [(i, (i + ahead) % pieces) for i in range(pieces)]
        )
        for ahead in range(1, pieces)
    )
    own = sum((block.astype(f32) for block in got), pick(part, place, 0).astype(f32))
    results, at = [], 0
    for size in rows:
        results.append(own[at : at + size])
        at += size
    return results


def mm(a, b):
    return lax.dot_general(a, b, (((1,), (0,)), ((), ())), preferred_element_type=f32)


def mm_nt(a, b):
    return lax.dot_general(a, b, (((1,), (1,)), ((), ())), preferred_element_type=f32)


def mm_tn(a, b):
    return lax.dot_general(a, b, (((0,), (0,)), ((), ())), preferred_element_type=f32)


def sigmoid(v):
    return 0.5 + 0.5 * jnp.tanh(0.5 * v)


def rows_at():
    return lax.broadcasted_iota(jnp.int32, (ROWS, LANES), 0)


def lanes_at():
    return lax.broadcasted_iota(jnp.int32, (ROWS, LANES), 1)


def slab(i):
    return slice(i * LANES, (i + 1) * LANES)


def wide(i):
    return slice(i * 2 * LANES, (i + 1) * 2 * LANES)


def halves(columns, heads):
    lane = lanes_at()
    high = columns.astype(bf16).astype(f32)
    rest = pltpu.roll(columns - high, heads, 1)
    return jnp.where(lane < heads, high, jnp.where(lane < 2 * heads, rest, 0.0)).astype(bf16)


def low_lanes():
    return (lanes_at() < LANES // 2).astype(f32).astype(bf16), (lanes_at() >= LANES // 2).astype(f32).astype(bf16)


def diagonal(block, low, high):
    return jnp.concatenate([block * low, block * high], axis=0)


def parts_of_step():
    return [slice(part * ROWS, (part + 1) * ROWS) for part in range(GROUP)]


def params(**more):
    return pltpu.CompilerParams(vmem_limit_bytes=VMEM, **more)


def cost(microseconds):
    return pl.CostEstimate(flops=int(microseconds * 1e9), bytes_accessed=4 * 1024 * 1024, transcendentals=0)


def whole(shape):
    return pl.BlockSpec(shape, lambda i: (0,) * len(shape))


def by_rows(width, rows=GROUP * ROWS):
    return pl.BlockSpec((rows, width), lambda i: (i, 0))


def conv_kernel(span, rows, pieces, order_ref, before_ref, own_ref, *refs):
    near_refs, far_refs = refs[:pieces], refs[pieces : 2 * pieces]
    taps_ref, bias_ref, act_ref, cin_ref, raw_ref, near_ref, far_ref, held, normed_ref = refs[2 * pieces :]
    at = pl.program_id(0)
    last = pl.num_programs(0) - 1
    near = jnp.concatenate([ref[...] for ref in near_refs], axis=0)
    far = jnp.concatenate([ref[...] for ref in far_refs], axis=0)
    near_ref[...] = near
    far_ref[...] = far
    half = near.shape[0]
    size = own_ref.shape[1] // order_ref.shape[0]

    @pl.when(at == 0)
    def _():
        for i in range(order_ref.shape[0]):
            source = pl.ds(pl.multiple_of(order_ref[i] * size, size), size)
            normed_ref[:HALO, i * size : (i + 1) * size] = before_ref[:, source]
            normed_ref[HALO:, i * size : (i + 1) * size] = own_ref[:, source]

    def projected(start, size):
        block = normed_ref[start : start + size, :]
        return mm(block[:, :half], near) + mm(block[:, half:], far)

    part = 256

    @pl.when(at == last)
    def _():
        for start in range(0, rows, part):
            raw_ref[start : start + part, :] = projected(HALO + start, part)[:, :LANES]

    @pl.when(at < last)
    def _():
        for start, size in [(0, HALO)] + [(HALO + at, part) for at in range(0, rows, part)]:
            block = projected(start, size).astype(bf16)
            cin_ref[start : start + size, :] = block
            held[start : start + size, :] = block.astype(f32)
        for start in range(0, rows, part):
            total = jnp.broadcast_to(bias_ref[0:1, :], (part, bias_ref.shape[1]))
            for k in range(span):
                first = HALO + start - (span - 1) + k
                total = total + taps_ref[k : k + 1, :] * held[first : first + part, :]
            act_ref[start : start + part, :] = (total * sigmoid(total)).astype(bf16)


def conv_forward(order, before, own, near, far, taps, bias):
    rows, width = own.shape
    channels = taps.shape[1]
    total = near[0].shape[1]
    cols = 2 * LANES
    blocks = channels // cols

    def columns(height, upto=blocks):
        return pl.BlockSpec((height, cols), lambda i: (0, jnp.minimum(i, upto)))

    return pl.pallas_call(
        functools.partial(conv_kernel, taps.shape[0], rows, len(near)),
        grid=(blocks + 1,),
        in_specs=[pl.BlockSpec(memory_space=pltpu.SMEM), whole((HALO, width)), whole((rows, width))]
        + [columns(piece.shape[0]) for piece in near + far]
        + [columns(taps.shape[0], blocks - 1), columns(1, blocks - 1)],
        out_specs=[
            columns(rows, blocks - 1),
            columns(rows + HALO, blocks - 1),
            whole((rows, LANES)),
            columns(width // 2),
            columns(width // 2),
        ],
        out_shape=[
            jax.ShapeDtypeStruct((rows, channels), bf16),
            jax.ShapeDtypeStruct((rows + HALO, channels), bf16),
            jax.ShapeDtypeStruct((rows, LANES), f32),
            jax.ShapeDtypeStruct((width // 2, total), bf16),
            jax.ShapeDtypeStruct((width // 2, total), bf16),
        ],
        scratch_shapes=[pltpu.VMEM((rows + HALO, cols), f32), pltpu.VMEM((rows + HALO, width), bf16)],
        compiler_params=params(),
        name="conv_forward",
        cost_estimate=cost(16),
    )(order, before, own, *near, *far, taps, bias)


def steps_kernel(blocks, heads, raw_ref, bias_ref, alog_ref, step_ref, cum_ref, left_ref, right_ref, rows3):
    lane = lanes_at()
    lower = (rows_at() >= lane).astype(f32)
    rates = -jnp.exp(alog_ref[...])
    rows3[...] = jnp.zeros_like(rows3)
    for b in range(blocks):
        rows = slice(b * ROWS, (b + 1) * ROWS)
        soft = raw_ref[rows, :] + bias_ref[...]
        soft = jnp.maximum(soft, 0.0) + jnp.log1p(jnp.exp(-jnp.abs(soft)))
        step = soft.astype(bf16).astype(f32)
        step_ref[rows, :] = step
        cum = jnp.dot(lower, step * rates, precision=highest, preferred_element_type=f32)
        cum_ref[rows, :] = cum
        cum = cum * LOG2E
        parts, rest = [], cum
        for _ in range(3):
            part = rest.astype(bf16).astype(f32)
            parts.append(part)
            rest = rest - part
        left = jnp.where(lane < 3 * heads + 3, 1.0, 0.0)
        for k in (2, 1, 0):
            left = jnp.where(lane < (k + 1) * heads, pltpu.roll(parts[k], k * heads, 1), left)
        left_ref[rows, :] = left.astype(bf16)
        for k in range(3):
            flipped = -parts[k].T
            for h in range(heads):
                rows3[k : k + 1, slab(h)] = flipped[h : h + 1, :]
        right_ref[b * HALO : (b + 1) * HALO, :] = rows3[...].astype(bf16)


def steps_forward(raw, bias, a_log, heads):
    rows = raw.shape[0]
    blocks = rows // ROWS
    shape = jax.ShapeDtypeStruct((rows, LANES), f32)
    return pl.pallas_call(
        functools.partial(steps_kernel, blocks, heads),
        out_shape=[
            shape,
            shape,
            jax.ShapeDtypeStruct((rows, LANES), bf16),
            jax.ShapeDtypeStruct((blocks * HALO, heads * LANES), bf16),
        ],
        scratch_shapes=[pltpu.VMEM((HALO, heads * LANES), f32)],
        compiler_params=params(),
        name="steps_forward",
        cost_estimate=cost(6),
    )(raw, bias, a_log)


def state_kernel(heads, v_ref, b_ref, step_ref, cum_ref, etot_ref, fan_ref, x_ref, f_ref, state, tails, both):
    at = pl.program_id(0)

    @pl.when(at == 0)
    def _():
        state[...] = jnp.zeros_like(state)

    for part, r in enumerate(parts_of_step()):
        cum, step = cum_ref[r, :], step_ref[r, :]
        tail = jnp.exp(cum[ROWS - 1 :, :] - cum) * step
        both[...] = mm(jnp.concatenate([halves(step, heads), halves(tail, heads)], axis=0), fan_ref[...])
        v = v_ref[r, :].astype(f32)
        x_ref[r, :] = (v * both[:ROWS, :]).astype(bf16)
        tails[...] = (v * both[ROWS:, :]).astype(bf16)
        etot = etot_ref[pl.ds(at * GROUP + part, 1), :]
        state[...] = etot * state[...] + mm_tn(b_ref[r, :], tails[...])

    @pl.when(at == pl.num_programs(0) - 1)
    def _():
        f_ref[...] = state[...].astype(bf16)


def piece_state(act, step, cum, etot, fan, heads, inner, width):
    rows = act.shape[0]
    inputs_at = inner // width
    return pl.pallas_call(
        functools.partial(state_kernel, heads),
        grid=(rows // (GROUP * ROWS),),
        in_specs=[
            by_rows(inner),
            pl.BlockSpec((GROUP * ROWS, width), lambda i: (i, inputs_at)),
            by_rows(LANES),
            by_rows(LANES),
            whole(etot.shape),
            whole(fan.shape),
        ],
        out_specs=[by_rows(inner), whole((width, inner))],
        out_shape=[
            jax.ShapeDtypeStruct((rows, inner), bf16),
            jax.ShapeDtypeStruct((width, inner), bf16),
        ],
        scratch_shapes=[
            pltpu.VMEM((width, inner), f32),
            pltpu.VMEM((ROWS, inner), bf16),
            pltpu.VMEM((2 * ROWS, inner), f32),
        ],
        compiler_params=params(),
        name="piece_state",
        cost_estimate=cost(6),
    )(act, act, step, cum, etot, fan)


def inside_kernel(pairs, x_ref, b_ref, c_ref, left_ref, right_ref, still_ref, y_ref, right):
    fixed = left_rows(right, still_ref, right_ref)
    low, high = low_lanes()
    for part, r in enumerate(parts_of_step()):
        scores = jnp.where(rows_at() >= lanes_at(), mm_nt(c_ref[r, :], b_ref[r, :]), 0.0)
        scores = jnp.concatenate([scores, scores], axis=1)
        left = left_ref[r, :]
        for i in range(pairs):
            spread = mm(left, fixed[part, :, wide(i)])
            weights = (scores * jnp.exp2(jnp.minimum(spread, 0.0))).astype(bf16)
            y_ref[r, slab(i)] = mm(weights, diagonal(x_ref[r, slab(i)], low, high))


def left_rows(right, still_ref, right_ref):
    @pl.when(pl.program_id(0) == 0)
    def _():
        for part in range(GROUP):
            right[part, :, :] = still_ref[...]

    own = still_ref.shape[0] - 2 * HALO
    for part in range(GROUP):
        right[part, own : own + HALO, :] = right_ref[part * HALO : (part + 1) * HALO, :]
    return right


def inside_forward(x, act, left, right, still, inner, width):
    rows = act.shape[0]
    inputs_at = inner // width
    return pl.pallas_call(
        functools.partial(inside_kernel, inner // LANES),
        grid=(rows // (GROUP * ROWS),),
        in_specs=[
            by_rows(inner),
            pl.BlockSpec((GROUP * ROWS, width), lambda i: (i, inputs_at)),
            pl.BlockSpec((GROUP * ROWS, width), lambda i: (i, inputs_at + 1)),
            by_rows(LANES),
            by_rows(right.shape[1], GROUP * HALO),
            whole(still.shape),
        ],
        out_specs=by_rows(inner),
        out_shape=jax.ShapeDtypeStruct((rows, inner), f32),
        scratch_shapes=[pltpu.VMEM((GROUP,) + still.shape, bf16)],
        compiler_params=params(),
        name="inside_forward",
        cost_estimate=cost(10),
    )(x, act, act, left, right, still)


def gate_kernel(
    heads,
    pairs,
    y_ref,
    v_ref,
    b_ref,
    c_ref,
    z_ref,
    gn_ref,
    step_ref,
    cum_ref,
    etot_ref,
    ebef_ref,
    skip_ref,
    gain_ref,
    start_ref,
    ones_ref,
    fan_ref,
    out_ref,
    gm_ref,
    gz_ref,
    states_ref,
    pac_ref,
    back_ref,
    ggain_ref,
    gskip_ref,
    state,
    back,
    across,
    mixer,
    gated,
    early,
    tails,
    products,
    both,
):
    at = pl.program_id(0)
    width = pairs * LANES

    @pl.when(at == 0)
    def _():
        state[...] = start_ref[...]
        back[...] = jnp.zeros_like(back)
        ggain_ref[...] = jnp.zeros_like(ggain_ref)
        gskip_ref[...] = jnp.zeros_like(gskip_ref)

    for part, r in enumerate(parts_of_step()):
        outputs = c_ref[r, :]
        entering = state[...].astype(bf16)
        states_ref[part * state.shape[0] : (part + 1) * state.shape[0], :] = entering
        across[...] = mm(outputs, entering)
        cum = cum_ref[r, :]
        grow = jnp.exp(cum)
        tail = jnp.exp(cum[ROWS - 1 :, :] - cum) * step_ref[r, :]
        both[...] = mm(jnp.concatenate([halves(grow, heads), halves(tail, heads)], axis=0), fan_ref[...])
        squares = jnp.zeros((ROWS, LANES), f32)
        meets = jnp.zeros((ROWS, LANES), f32)
        for i in range(pairs):
            s = slab(i)
            v = v_ref[r, s].astype(f32)
            ya = across[:, s] * both[:ROWS, s]
            across[:, s] = ya
            m = (y_ref[r, s] + ya + skip_ref[:, s] * v).astype(bf16)
            mixer[:, s] = m
            z = z_ref[r, s]
            product = m.astype(f32) * (z * sigmoid(z))
            gated[:, s] = product
            squares = squares + product * product
            meets = meets + gn_ref[r, s] * gain_ref[:, s] * product
            tails[:, s] = (v * both[ROWS:, s]).astype(bf16)
        scale = lax.rsqrt(jnp.sum(squares, axis=1, keepdims=True) / width + epsilon)
        pull = scale * scale * scale * (jnp.sum(meets, axis=1, keepdims=True) / width)
        for i in range(pairs):
            s = slab(i)
            v = v_ref[r, s].astype(f32)
            product = gated[:, s]
            unit = product * scale
            gain = gain_ref[:, s]
            gn = gn_ref[r, s]
            out_ref[r, s] = (unit * gain).astype(bf16)
            ggain_ref[:, s] += jnp.sum(gn * unit, axis=0, keepdims=True)
            grad = gn * gain * scale - product * pull
            z = z_ref[r, s]
            sig = sigmoid(z)
            swish = z * sig
            gm = (grad * swish).astype(bf16)
            gm_ref[r, s] = gm
            slope = sig + swish * (1.0 - sig)
            gz_ref[r, s] = (grad * mixer[:, s].astype(f32) * slope).astype(bf16)
            g = gm.astype(f32)
            gskip_ref[:, s] += jnp.sum(g * v, axis=0, keepdims=True)
            products[:, s] = (g * across[:, s]).astype(bf16)
            early[:, s] = (g * both[:ROWS, s]).astype(bf16)
        pac_ref[r, :] = mm(products[...], ones_ref[...])
        block = at * GROUP + part
        back[...] += ebef_ref[pl.ds(block, 1), :] * mm_tn(outputs, early[...])
        state[...] = etot_ref[pl.ds(block, 1), :] * state[...] + mm_tn(b_ref[r, :], tails[...])

    @pl.when(at == pl.num_programs(0) - 1)
    def _():
        back_ref[...] = back[...].astype(bf16)


def gate_both(y, act, z, gn, step, cum, etot, ebef, skip, gain, start, ones, fan, heads, inner, width):
    rows = act.shape[0]
    inputs_at = inner // width
    blocks = rows // ROWS
    return pl.pallas_call(
        functools.partial(gate_kernel, heads, inner // LANES),
        grid=(blocks // GROUP,),
        in_specs=[
            by_rows(inner),
            by_rows(inner),
            pl.BlockSpec((GROUP * ROWS, width), lambda i: (i, inputs_at)),
            pl.BlockSpec((GROUP * ROWS, width), lambda i: (i, inputs_at + 1)),
            by_rows(inner),
            by_rows(inner),
            by_rows(LANES),
            by_rows(LANES),
            whole(etot.shape),
            whole(ebef.shape),
            whole((1, inner)),
            whole((1, inner)),
            whole((width, inner)),
            whole((inner, LANES)),
            whole(fan.shape),
        ],
        out_specs=[
            by_rows(inner),
            by_rows(inner),
            by_rows(inner),
            by_rows(inner, GROUP * width),
            by_rows(LANES),
            whole((width, inner)),
            whole((1, inner)),
            whole((1, inner)),
        ],
        out_shape=[
            jax.ShapeDtypeStruct((rows, inner), bf16),
            jax.ShapeDtypeStruct((rows, inner), bf16),
            jax.ShapeDtypeStruct((rows, inner), bf16),
            jax.ShapeDtypeStruct((blocks * width, inner), bf16),
            jax.ShapeDtypeStruct((rows, LANES), f32),
            jax.ShapeDtypeStruct((width, inner), bf16),
            jax.ShapeDtypeStruct((1, inner), f32),
            jax.ShapeDtypeStruct((1, inner), f32),
        ],
        scratch_shapes=[
            pltpu.VMEM((width, inner), f32),
            pltpu.VMEM((width, inner), f32),
            pltpu.VMEM((ROWS, inner), f32),
            pltpu.VMEM((ROWS, inner), bf16),
            pltpu.VMEM((ROWS, inner), f32),
            pltpu.VMEM((ROWS, inner), bf16),
            pltpu.VMEM((ROWS, inner), bf16),
            pltpu.VMEM((ROWS, inner), bf16),
            pltpu.VMEM((2 * ROWS, inner), f32),
        ],
        compiler_params=params(),
        name="gate_both",
        cost_estimate=cost(18),
    )(y, act, act, act, z, gn, step, cum, etot, ebef, skip, gain, start, ones, fan)


def inside_back_kernel(
    pairs, x_ref, b_ref, c_ref, g_ref, left_ref, right_ref, still_ref, taken_ref,
    dx_ref, db_ref, dc_ref, pq_ref, right, moved, late,
):
    fixed = left_rows(right, still_ref, right_ref)
    lane = lanes_at()
    low, high = low_lanes()
    ones = jnp.ones((16, ROWS), bf16)
    for part, r in enumerate(parts_of_step()):
        inputs, outputs = b_ref[r, :], c_ref[r, :]
        raw_scores = mm_nt(inputs, outputs)
        scores = jnp.where(rows_at() <= lane, raw_scores, 0.0)
        strict = jnp.where(rows_at() < lane, raw_scores, 0.0)
        scores = jnp.concatenate([scores, scores], axis=1)
        strict = jnp.concatenate([strict, strict], axis=1)
        left = -left_ref[r, :]
        gathered = jnp.zeros((ROWS, 2 * LANES), f32)
        for i in range(pairs):
            spread = mm(left, fixed[part, :, wide(i)])
            decay = jnp.exp2(jnp.minimum(spread, 0.0))
            stacked = diagonal(g_ref[r, slab(i)], low, high)
            grad = mm_nt(x_ref[r, slab(i)], stacked) * decay
            gathered = gathered + grad
            moved[:, wide(i)] = (grad * strict).astype(bf16)
            dx_ref[r, slab(i)] = mm((scores * decay).astype(bf16), stacked)
        late[...] = jnp.zeros_like(late)
        for i in range(pairs):
            sums = mm(ones, moved[:, wide(i)])
            late[2 * i : 2 * i + 1, :] = sums[0:1, :LANES]
            late[2 * i + 1 : 2 * i + 2, :] = sums[0:1, LANES:]
        pq_ref[r, :] = late[...].T - mm(moved[...], taken_ref[...])
        gathered = gathered[:, :LANES] + gathered[:, LANES:]
        gathered = jnp.where(rows_at() <= lane, gathered, 0.0).astype(bf16)
        db_ref[r, :] = mm(gathered, outputs)
        dc_ref[r, :] = mm_tn(gathered, inputs)


def inside_backward(x, act, gm, left, right, still, taken, inner, width):
    rows = act.shape[0]
    inputs_at = inner // width
    return pl.pallas_call(
        functools.partial(inside_back_kernel, inner // LANES),
        grid=(rows // (GROUP * ROWS),),
        in_specs=[
            by_rows(inner),
            pl.BlockSpec((GROUP * ROWS, width), lambda i: (i, inputs_at)),
            pl.BlockSpec((GROUP * ROWS, width), lambda i: (i, inputs_at + 1)),
            by_rows(inner),
            by_rows(LANES),
            by_rows(right.shape[1], GROUP * HALO),
            whole(still.shape),
            whole(taken.shape),
        ],
        out_specs=[by_rows(inner), by_rows(width), by_rows(width), by_rows(LANES)],
        out_shape=[
            jax.ShapeDtypeStruct((rows, inner), f32),
            jax.ShapeDtypeStruct((rows, width), f32),
            jax.ShapeDtypeStruct((rows, width), f32),
            jax.ShapeDtypeStruct((rows, LANES), f32),
        ],
        scratch_shapes=[
            pltpu.VMEM((GROUP,) + still.shape, bf16),
            pltpu.VMEM((ROWS, 2 * inner), bf16),
            pltpu.VMEM((LANES, ROWS), f32),
        ],
        compiler_params=params(),
        name="inside_backward",
        cost_estimate=cost(20),
    )(x, act, act, gm, left, right, still, taken)


def finish_kernel(
    heads,
    pairs,
    blocks,
    v_ref,
    x_ref,
    b_ref,
    c_ref,
    g_ref,
    dx_ref,
    db_ref,
    dc_ref,
    pq_ref,
    pac_ref,
    states_ref,
    step_ref,
    cum_ref,
    raw_ref,
    bias_ref,
    alog_ref,
    etot_ref,
    skip_ref,
    start_ref,
    ones_ref,
    fan_ref,
    gact_ref,
    graw_ref,
    gbias_ref,
    grate_ref,
    state,
    tails,
    early,
    first,
    second,
    third,
    spread,
    three,
):
    at = pl.program_id(0)
    step_at = blocks // GROUP - 1 - at
    inner = pairs * LANES
    width = state.shape[0]

    @pl.when(at == 0)
    def _():
        state[...] = start_ref[...]
        gbias_ref[...] = jnp.zeros_like(gbias_ref)
        grate_ref[...] = jnp.zeros_like(grate_ref)

    later = (rows_at() <= lanes_at()).astype(f32)
    earlier = (rows_at() > lanes_at()).astype(f32)
    rates = jnp.exp(alog_ref[...])
    for part, r in reversed(list(enumerate(parts_of_step()))):
        inputs, outputs = b_ref[r, :], c_ref[r, :]
        leaving = state[...]
        leaving_low = leaving.astype(bf16)
        entering = states_ref[part * width : (part + 1) * width, :]
        etot = etot_ref[pl.ds(step_at * GROUP + part, 1), :]
        held = jnp.sum(leaving * entering.astype(f32), axis=0, keepdims=True) * etot
        held = mm(jnp.broadcast_to(held, (8, inner)).astype(bf16), ones_ref[...])[0:1, :]
        spread[...] = mm(inputs, leaving_low)
        cum, step = cum_ref[r, :], step_ref[r, :]
        grow = jnp.exp(cum)
        tail = jnp.exp(cum[ROWS - 1 :, :] - cum)
        three[...] = mm(
            jnp.concatenate([halves(step, heads), halves(tail, heads), halves(grow, heads)], axis=0),
            fan_ref[...],
        )
        for i in range(pairs):
            s = slab(i)
            v = v_ref[r, s].astype(f32)
            g = g_ref[r, s].astype(f32)
            steps = three[:ROWS, s]
            x = x_ref[r, s].astype(f32)
            part_tail = three[ROWS : 2 * ROWS, s]
            more = spread[:, s] * part_tail
            dx = dx_ref[r, s] + more
            first[:, s] = (x * more).astype(bf16)
            direct = v * dx
            high = direct.astype(bf16)
            second[:, s] = high
            third[:, s] = (direct - high.astype(f32)).astype(bf16)
            gact_ref[r, s] = (steps * dx + skip_ref[:, s] * g).astype(bf16)
            tails[:, s] = (x * part_tail).astype(bf16)
            early[:, s] = (g * three[2 * ROWS :, s]).astype(bf16)
        gact_ref[r, inner : inner + width] = (db_ref[r, :] + mm_nt(tails[...], leaving_low)).astype(bf16)
        gact_ref[r, inner + width :] = (dc_ref[r, :] + mm_nt(early[...], entering)).astype(bf16)
        gdecay = (
            jnp.dot(later, pq_ref[r, :] + pac_ref[r, :], precision=highest, preferred_element_type=f32)
            + jnp.dot(
                earlier, mm(first[...], ones_ref[...]), precision=highest, preferred_element_type=f32
            )
            + held
        )
        gstep = mm(second[...], ones_ref[...]) + mm(third[...], ones_ref[...]) - rates * gdecay
        graw = gstep.astype(bf16).astype(f32) * sigmoid(raw_ref[r, :] + bias_ref[...])
        graw_ref[r, :] = graw.astype(bf16)
        gbias_ref[...] += jnp.sum(graw, axis=0, keepdims=True)
        grate_ref[...] += jnp.sum(step * gdecay, axis=0, keepdims=True)
        state[...] = etot * leaving + mm_tn(outputs, early[...])


def mixer_finish(
    act, x, gm, dx, db, dc, pq, pac, states, step, cum, raw, bias, a_log, etot, skip, start, ones, fan, heads, inner, width
):
    rows = act.shape[0]
    blocks = rows // ROWS
    inputs_at = inner // width
    channels = act.shape[1]

    def backwards(columns, height=GROUP * ROWS, column_at=0):
        return pl.BlockSpec((height, columns), lambda i: (blocks // GROUP - 1 - i, column_at))

    return pl.pallas_call(
        functools.partial(finish_kernel, heads, inner // LANES, blocks),
        grid=(blocks // GROUP,),
        in_specs=[
            backwards(inner),
            backwards(inner),
            backwards(width, column_at=inputs_at),
            backwards(width, column_at=inputs_at + 1),
            backwards(inner),
            backwards(inner),
            backwards(width),
            backwards(width),
            backwards(LANES),
            backwards(LANES),
            backwards(inner, GROUP * width),
            backwards(LANES),
            backwards(LANES),
            backwards(LANES),
            whole((1, LANES)),
            whole((1, LANES)),
            whole(etot.shape),
            whole((1, inner)),
            whole((width, inner)),
            whole((inner, LANES)),
            whole(fan.shape),
        ],
        out_specs=[backwards(channels), backwards(LANES), whole((1, LANES)), whole((1, LANES))],
        out_shape=[
            jax.ShapeDtypeStruct((rows, channels), bf16),
            jax.ShapeDtypeStruct((rows, LANES), bf16),
            jax.ShapeDtypeStruct((1, LANES), f32),
            jax.ShapeDtypeStruct((1, LANES), f32),
        ],
        scratch_shapes=[
            pltpu.VMEM((width, inner), f32),
            pltpu.VMEM((ROWS, inner), bf16),
            pltpu.VMEM((ROWS, inner), bf16),
            pltpu.VMEM((ROWS, inner), bf16),
            pltpu.VMEM((ROWS, inner), bf16),
            pltpu.VMEM((ROWS, inner), bf16),
            pltpu.VMEM((ROWS, inner), f32),
            pltpu.VMEM((3 * ROWS, inner), f32),
        ],
        compiler_params=params(),
        name="mixer_finish",
        cost_estimate=cost(16),
    )(act, x, act, act, gm, dx, db, dc, pq, pac, states, step, cum, raw, bias, a_log, etot, skip, start, ones, fan)


def conv_back_kernel(
    span, rows, blocks, cin_ref, gact_ref, graw_ref, taps_ref, bias_ref,
    gproj_ref, gtaps_ref, gbias_ref, top_ref, rest_ref, held, grads,
):
    part = 128
    cols = held.shape[1]
    at = pl.program_id(0)

    @pl.when(at == blocks)
    def _():
        gproj_ref[:, :LANES] = graw_ref[...]

    @pl.when(at < blocks)
    def _():
        held[...] = cin_ref[...].astype(f32)
        grads[rows:, :] = jnp.zeros((HALO, cols), f32)
        gbias = jnp.zeros((1, cols), f32)
        gtaps = [jnp.zeros((1, cols), f32)] * span
        for start in range(0, rows, part):
            total = jnp.broadcast_to(bias_ref[0:1, :], (part, cols))
            seen = []
            for k in range(span):
                first = HALO + start - (span - 1) + k
                seen.append(held[first : first + part, :])
                total = total + taps_ref[k : k + 1, :] * seen[k]
            sig = sigmoid(total)
            grad = gact_ref[start : start + part, :].astype(f32) * (sig * (1.0 + total * (1.0 - sig)))
            grads[start : start + part, :] = grad
            gbias = gbias + jnp.sum(grad, axis=0, keepdims=True)
            for k in range(span):
                gtaps[k] = gtaps[k] + jnp.sum(seen[k] * grad, axis=0, keepdims=True)
        gbias_ref[...] = gbias
        for k in range(span):
            gtaps_ref[k : k + 1, :] = gtaps[k]
        top_ref[...] = grads[0:8, :]
        for start in range(0, rows, part):
            total = jnp.zeros((part, cols), f32)
            for k in range(span):
                first = start + span - 1 - k
                total = total + taps_ref[k : k + 1, :] * grads[first : first + part, :]
            gproj_ref[start : start + part, :] = total.astype(bf16)
            if start + part == rows:
                rest_ref[...] = total[part - 8 :, :]


def conv_backward(cin, gact, graw, taps, bias):
    rows, channels = gact.shape
    cols = 2 * LANES
    blocks = channels // cols
    span = taps.shape[0]

    def columns(height):
        return pl.BlockSpec((height, cols), lambda i: (0, jnp.minimum(i, blocks - 1)))

    return pl.pallas_call(
        functools.partial(conv_back_kernel, span, rows, blocks),
        grid=(blocks + 1,),
        in_specs=[columns(rows + HALO), columns(rows), whole((rows, LANES)), columns(span), columns(1)],
        out_specs=[
            pl.BlockSpec((rows, cols), lambda i: (0, i)),
            columns(span),
            columns(1),
            columns(8),
            columns(8),
        ],
        out_shape=[
            jax.ShapeDtypeStruct((rows, channels + LANES), bf16),
            jax.ShapeDtypeStruct((span, channels), f32),
            jax.ShapeDtypeStruct((1, channels), f32),
            jax.ShapeDtypeStruct((8, channels), f32),
            jax.ShapeDtypeStruct((8, channels), f32),
        ],
        scratch_shapes=[pltpu.VMEM((rows + HALO, cols), f32), pltpu.VMEM((rows + HALO, cols), f32)],
        compiler_params=params(),
        name="conv_backward",
        cost_estimate=cost(18),
    )(cin, gact, graw, taps, bias)


def local(
    tokens,
    norm_gain,
    in_weight,
    conv_weight,
    conv_bias,
    dt_bias,
    a_log,
    skip_gain,
    gate_gain,
    out_weight,
    cotangent,
):
    tokens, incoming = tokens[0], cotangent[0]
    rows, model = tokens.shape
    heads = a_log.shape[0]
    span, channels = conv_weight.shape
    inner = gate_gain.shape[0]
    width = (channels - inner) // 2
    head_width = inner // heads
    blocks = rows // ROWS
    pad = LANES - heads

    order = gathered_order()
    conv_flight = Flight(gather(jnp.pad(in_weight[:, inner:], ((0, 0), (0, pad)))))
    before = shifted(tokens[rows - HALO :], "seq", 1)

    def first_norm(block):
        block = block.astype(f32)
        scale = lax.rsqrt(jnp.mean(block * block, axis=1, keepdims=True) + epsilon)
        return (block * scale * norm_gain).astype(bf16), scale

    own, own_scale = first_norm(tokens)
    gate_part, out_weight, own = conv_flight.step(in_weight[:, :inner], out_weight, own)
    w_gate = lax.all_gather(gate_part, "fsdp", axis=0, tiled=True)
    w_out = lax.all_gather(out_weight, "fsdp", axis=0, tiled=True)
    conv_near, conv_far = conv_flight.finish()
    act, cin, raw, conv_near, conv_far = conv_forward(
        jnp.stack([jnp.int32(at) for at in order]), first_norm(before)[0], own, conv_near, conv_far,
        conv_weight, conv_bias[None],
    )
    bias_row = jnp.pad(dt_bias, (0, pad))[None]
    alog_row = jnp.pad(a_log, (0, pad))[None]
    step, cum, left, right = steps_forward(raw, bias_row, alog_row, heads)

    totals = cum.reshape(blocks, ROWS, LANES)[:, -1, :heads]
    befores = jnp.cumsum(totals, axis=0) - totals
    etot = jnp.repeat(jnp.exp(totals), head_width, axis=1)
    ebef = jnp.repeat(jnp.exp(befores), head_width, axis=1)
    skip = jnp.repeat(skip_gain, head_width)[None]
    def fanned(count, each):
        row, column = np.arange(LANES)[:, None], np.arange(count)[None]
        return ((row < 3 * heads) & (row % heads == column // each)).astype(ml_dtypes.bfloat16)

    def gathering(count, each):
        return (np.arange(count)[:, None] // each == np.arange(LANES)[None]).astype(ml_dtypes.bfloat16)

    fan = fanned(inner, head_width)
    still = fanned(heads * LANES, LANES)
    ones = gathering(inner, head_width)
    taken = gathering(heads * LANES, LANES)
    whole_decay = jnp.repeat(jnp.exp(jnp.sum(totals, axis=0)), head_width)[None]

    x, leaves = piece_state(act, step, cum, etot, fan, heads, inner, width)
    ahead = Flight(handed_on(leaves, whole_decay, 1))
    y = inside_forward(x, act, left, right, still, inner, width)
    y = ahead.step(y)
    z = mm(own, w_gate)
    z = ahead.step(z)
    gn = mm_nt(incoming, w_out)
    gn = ahead.step(gn)
    start = ahead.finish()
    out_in, gm, gz, states, pac, back, ggain, gskip = gate_both(
        y, act, z, gn, step, cum, etot, ebef, skip, gate_gain[None], start, ones, fan, heads, inner, width
    )

    behind = Flight(handed_on(back, whole_decay, -1))
    part_out = mm_tn(out_in, incoming).astype(bf16)
    part_gate = mm_tn(own, gz).astype(bf16)
    pulled_gate = mm_nt(gz, w_gate)
    part_out, part_gate, pulled_gate = behind.step(part_out, part_gate, pulled_gate)
    slices = inner // model
    sums = Flight(
        sum_scatter([part_out] + [part_gate[:, i * model : (i + 1) * model] for i in range(slices)])
    )
    mixed = (tokens.astype(f32) + mm(out_in, w_out)).astype(bf16)
    mixed = behind.step(mixed)
    mixed, gm = sums.step(mixed, gm)
    dx, db, dc, pq = inside_backward(x, act, gm, left, right, still, taken, inner, width)
    dx = behind.step(dx)
    dx = sums.step(dx)
    back_start = behind.finish()
    gact, graw, gdt, grate = mixer_finish(
        act, x, gm, dx, db, dc, pq, pac, states, step, cum, raw, bias_row, alog_row, etot, skip,
        back_start, ones, fan, heads, inner, width,
    )
    gact = sums.step(gact)
    cin = sums.step(cin)
    gproj, gtaps, gcbias, top, rest = conv_backward(cin, gact, graw, conv_weight, conv_bias[None])
    nexts = shifted(top, "seq", -1)
    gproj = sums.step(gproj)
    owed = jnp.zeros((8, channels), f32)
    for k in range(span - 1):
        reach = span - 1 - k
        owed = owed + jnp.pad(conv_weight[k] * nexts[:reach], ((8 - reach, 0), (0, 0)))
    gproj = lax.dynamic_update_slice(gproj, (rest + owed).astype(bf16), (rows - 8, 0))

    part_conv = mm_tn(own, gproj).astype(bf16)
    conv_sums = Flight(sum_scatter([part_conv]))
    pulled_near = mm_nt(gproj, conv_near)
    pulled_near = conv_sums.step(pulled_near)
    pulled_conv = jnp.concatenate([pulled_near, mm_nt(gproj, conv_far)], axis=1)
    places = [sum(jnp.where(at == block, i, 0) for i, at in enumerate(order)) for block in range(len(order))]
    grad_normed = pulled_gate + in_order(pulled_conv, places)
    unit = tokens.astype(f32) * own_scale
    pulled = grad_normed * norm_gain
    mean_pull = jnp.mean(pulled * unit, axis=1, keepdims=True)
    grad_tokens = incoming.astype(f32) + own_scale * (pulled - unit * mean_pull)
    grad_norm_gain = jnp.sum(grad_normed * unit, axis=0)
    small = [
        grad_norm_gain,
        gtaps.reshape(-1),
        gcbias[0],
        gdt[0, :heads],
        grate[0, :heads] * -jnp.exp(a_log),
        jnp.sum(gskip.reshape(heads, head_width), axis=1),
        ggain[0],
    ]
    small_sums = Flight(sum_all(jnp.concatenate(small)))
    small_sums.step()
    small_sums.flying = (conv_sums.step(*small_sums.flying),)
    small_sums.step()
    conv_sums.step()
    summed_parts = sums.finish()
    grad_out_weight = summed_parts[0]
    (grad_conv_part,) = conv_sums.finish()
    summed = small_sums.finish()

    grad_in_weight = jnp.concatenate(
        summed_parts[1:] + [grad_conv_part[:, : channels + heads]], axis=1
    )
    sizes = [part.shape[0] for part in small]
    split, at = [], 0
    for size in sizes:
        split.append(summed[at : at + size])
        at += size
    return (
        mixed[None],
        grad_tokens[None],
        grad_in_weight,
        grad_out_weight,
        split[0],
        split[1].reshape(span, channels),
        *split[2:],
    )


def solution(mesh):
    tokens = P("fsdp", "seq", None)
    sharded = P("fsdp", None)
    spread = P(("seq", "fsdp"), None)
    return jax.shard_map(
        local,
        mesh=mesh,
        in_specs=(tokens, P(), sharded, P(), P(), P(), P(), P(), P(), sharded, tokens),
        out_specs=(tokens, tokens, spread, spread, P(), P(), P(), P(), P(), P(), P()),
        check_vma=False,
    )
```

```python
import functools

import jax
import jax.numpy as jnp
import ml_dtypes
import numpy as np
from jax import lax
from jax.experimental import pallas as pl
from jax.experimental.pallas import tpu as pltpu
from jax.sharding import PartitionSpec as P

ROWS = 128
GROUP = 2
LANES = 128
HALO = 16
VMEM = 48 * 1024 * 1024
LOG2E = 1.4426950408889634
epsilon = 1e-05
bf16 = jnp.bfloat16
f32 = jnp.float32
highest = lax.Precision.HIGHEST


def shifted(block, axis, distance):
    size = lax.axis_size(axis)
    route = [(i - distance, i) for i in range(size) if 0 <= i - distance < size]
    return lax.ppermute(block, axis, route)


def exchanged(block, axis, bit):
    return lax.ppermute(block, axis, [(i, i ^ bit) for i in range(lax.axis_size(axis))])


def pick(block, at, axis):
    return lax.dynamic_index_in_dim(block, at, axis, keepdims=False)


class Flight:
    def __init__(self, steps):
        self.steps, self.value, self.flying = steps, None, None
        self.advance(None)

    def advance(self, arrived):
        try:
            self.flying = self.steps.send(arrived)
        except StopIteration as end:
            self.flying, self.value = None, end.value

    def step(self, *others):
        if self.flying is not None:
            count = len(self.flying)
            tied = lax.optimization_barrier((*self.flying, *others))
            others = tied[count:]
            self.advance(tuple(tied[:count]))
        return others[0] if len(others) == 1 else others

    def finish(self):
        while self.flying is not None:
            self.advance(self.flying)
        return self.value


def gather(weight):
    rows = weight.shape[0]
    if lax.axis_size("fsdp") != 8 or rows % 32:
        full = lax.all_gather(weight, "fsdp", axis=0, tiled=True)
        return [full[: full.shape[0] // 2]], [full[full.shape[0] // 2 :]]
    first, last = weight[: rows // 2], weight[rows // 2 :]

    def crossed(block):
        return exchanged(block, "fsdp", 1)

    first_y, last_x = exchanged(first, "fsdp", 4), exchanged(last, "fsdp", 2)
    first_x, last_y = exchanged(first, "fsdp", 2), exchanged(last, "fsdp", 4)
    far = [crossed(weight)]
    first_y, last_x, first_x, last_y = yield first_y, last_x, first_x, last_y
    first_xy, last_xy = exchanged(first_y, "fsdp", 2), exchanged(last_x, "fsdp", 4)
    far += [crossed(block) for block in (first_x, last_x, first_y, last_y)]
    first_xy, last_xy, *far = yield first_xy, last_xy, *far
    far += [crossed(first_xy), crossed(last_xy)]
    far = yield tuple(far)
    return [weight, first_x, last_x, first_y, last_y, first_xy, last_xy], list(far)


def gathered_order():
    group = lax.axis_size("fsdp")
    if group != 8:
        return list(range(group))
    me = lax.axis_index("fsdp")
    return [me ^ distance for distance in (0, 2, 4, 6, 1, 3, 5, 7)]


def in_order(block, order):
    size = block.shape[1] // len(order)
    return jnp.concatenate(
        [lax.dynamic_slice_in_dim(block, at * size, size, axis=1) for at in order], axis=1
    )


def handed_on(state, decay, distance):
    entering = jnp.zeros(state.shape, f32)
    state = state.astype(f32)
    for _ in range(lax.axis_size("seq") - 1):
        leaving = (state + decay * entering).astype(bf16)
        (arrived,) = yield (shifted(leaving, "seq", distance),)
        entering = arrived.astype(f32)
    return entering


def sum_all(vector):
    for axis in ("fsdp", "seq"):
        size = lax.axis_size(axis)
        if size & (size - 1):
            vector = lax.psum(vector, axis)
            continue
        for bit in range(size.bit_length() - 1):
            (other,) = yield (exchanged(vector, axis, 1 << bit),)
            vector = vector + other
    return vector


def sum_scatter(parts):
    pieces, group = lax.axis_size("seq"), lax.axis_size("fsdp")
    bits = group.bit_length() - 1
    columns = parts[0].shape[1]
    rows = [part.shape[0] // (pieces * group) for part in parts]
    total = sum(rows)
    if group != 1 << bits or bits < 1 or total % 2:
        return [
            lax.psum_scatter(part.astype(f32), ("seq", "fsdp"), scatter_dimension=0, tiled=True)
            for part in parts
        ]
    me = lax.axis_index("fsdp")
    parts = [part.reshape(pieces, group // 2, 2, -1, columns) for part in parts]
    mine = me & 1
    (got,) = yield (
        exchanged(jnp.concatenate([pick(part, 1 - mine, 2) for part in parts], axis=2), "fsdp", 1),
    )
    block = jnp.concatenate([pick(part, mine, 2) for part in parts], axis=2) + got
    ways = [list(range(bits - 1, 0, -1)), list(range(bits - 1, 0, -1))]
    halves = [
        part.reshape((pieces,) + (2,) * (bits - 1) + part.shape[2:])
        for part in (block[:, :, : total // 2], block[:, :, total // 2 :])
    ]
    for _ in range(bits - 1):
        taken = [ways[0][-1], ways[1][0]]
        places = [1 + ways[way].index(taken[way]) for way in (0, 1)]
        sides = [(me >> taken[way]) & 1 for way in (0, 1)]
        got = yield tuple(
            exchanged(pick(halves[way], 1 - sides[way], places[way]), "fsdp", 1 << taken[way])
            for way in (0, 1)
        )
        halves = [pick(halves[way], sides[way], places[way]) + got[way] for way in (0, 1)]
        for way in (0, 1):
            ways[way].remove(taken[way])
    part = jnp.concatenate(halves, axis=1)
    (part,) = yield (part,)
    place = lax.axis_index("seq")
    got = yield tuple(
        lax.ppermute(
            pick(part, (place + ahead) % pieces, 0), "seq", [(i, (i + ahead) % pieces) for i in range(pieces)]
        )
        for ahead in range(1, pieces)
    )
    own = sum((block.astype(f32) for block in got), pick(part, place, 0).astype(f32))
    results, at = [], 0
    for size in rows:
        results.append(own[at : at + size])
        at += size
    return results


def mm(a, b):
    return lax.dot_general(a, b, (((1,), (0,)), ((), ())), preferred_element_type=f32)


def mm_nt(a, b):
    return lax.dot_general(a, b, (((1,), (1,)), ((), ())), preferred_element_type=f32)


def mm_tn(a, b):
    return lax.dot_general(a, b, (((0,), (0,)), ((), ())), preferred_element_type=f32)


def sigmoid(v):
    return 0.5 + 0.5 * jnp.tanh(0.5 * v)


def rows_at():
    return lax.broadcasted_iota(jnp.int32, (ROWS, LANES), 0)


def lanes_at():
    return lax.broadcasted_iota(jnp.int32, (ROWS, LANES), 1)


def slab(i):
    return slice(i * LANES, (i + 1) * LANES)


def wide(i):
    return slice(i * 2 * LANES, (i + 1) * 2 * LANES)


def halves(columns, heads):
    lane = lanes_at()
    high = columns.astype(bf16).astype(f32)
    rest = pltpu.roll(columns - high, heads, 1)
    return jnp.where(lane < heads, high, jnp.where(lane < 2 * heads, rest, 0.0)).astype(bf16)


def low_lanes():
    return (lanes_at() < LANES // 2).astype(f32).astype(bf16), (lanes_at() >= LANES // 2).astype(f32).astype(bf16)


def diagonal(block, low, high):
    return jnp.concatenate([block * low, block * high], axis=0)


def parts_of_step():
    return [slice(part * ROWS, (part + 1) * ROWS) for part in range(GROUP)]


def params(**more):
    return pltpu.CompilerParams(vmem_limit_bytes=VMEM, **more)


def cost(microseconds):
    return pl.CostEstimate(flops=int(microseconds * 1e9), bytes_accessed=4 * 1024 * 1024, transcendentals=0)


def whole(shape):
    return pl.BlockSpec(shape, lambda i: (0,) * len(shape))


def by_rows(width, rows=GROUP * ROWS):
    return pl.BlockSpec((rows, width), lambda i: (i, 0))


def conv_kernel(span, rows, pieces, order_ref, before_ref, own_ref, *refs):
    near_refs, far_refs = refs[:pieces], refs[pieces : 2 * pieces]
    taps_ref, bias_ref, act_ref, cin_ref, raw_ref, near_ref, far_ref, held, normed_ref = refs[2 * pieces :]
    at = pl.program_id(0)
    last = pl.num_programs(0) - 1
    near = jnp.concatenate([ref[...] for ref in near_refs], axis=0)
    far = jnp.concatenate([ref[...] for ref in far_refs], axis=0)
    near_ref[...] = near
    far_ref[...] = far
    half = near.shape[0]
    size = own_ref.shape[1] // order_ref.shape[0]

    @pl.when(at == 0)
    def _():
        for i in range(order_ref.shape[0]):
            source = pl.ds(pl.multiple_of(order_ref[i] * size, size), size)
            normed_ref[:HALO, i * size : (i + 1) * size] = before_ref[:, source]
            normed_ref[HALO:, i * size : (i + 1) * size] = own_ref[:, source]

    def projected(start, size):
        block = normed_ref[start : start + size, :]
        return mm(block[:, :half], near) + mm(block[:, half:], far)

    part = 256

    @pl.when(at == last)
    def _():
        for start in range(0, rows, part):
            raw_ref[start : start + part, :] = projected(HALO + start, part)[:, :LANES]

    @pl.when(at < last)
    def _():
        for start, size in [(0, HALO)] + [(HALO + at, part) for at in range(0, rows, part)]:
            block = projected(start, size).astype(bf16)
            cin_ref[start : start + size, :] = block
            held[start : start + size, :] = block.astype(f32)
        for start in range(0, rows, part):
            total = jnp.broadcast_to(bias_ref[0:1, :], (part, bias_ref.shape[1]))
            for k in range(span):
                first = HALO + start - (span - 1) + k
                total = total + taps_ref[k : k + 1, :] * held[first : first + part, :]
            act_ref[start : start + part, :] = (total * sigmoid(total)).astype(bf16)


def conv_forward(order, before, own, near, far, taps, bias):
    rows, width = own.shape
    channels = taps.shape[1]
    total = near[0].shape[1]
    cols = 2 * LANES
    blocks = channels // cols

    def columns(height, upto=blocks):
        return pl.BlockSpec((height, cols), lambda i: (0, jnp.minimum(i, upto)))

    return pl.pallas_call(
        functools.partial(conv_kernel, taps.shape[0], rows, len(near)),
        grid=(blocks + 1,),
        in_specs=[pl.BlockSpec(memory_space=pltpu.SMEM), whole((HALO, width)), whole((rows, width))]
        + [columns(piece.shape[0]) for piece in near + far]
        + [columns(taps.shape[0], blocks - 1), columns(1, blocks - 1)],
        out_specs=[
            columns(rows, blocks - 1),
            columns(rows + HALO, blocks - 1),
            whole((rows, LANES)),
            columns(width // 2),
            columns(width // 2),
        ],
        out_shape=[
            jax.ShapeDtypeStruct((rows, channels), bf16),
            jax.ShapeDtypeStruct((rows + HALO, channels), bf16),
            jax.ShapeDtypeStruct((rows, LANES), f32),
            jax.ShapeDtypeStruct((width // 2, total), bf16),
            jax.ShapeDtypeStruct((width // 2, total), bf16),
        ],
        scratch_shapes=[pltpu.VMEM((rows + HALO, cols), f32), pltpu.VMEM((rows + HALO, width), bf16)],
        compiler_params=params(),
        name="conv_forward",
        cost_estimate=cost(16),
    )(order, before, own, *near, *far, taps, bias)


def steps_kernel(blocks, heads, raw_ref, bias_ref, alog_ref, step_ref, cum_ref, left_ref, right_ref, rows3):
    lane = lanes_at()
    lower = (rows_at() >= lane).astype(f32)
    rates = -jnp.exp(alog_ref[...])
    rows3[...] = jnp.zeros_like(rows3)
    for b in range(blocks):
        rows = slice(b * ROWS, (b + 1) * ROWS)
        soft = raw_ref[rows, :] + bias_ref[...]
        soft = jnp.maximum(soft, 0.0) + jnp.log1p(jnp.exp(-jnp.abs(soft)))
        step = soft.astype(bf16).astype(f32)
        step_ref[rows, :] = step
        cum = jnp.dot(lower, step * rates, precision=highest, preferred_element_type=f32)
        cum_ref[rows, :] = cum
        cum = cum * LOG2E
        parts, rest = [], cum
        for _ in range(3):
            part = rest.astype(bf16).astype(f32)
            parts.append(part)
            rest = rest - part
        left = jnp.where(lane < 3 * heads + 3, 1.0, 0.0)
        for k in (2, 1, 0):
            left = jnp.where(lane < (k + 1) * heads, pltpu.roll(parts[k], k * heads, 1), left)
        left_ref[rows, :] = left.astype(bf16)
        for k in range(3):
            flipped = -parts[k].T
            for h in range(heads):
                rows3[k : k + 1, slab(h)] = flipped[h : h + 1, :]
        right_ref[b * HALO : (b + 1) * HALO, :] = rows3[...].astype(bf16)


def steps_forward(raw, bias, a_log, heads):
    rows = raw.shape[0]
    blocks = rows // ROWS
    shape = jax.ShapeDtypeStruct((rows, LANES), f32)
    return pl.pallas_call(
        functools.partial(steps_kernel, blocks, heads),
        out_shape=[
            shape,
            shape,
            jax.ShapeDtypeStruct((rows, LANES), bf16),
            jax.ShapeDtypeStruct((blocks * HALO, heads * LANES), bf16),
        ],
        scratch_shapes=[pltpu.VMEM((HALO, heads * LANES), f32)],
        compiler_params=params(),
        name="steps_forward",
        cost_estimate=cost(6),
    )(raw, bias, a_log)


def state_kernel(heads, v_ref, b_ref, step_ref, cum_ref, etot_ref, fan_ref, x_ref, f_ref, state, tails, both):
    at = pl.program_id(0)

    @pl.when(at == 0)
    def _():
        state[...] = jnp.zeros_like(state)

    for part, r in enumerate(parts_of_step()):
        cum, step = cum_ref[r, :], step_ref[r, :]
        tail = jnp.exp(cum[ROWS - 1 :, :] - cum) * step
        both[...] = mm(jnp.concatenate([halves(step, heads), halves(tail, heads)], axis=0), fan_ref[...])
        v = v_ref[r, :].astype(f32)
        x_ref[r, :] = (v * both[:ROWS, :]).astype(bf16)
        tails[...] = (v * both[ROWS:, :]).astype(bf16)
        etot = etot_ref[pl.ds(at * GROUP + part, 1), :]
        state[...] = etot * state[...] + mm_tn(b_ref[r, :], tails[...])

    @pl.when(at == pl.num_programs(0) - 1)
    def _():
        f_ref[...] = state[...].astype(bf16)


def piece_state(act, step, cum, etot, fan, heads, inner, width):
    rows = act.shape[0]
    inputs_at = inner // width
    return pl.pallas_call(
        functools.partial(state_kernel, heads),
        grid=(rows // (GROUP * ROWS),),
        in_specs=[
            by_rows(inner),
            pl.BlockSpec((GROUP * ROWS, width), lambda i: (i, inputs_at)),
            by_rows(LANES),
            by_rows(LANES),
            whole(etot.shape),
            whole(fan.shape),
        ],
        out_specs=[by_rows(inner), whole((width, inner))],
        out_shape=[
            jax.ShapeDtypeStruct((rows, inner), bf16),
            jax.ShapeDtypeStruct((width, inner), bf16),
        ],
        scratch_shapes=[
            pltpu.VMEM((width, inner), f32),
            pltpu.VMEM((ROWS, inner), bf16),
            pltpu.VMEM((2 * ROWS, inner), f32),
        ],
        compiler_params=params(),
        name="piece_state",
        cost_estimate=cost(6),
    )(act, act, step, cum, etot, fan)


def inside_kernel(pairs, x_ref, b_ref, c_ref, left_ref, right_ref, still_ref, y_ref, right):
    fixed = left_rows(right, still_ref, right_ref)
    low, high = low_lanes()
    for part, r in enumerate(parts_of_step()):
        scores = jnp.where(rows_at() >= lanes_at(), mm_nt(c_ref[r, :], b_ref[r, :]), 0.0)
        scores = jnp.concatenate([scores, scores], axis=1)
        left = left_ref[r, :]
        for i in range(pairs):
            spread = mm(left, fixed[part, :, wide(i)])
            weights = (scores * jnp.exp2(jnp.minimum(spread, 0.0))).astype(bf16)
            y_ref[r, slab(i)] = mm(weights, diagonal(x_ref[r, slab(i)], low, high))


def left_rows(right, still_ref, right_ref):
    @pl.when(pl.program_id(0) == 0)
    def _():
        for part in range(GROUP):
            right[part, :, :] = still_ref[...]

    own = still_ref.shape[0] - 2 * HALO
    for part in range(GROUP):
        right[part, own : own + HALO, :] = right_ref[part * HALO : (part + 1) * HALO, :]
    return right


def inside_forward(x, act, left, right, still, inner, width):
    rows = act.shape[0]
    inputs_at = inner // width
    return pl.pallas_call(
        functools.partial(inside_kernel, inner // LANES),
        grid=(rows // (GROUP * ROWS),),
        in_specs=[
            by_rows(inner),
            pl.BlockSpec((GROUP * ROWS, width), lambda i: (i, inputs_at)),
            pl.BlockSpec((GROUP * ROWS, width), lambda i: (i, inputs_at + 1)),
            by_rows(LANES),
            by_rows(right.shape[1], GROUP * HALO),
            whole(still.shape),
        ],
        out_specs=by_rows(inner),
        out_shape=jax.ShapeDtypeStruct((rows, inner), f32),
        scratch_shapes=[pltpu.VMEM((GROUP,) + still.shape, bf16)],
        compiler_params=params(),
        name="inside_forward",
        cost_estimate=cost(10),
    )(x, act, act, left, right, still)


def gate_kernel(
    heads,
    pairs,
    y_ref,
    v_ref,
    b_ref,
    c_ref,
    z_ref,
    gn_ref,
    step_ref,
    cum_ref,
    etot_ref,
    ebef_ref,
    skip_ref,
    gain_ref,
    start_ref,
    ones_ref,
    fan_ref,
    out_ref,
    gm_ref,
    gz_ref,
    states_ref,
    pac_ref,
    back_ref,
    ggain_ref,
    gskip_ref,
    state,
    back,
    across,
    mixer,
    gated,
    early,
    tails,
    products,
    both,
):
    at = pl.program_id(0)
    width = pairs * LANES

    @pl.when(at == 0)
    def _():
        state[...] = start_ref[...]
        back[...] = jnp.zeros_like(back)
        ggain_ref[...] = jnp.zeros_like(ggain_ref)
        gskip_ref[...] = jnp.zeros_like(gskip_ref)

    for part, r in enumerate(parts_of_step()):
        outputs = c_ref[r, :]
        entering = state[...].astype(bf16)
        states_ref[part * state.shape[0] : (part + 1) * state.shape[0], :] = entering
        across[...] = mm(outputs, entering)
        cum = cum_ref[r, :]
        grow = jnp.exp(cum)
        tail = jnp.exp(cum[ROWS - 1 :, :] - cum) * step_ref[r, :]
        both[...] = mm(jnp.concatenate([halves(grow, heads), halves(tail, heads)], axis=0), fan_ref[...])
        squares = jnp.zeros((ROWS, LANES), f32)
        meets = jnp.zeros((ROWS, LANES), f32)
        for i in range(pairs):
            s = slab(i)
            v = v_ref[r, s].astype(f32)
            ya = across[:, s] * both[:ROWS, s]
            across[:, s] = ya
            m = (y_ref[r, s] + ya + skip_ref[:, s] * v).astype(bf16)
            mixer[:, s] = m
            z = z_ref[r, s]
            product = m.astype(f32) * (z * sigmoid(z))
            gated[:, s] = product
            squares = squares + product * product
            meets = meets + gn_ref[r, s] * gain_ref[:, s] * product
            tails[:, s] = (v * both[ROWS:, s]).astype(bf16)
        scale = lax.rsqrt(jnp.sum(squares, axis=1, keepdims=True) / width + epsilon)
        pull = scale * scale * scale * (jnp.sum(meets, axis=1, keepdims=True) / width)
        for i in range(pairs):
            s = slab(i)
            v = v_ref[r, s].astype(f32)
            product = gated[:, s]
            unit = product * scale
            gain = gain_ref[:, s]
            gn = gn_ref[r, s]
            out_ref[r, s] = (unit * gain).astype(bf16)
            ggain_ref[:, s] += jnp.sum(gn * unit, axis=0, keepdims=True)
            grad = gn * gain * scale - product * pull
            z = z_ref[r, s]
            sig = sigmoid(z)
            swish = z * sig
            gm = (grad * swish).astype(bf16)
            gm_ref[r, s] = gm
            slope = sig + swish * (1.0 - sig)
            gz_ref[r, s] = (grad * mixer[:, s].astype(f32) * slope).astype(bf16)
            g = gm.astype(f32)
            gskip_ref[:, s] += jnp.sum(g * v, axis=0, keepdims=True)
            products[:, s] = (g * across[:, s]).astype(bf16)
            early[:, s] = (g * both[:ROWS, s]).astype(bf16)
        pac_ref[r, :] = mm(products[...], ones_ref[...])
        block = at * GROUP + part
        back[...] += ebef_ref[pl.ds(block, 1), :] * mm_tn(outputs, early[...])
        state[...] = etot_ref[pl.ds(block, 1), :] * state[...] + mm_tn(b_ref[r, :], tails[...])

    @pl.when(at == pl.num_programs(0) - 1)
    def _():
        back_ref[...] = back[...].astype(bf16)


def gate_both(y, act, z, gn, step, cum, etot, ebef, skip, gain, start, ones, fan, heads, inner, width):
    rows = act.shape[0]
    inputs_at = inner // width
    blocks = rows // ROWS
    return pl.pallas_call(
        functools.partial(gate_kernel, heads, inner // LANES),
        grid=(blocks // GROUP,),
        in_specs=[
            by_rows(inner),
            by_rows(inner),
            pl.BlockSpec((GROUP * ROWS, width), lambda i: (i, inputs_at)),
            pl.BlockSpec((GROUP * ROWS, width), lambda i: (i, inputs_at + 1)),
            by_rows(inner),
            by_rows(inner),
            by_rows(LANES),
            by_rows(LANES),
            whole(etot.shape),
            whole(ebef.shape),
            whole((1, inner)),
            whole((1, inner)),
            whole((width, inner)),
            whole((inner, LANES)),
            whole(fan.shape),
        ],
        out_specs=[
            by_rows(inner),
            by_rows(inner),
            by_rows(inner),
            by_rows(inner, GROUP * width),
            by_rows(LANES),
            whole((width, inner)),
            whole((1, inner)),
            whole((1, inner)),
        ],
        out_shape=[
            jax.ShapeDtypeStruct((rows, inner), bf16),
            jax.ShapeDtypeStruct((rows, inner), bf16),
            jax.ShapeDtypeStruct((rows, inner), bf16),
            jax.ShapeDtypeStruct((blocks * width, inner), bf16),
            jax.ShapeDtypeStruct((rows, LANES), f32),
            jax.ShapeDtypeStruct((width, inner), bf16),
            jax.ShapeDtypeStruct((1, inner), f32),
            jax.ShapeDtypeStruct((1, inner), f32),
        ],
        scratch_shapes=[
            pltpu.VMEM((width, inner), f32),
            pltpu.VMEM((width, inner), f32),
            pltpu.VMEM((ROWS, inner), f32),
            pltpu.VMEM((ROWS, inner), bf16),
            pltpu.VMEM((ROWS, inner), f32),
            pltpu.VMEM((ROWS, inner), bf16),
            pltpu.VMEM((ROWS, inner), bf16),
            pltpu.VMEM((ROWS, inner), bf16),
            pltpu.VMEM((2 * ROWS, inner), f32),
        ],
        compiler_params=params(),
        name="gate_both",
        cost_estimate=cost(18),
    )(y, act, act, act, z, gn, step, cum, etot, ebef, skip, gain, start, ones, fan)


def inside_back_kernel(
    pairs, x_ref, b_ref, c_ref, g_ref, left_ref, right_ref, still_ref, taken_ref,
    dx_ref, db_ref, dc_ref, pq_ref, right, moved, late,
):
    fixed = left_rows(right, still_ref, right_ref)
    lane = lanes_at()
    low, high = low_lanes()
    ones = jnp.ones((16, ROWS), bf16)
    for part, r in enumerate(parts_of_step()):
        inputs, outputs = b_ref[r, :], c_ref[r, :]
        raw_scores = mm_nt(inputs, outputs)
        scores = jnp.where(rows_at() <= lane, raw_scores, 0.0)
        strict = jnp.where(rows_at() < lane, raw_scores, 0.0)
        scores = jnp.concatenate([scores, scores], axis=1)
        strict = jnp.concatenate([strict, strict], axis=1)
        left = -left_ref[r, :]
        gathered = jnp.zeros((ROWS, 2 * LANES), f32)
        for i in range(pairs):
            spread = mm(left, fixed[part, :, wide(i)])
            decay = jnp.exp2(jnp.minimum(spread, 0.0))
            stacked = diagonal(g_ref[r, slab(i)], low, high)
            grad = mm_nt(x_ref[r, slab(i)], stacked) * decay
            gathered = gathered + grad
            moved[:, wide(i)] = (grad * strict).astype(bf16)
            dx_ref[r, slab(i)] = mm((scores * decay).astype(bf16), stacked)
        late[...] = jnp.zeros_like(late)
        for i in range(pairs):
            sums = mm(ones, moved[:, wide(i)])
            late[2 * i : 2 * i + 1, :] = sums[0:1, :LANES]
            late[2 * i + 1 : 2 * i + 2, :] = sums[0:1, LANES:]
        pq_ref[r, :] = late[...].T - mm(moved[...], taken_ref[...])
        gathered = gathered[:, :LANES] + gathered[:, LANES:]
        gathered = jnp.where(rows_at() <= lane, gathered, 0.0).astype(bf16)
        db_ref[r, :] = mm(gathered, outputs)
        dc_ref[r, :] = mm_tn(gathered, inputs)


def inside_backward(x, act, gm, left, right, still, taken, inner, width):
    rows = act.shape[0]
    inputs_at = inner // width
    return pl.pallas_call(
        functools.partial(inside_back_kernel, inner // LANES),
        grid=(rows // (GROUP * ROWS),),
        in_specs=[
            by_rows(inner),
            pl.BlockSpec((GROUP * ROWS, width), lambda i: (i, inputs_at)),
            pl.BlockSpec((GROUP * ROWS, width), lambda i: (i, inputs_at + 1)),
            by_rows(inner),
            by_rows(LANES),
            by_rows(right.shape[1], GROUP * HALO),
            whole(still.shape),
            whole(taken.shape),
        ],
        out_specs=[by_rows(inner), by_rows(width), by_rows(width), by_rows(LANES)],
        out_shape=[
            jax.ShapeDtypeStruct((rows, inner), f32),
            jax.ShapeDtypeStruct((rows, width), f32),
            jax.ShapeDtypeStruct((rows, width), f32),
            jax.ShapeDtypeStruct((rows, LANES), f32),
        ],
        scratch_shapes=[
            pltpu.VMEM((GROUP,) + still.shape, bf16),
            pltpu.VMEM((ROWS, 2 * inner), bf16),
            pltpu.VMEM((LANES, ROWS), f32),
        ],
        compiler_params=params(),
        name="inside_backward",
        cost_estimate=cost(20),
    )(x, act, act, gm, left, right, still, taken)


def finish_kernel(
    heads,
    pairs,
    blocks,
    v_ref,
    x_ref,
    b_ref,
    c_ref,
    g_ref,
    dx_ref,
    db_ref,
    dc_ref,
    pq_ref,
    pac_ref,
    states_ref,
    step_ref,
    cum_ref,
    raw_ref,
    bias_ref,
    alog_ref,
    etot_ref,
    skip_ref,
    start_ref,
    ones_ref,
    fan_ref,
    gact_ref,
    graw_ref,
    gbias_ref,
    grate_ref,
    state,
    tails,
    early,
    first,
    second,
    third,
    spread,
    three,
):
    at = pl.program_id(0)
    step_at = blocks // GROUP - 1 - at
    inner = pairs * LANES
    width = state.shape[0]

    @pl.when(at == 0)
    def _():
        state[...] = start_ref[...]
        gbias_ref[...] = jnp.zeros_like(gbias_ref)
        grate_ref[...] = jnp.zeros_like(grate_ref)

    later = (rows_at() <= lanes_at()).astype(f32)
    earlier = (rows_at() > lanes_at()).astype(f32)
    rates = jnp.exp(alog_ref[...])
    for part, r in reversed(list(enumerate(parts_of_step()))):
        inputs, outputs = b_ref[r, :], c_ref[r, :]
        leaving = state[...]
        leaving_low = leaving.astype(bf16)
        entering = states_ref[part * width : (part + 1) * width, :]
        etot = etot_ref[pl.ds(step_at * GROUP + part, 1), :]
        held = jnp.sum(leaving * entering.astype(f32), axis=0, keepdims=True) * etot
        held = mm(jnp.broadcast_to(held, (8, inner)).astype(bf16), ones_ref[...])[0:1, :]
        spread[...] = mm(inputs, leaving_low)
        cum, step = cum_ref[r, :], step_ref[r, :]
        grow = jnp.exp(cum)
        tail = jnp.exp(cum[ROWS - 1 :, :] - cum)
        three[...] = mm(
            jnp.concatenate([halves(step, heads), halves(tail, heads), halves(grow, heads)], axis=0),
            fan_ref[...],
        )
        for i in range(pairs):
            s = slab(i)
            v = v_ref[r, s].astype(f32)
            g = g_ref[r, s].astype(f32)
            steps = three[:ROWS, s]
            x = x_ref[r, s].astype(f32)
            part_tail = three[ROWS : 2 * ROWS, s]
            more = spread[:, s] * part_tail
            dx = dx_ref[r, s] + more
            first[:, s] = (x * more).astype(bf16)
            direct = v * dx
            high = direct.astype(bf16)
            second[:, s] = high
            third[:, s] = (direct - high.astype(f32)).astype(bf16)
            gact_ref[r, s] = (steps * dx + skip_ref[:, s] * g).astype(bf16)
            tails[:, s] = (x * part_tail).astype(bf16)
            early[:, s] = (g * three[2 * ROWS :, s]).astype(bf16)
        gact_ref[r, inner : inner + width] = (db_ref[r, :] + mm_nt(tails[...], leaving_low)).astype(bf16)
        gact_ref[r, inner + width :] = (dc_ref[r, :] + mm_nt(early[...], entering)).astype(bf16)
        gdecay = (
            jnp.dot(later, pq_ref[r, :] + pac_ref[r, :], precision=highest, preferred_element_type=f32)
            + jnp.dot(
                earlier, mm(first[...], ones_ref[...]), precision=highest, preferred_element_type=f32
            )
            + held
        )
        gstep = mm(second[...], ones_ref[...]) + mm(third[...], ones_ref[...]) - rates * gdecay
        graw = gstep.astype(bf16).astype(f32) * sigmoid(raw_ref[r, :] + bias_ref[...])
        graw_ref[r, :] = graw.astype(bf16)
        gbias_ref[...] += jnp.sum(graw, axis=0, keepdims=True)
        grate_ref[...] += jnp.sum(step * gdecay, axis=0, keepdims=True)
        state[...] = etot * leaving + mm_tn(outputs, early[...])


def mixer_finish(
    act, x, gm, dx, db, dc, pq, pac, states, step, cum, raw, bias, a_log, etot, skip, start, ones, fan, heads, inner, width
):
    rows = act.shape[0]
    blocks = rows // ROWS
    inputs_at = inner // width
    channels = act.shape[1]

    def backwards(columns, height=GROUP * ROWS, column_at=0):
        return pl.BlockSpec((height, columns), lambda i: (blocks // GROUP - 1 - i, column_at))

    return pl.pallas_call(
        functools.partial(finish_kernel, heads, inner // LANES, blocks),
        grid=(blocks // GROUP,),
        in_specs=[
            backwards(inner),
            backwards(inner),
            backwards(width, column_at=inputs_at),
            backwards(width, column_at=inputs_at + 1),
            backwards(inner),
            backwards(inner),
            backwards(width),
            backwards(width),
            backwards(LANES),
            backwards(LANES),
            backwards(inner, GROUP * width),
            backwards(LANES),
            backwards(LANES),
            backwards(LANES),
            whole((1, LANES)),
            whole((1, LANES)),
            whole(etot.shape),
            whole((1, inner)),
            whole((width, inner)),
            whole((inner, LANES)),
            whole(fan.shape),
        ],
        out_specs=[backwards(channels), backwards(LANES), whole((1, LANES)), whole((1, LANES))],
        out_shape=[
            jax.ShapeDtypeStruct((rows, channels), bf16),
            jax.ShapeDtypeStruct((rows, LANES), bf16),
            jax.ShapeDtypeStruct((1, LANES), f32),
            jax.ShapeDtypeStruct((1, LANES), f32),
        ],
        scratch_shapes=[
            pltpu.VMEM((width, inner), f32),
            pltpu.VMEM((ROWS, inner), bf16),
            pltpu.VMEM((ROWS, inner), bf16),
            pltpu.VMEM((ROWS, inner), bf16),
            pltpu.VMEM((ROWS, inner), bf16),
            pltpu.VMEM((ROWS, inner), bf16),
            pltpu.VMEM((ROWS, inner), f32),
            pltpu.VMEM((3 * ROWS, inner), f32),
        ],
        compiler_params=params(),
        name="mixer_finish",
        cost_estimate=cost(16),
    )(act, x, act, act, gm, dx, db, dc, pq, pac, states, step, cum, raw, bias, a_log, etot, skip, start, ones, fan)


def conv_back_kernel(
    span, rows, blocks, cin_ref, gact_ref, graw_ref, taps_ref, bias_ref, next_ref,
    gproj_ref, gtaps_ref, gbias_ref, held, grads,
):
    part = 256
    at = pl.program_id(0)

    @pl.when(at == blocks)
    def _():
        gproj_ref[...] = graw_ref[...]

    @pl.when(at < blocks)
    def _():
        held[...] = cin_ref[...].astype(f32)
        grads[rows : rows + 8, :] = next_ref[...]
        gbias = jnp.zeros((1, LANES), f32)
        gtaps = [jnp.zeros((1, LANES), f32)] * span
        for start in range(0, rows, part):
            total = jnp.broadcast_to(bias_ref[0:1, :], (part, LANES))
            seen = []
            for k in range(span):
                first = HALO + start - (span - 1) + k
                seen.append(held[first : first + part, :])
                total = total + taps_ref[k : k + 1, :] * seen[k]
            sig = sigmoid(total)
            grad = gact_ref[start : start + part, :].astype(f32) * (sig * (1.0 + total * (1.0 - sig)))
            grads[start : start + part, :] = grad
            gbias = gbias + jnp.sum(grad, axis=0, keepdims=True)
            for k in range(span):
                gtaps[k] = gtaps[k] + jnp.sum(seen[k] * grad, axis=0, keepdims=True)
        gbias_ref[...] = gbias
        for k in range(span):
            gtaps_ref[k : k + 1, :] = gtaps[k]
        for start in range(0, rows, part):
            total = jnp.zeros((part, LANES), f32)
            for k in range(span):
                first = start + span - 1 - k
                total = total + taps_ref[k : k + 1, :] * grads[first : first + part, :]
            gproj_ref[start : start + part, :] = total.astype(bf16)


def conv_backward(cin, gact, graw, taps, bias, nexts, begin, blocks, extra):
    rows = gact.shape[0]
    span = taps.shape[0]

    def columns(height, offset=begin):
        return pl.BlockSpec((height, LANES), lambda i: (0, offset + jnp.minimum(i, blocks - 1)))

    return pl.pallas_call(
        functools.partial(conv_back_kernel, span, rows, blocks),
        grid=(blocks + extra,),
        in_specs=[
            columns(rows + HALO),
            columns(rows),
            whole((rows, LANES)),
            columns(span),
            columns(1),
            columns(8),
        ],
        out_specs=[
            pl.BlockSpec((rows, LANES), lambda i: (0, i)),
            columns(span, 0),
            columns(1, 0),
        ],
        out_shape=[
            jax.ShapeDtypeStruct((rows, (blocks + extra) * LANES), bf16),
            jax.ShapeDtypeStruct((span, blocks * LANES), f32),
            jax.ShapeDtypeStruct((1, blocks * LANES), f32),
        ],
        scratch_shapes=[pltpu.VMEM((rows + HALO, LANES), f32), pltpu.VMEM((rows + HALO, LANES), f32)],
        compiler_params=params(),
        name="conv_backward",
        cost_estimate=cost(10),
    )(cin, gact, graw, taps, bias, nexts)


def local(
    tokens,
    norm_gain,
    in_weight,
    conv_weight,
    conv_bias,
    dt_bias,
    a_log,
    skip_gain,
    gate_gain,
    out_weight,
    cotangent,
):
    tokens, incoming = tokens[0], cotangent[0]
    rows, model = tokens.shape
    heads = a_log.shape[0]
    span, channels = conv_weight.shape
    inner = gate_gain.shape[0]
    width = (channels - inner) // 2
    head_width = inner // heads
    blocks = rows // ROWS
    pad = LANES - heads

    order = gathered_order()
    conv_flight = Flight(gather(jnp.pad(in_weight[:, inner:], ((0, 0), (0, pad)))))
    before = shifted(tokens[rows - HALO :], "seq", 1)

    def first_norm(block):
        block = block.astype(f32)
        scale = lax.rsqrt(jnp.mean(block * block, axis=1, keepdims=True) + epsilon)
        return (block * scale * norm_gain).astype(bf16), scale

    own, own_scale = first_norm(tokens)
    gate_part, out_weight, own = conv_flight.step(in_weight[:, :inner], out_weight, own)
    w_gate = lax.all_gather(gate_part, "fsdp", axis=0, tiled=True)
    w_out = lax.all_gather(out_weight, "fsdp", axis=0, tiled=True)
    conv_near, conv_far = conv_flight.finish()
    act, cin, raw, conv_near, conv_far = conv_forward(
        jnp.stack([jnp.int32(at) for at in order]), first_norm(before)[0], own, conv_near, conv_far,
        conv_weight, conv_bias[None],
    )
    bias_row = jnp.pad(dt_bias, (0, pad))[None]
    alog_row = jnp.pad(a_log, (0, pad))[None]
    step, cum, left, right = steps_forward(raw, bias_row, alog_row, heads)

    totals = cum.reshape(blocks, ROWS, LANES)[:, -1, :heads]
    befores = jnp.cumsum(totals, axis=0) - totals
    etot = jnp.repeat(jnp.exp(totals), head_width, axis=1)
    ebef = jnp.repeat(jnp.exp(befores), head_width, axis=1)
    skip = jnp.repeat(skip_gain, head_width)[None]
    def fanned(count, each):
        row, column = np.arange(LANES)[:, None], np.arange(count)[None]
        return ((row < 3 * heads) & (row % heads == column // each)).astype(ml_dtypes.bfloat16)

    def gathering(count, each):
        return (np.arange(count)[:, None] // each == np.arange(LANES)[None]).astype(ml_dtypes.bfloat16)

    fan = fanned(inner, head_width)
    still = fanned(heads * LANES, LANES)
    ones = gathering(inner, head_width)
    taken = gathering(heads * LANES, LANES)
    whole_decay = jnp.repeat(jnp.exp(jnp.sum(totals, axis=0)), head_width)[None]

    x, leaves = piece_state(act, step, cum, etot, fan, heads, inner, width)
    ahead = Flight(handed_on(leaves, whole_decay, 1))
    y = inside_forward(x, act, left, right, still, inner, width)
    y = ahead.step(y)
    z = mm(own, w_gate)
    z = ahead.step(z)
    gn = mm_nt(incoming, w_out)
    gn = ahead.step(gn)
    start = ahead.finish()
    out_in, gm, gz, states, pac, back, ggain, gskip = gate_both(
        y, act, z, gn, step, cum, etot, ebef, skip, gate_gain[None], start, ones, fan, heads, inner, width
    )

    behind = Flight(handed_on(back, whole_decay, -1))
    part_out = mm_tn(out_in, incoming).astype(bf16)
    part_gate = mm_tn(own, gz).astype(bf16)
    pulled_gate = mm_nt(gz, w_gate)
    part_out, part_gate, pulled_gate = behind.step(part_out, part_gate, pulled_gate)
    slices = inner // model
    sums = Flight(
        sum_scatter([part_out] + [part_gate[:, i * model : (i + 1) * model] for i in range(slices)])
    )
    gm = behind.step(gm)
    gm = sums.step(gm)
    dx, db, dc, pq = inside_backward(x, act, gm, left, right, still, taken, inner, width)
    dx = behind.step(dx)
    dx = sums.step(dx)
    back_start = behind.finish()
    gact, graw, gdt, grate = mixer_finish(
        act, x, gm, dx, db, dc, pq, pac, states, step, cum, raw, bias_row, alog_row, etot, skip,
        back_start, ones, fan, heads, inner, width,
    )
    top = conv_bias + jnp.zeros((8, channels), f32)
    for k in range(span):
        first = HALO - (span - 1) + k
        top = top + conv_weight[k] * cin[first : first + 8].astype(f32)
    sig = sigmoid(top)
    nexts = shifted(gact[:8].astype(f32) * (sig * (1.0 + top * (1.0 - sig))), "seq", -1)
    blocks_a = channels // LANES // 2
    blocks_b = channels // LANES - blocks_a
    cut = blocks_a * LANES
    gproj_a, gtaps_a, gcbias_a = conv_backward(
        cin, gact, graw, conv_weight, conv_bias[None], nexts, 0, blocks_a, 0
    )
    part_a = mm_tn(own, gproj_a).astype(bf16)
    part_a, gact = sums.step(part_a, gact)
    sums.step()
    sums_a = Flight(sum_scatter([part_a]))
    gproj_b, gtaps_b, gcbias_b = conv_backward(
        cin, gact, graw, conv_weight, conv_bias[None], nexts, blocks_a, blocks_b, 1
    )
    gproj_b = sums_a.step(gproj_b)
    part_b = mm_tn(own, gproj_b).astype(bf16)
    sums_b = Flight(sum_scatter([part_b]))
    pulled_near = mm_nt(gproj_a, conv_near[:, :cut])
    pulled_far = mm_nt(gproj_a, conv_far[:, :cut])
    pulled_near, pulled_far = sums_b.step(pulled_near, pulled_far)
    pulled_near, pulled_far = sums_a.step(pulled_near, pulled_far)
    pulled_near = pulled_near + mm_nt(gproj_b, conv_near[:, cut:])
    pulled_far = pulled_far + mm_nt(gproj_b, conv_far[:, cut:])
    pulled_near, pulled_far = sums.step(pulled_near, pulled_far)
    pulled_conv = jnp.concatenate([pulled_near, pulled_far], axis=1)
    places = [sum(jnp.where(at == block, i, 0) for i, at in enumerate(order)) for block in range(len(order))]
    grad_normed = pulled_gate + in_order(pulled_conv, places)
    unit = tokens.astype(f32) * own_scale
    pulled = grad_normed * norm_gain
    mean_pull = jnp.mean(pulled * unit, axis=1, keepdims=True)
    grad_tokens = incoming.astype(f32) + own_scale * (pulled - unit * mean_pull)
    grad_norm_gain = jnp.sum(grad_normed * unit, axis=0)
    small = [
        grad_norm_gain,
        jnp.concatenate([gtaps_a, gtaps_b], axis=1).reshape(-1),
        gcbias_a[0],
        gcbias_b[0],
        gdt[0, :heads],
        grate[0, :heads] * -jnp.exp(a_log),
        jnp.sum(gskip.reshape(heads, head_width), axis=1),
        ggain[0],
    ]
    small_sums = Flight(sum_all(jnp.concatenate(small)))
    small_sums.flying = (sums_a.step(*small_sums.flying),)
    sums_a.step()
    small_sums.step()
    small_sums.flying = (sums_b.step(*small_sums.flying),)
    sums_b.step()
    small_sums.step()
    mixed = (tokens.astype(f32) + mm(out_in, w_out)).astype(bf16)
    mixed = small_sums.step(mixed)
    summed_parts = sums.finish()
    grad_out_weight = summed_parts[0]
    (grad_conv_a,) = sums_a.finish()
    (grad_conv_b,) = sums_b.finish()
    summed = small_sums.finish()

    grad_in_weight = jnp.concatenate(
        summed_parts[1:] + [grad_conv_a, grad_conv_b[:, : channels - cut + heads]], axis=1
    )
    sizes = [part.shape[0] for part in small]
    split, at = [], 0
    for size in sizes:
        split.append(summed[at : at + size])
        at += size
    return (
        mixed[None],
        grad_tokens[None],
        grad_in_weight,
        grad_out_weight,
        split[0],
        split[1].reshape(span, channels),
        jnp.concatenate(split[2:4]),
        *split[4:],
    )


def solution(mesh):
    tokens = P("fsdp", "seq", None)
    sharded = P("fsdp", None)
    spread = P(("seq", "fsdp"), None)
    return jax.shard_map(
        local,
        mesh=mesh,
        in_specs=(tokens, P(), sharded, P(), P(), P(), P(), P(), P(), sharded, tokens),
        out_specs=(tokens, tokens, spread, spread, P(), P(), P(), P(), P(), P(), P()),
        check_vma=False,
    )
```

```python
import functools

import jax
import jax.numpy as jnp
import ml_dtypes
import numpy as np
from jax import lax
from jax.experimental import pallas as pl
from jax.experimental.pallas import tpu as pltpu
from jax.sharding import PartitionSpec as P

ROWS = 128
GROUP = 2
LANES = 128
HALO = 16
VMEM = 48 * 1024 * 1024
LOG2E = 1.4426950408889634
epsilon = 1e-05
bf16 = jnp.bfloat16
f32 = jnp.float32
highest = lax.Precision.HIGHEST


def shifted(block, axis, distance):
    size = lax.axis_size(axis)
    route = [(i - distance, i) for i in range(size) if 0 <= i - distance < size]
    return lax.ppermute(block, axis, route)


def exchanged(block, axis, bit):
    return lax.ppermute(block, axis, [(i, i ^ bit) for i in range(lax.axis_size(axis))])


def pick(block, at, axis):
    return lax.dynamic_index_in_dim(block, at, axis, keepdims=False)


class Flight:
    def __init__(self, steps):
        self.steps, self.value, self.flying = steps, None, None
        self.advance(None)

    def advance(self, arrived):
        try:
            self.flying = self.steps.send(arrived)
        except StopIteration as end:
            self.flying, self.value = None, end.value

    def step(self, *others):
        if self.flying is not None:
            count = len(self.flying)
            tied = lax.optimization_barrier((*self.flying, *others))
            others = tied[count:]
            self.advance(tuple(tied[:count]))
        return others[0] if len(others) == 1 else others

    def finish(self):
        while self.flying is not None:
            self.advance(self.flying)
        return self.value


def gather(weight):
    rows = weight.shape[0]
    if lax.axis_size("fsdp") != 8 or rows % 32:
        full = lax.all_gather(weight, "fsdp", axis=0, tiled=True)
        return [full[: full.shape[0] // 2]], [full[full.shape[0] // 2 :]]
    first, last = weight[: rows // 2], weight[rows // 2 :]

    def crossed(block):
        return exchanged(block, "fsdp", 1)

    first_y, last_x = exchanged(first, "fsdp", 4), exchanged(last, "fsdp", 2)
    first_x, last_y = exchanged(first, "fsdp", 2), exchanged(last, "fsdp", 4)
    far = [crossed(weight)]
    first_y, last_x, first_x, last_y = yield first_y, last_x, first_x, last_y
    first_xy, last_xy = exchanged(first_y, "fsdp", 2), exchanged(last_x, "fsdp", 4)
    far += [crossed(block) for block in (first_x, last_x, first_y, last_y)]
    first_xy, last_xy, *far = yield first_xy, last_xy, *far
    far += [crossed(first_xy), crossed(last_xy)]
    far = yield tuple(far)
    return [weight, first_x, last_x, first_y, last_y, first_xy, last_xy], list(far)


def gathered_order():
    group = lax.axis_size("fsdp")
    if group != 8:
        return list(range(group))
    me = lax.axis_index("fsdp")
    return [me ^ distance for distance in (0, 2, 4, 6, 1, 3, 5, 7)]


def in_order(block, order):
    size = block.shape[1] // len(order)
    return jnp.concatenate(
        [lax.dynamic_slice_in_dim(block, at * size, size, axis=1) for at in order], axis=1
    )


def handed_on(state, decay, distance):
    entering = jnp.zeros(state.shape, f32)
    state = state.astype(f32)
    for _ in range(lax.axis_size("seq") - 1):
        leaving = (state + decay * entering).astype(bf16)
        (arrived,) = yield (shifted(leaving, "seq", distance),)
        entering = arrived.astype(f32)
    return entering


def sum_all(vector):
    for axis in ("fsdp", "seq"):
        size = lax.axis_size(axis)
        if size & (size - 1):
            vector = lax.psum(vector, axis)
            continue
        for bit in range(size.bit_length() - 1):
            (other,) = yield (exchanged(vector, axis, 1 << bit),)
            vector = vector + other
    return vector


def sum_scatter(parts):
    pieces, group = lax.axis_size("seq"), lax.axis_size("fsdp")
    bits = group.bit_length() - 1
    rows = [part.shape[0] // (pieces * group) for part in parts]
    widths = [part.shape[1] for part in parts]
    fits = len(parts) == 2 and (rows[1] * widths[1]) % widths[0] == 0 or len(parts) == 1 and rows[0] % 2 == 0
    if group != 1 << bits or bits < 1 or not fits:
        return [
            lax.psum_scatter(part.astype(f32), ("seq", "fsdp"), scatter_dimension=0, tiled=True)
            for part in parts
        ]
    me, place = lax.axis_index("fsdp"), lax.axis_index("seq")
    parts = [part.reshape(pieces, group // 2, 2, -1, part.shape[1]) for part in parts]
    mine = me & 1
    got = yield tuple(exchanged(pick(part, 1 - mine, 2), "fsdp", 1) for part in parts)
    halves = [pick(part, mine, 2) + other for part, other in zip(parts, got)]
    if len(halves) == 1:
        halves = [halves[0][:, :, : rows[0] // 2], halves[0][:, :, rows[0] // 2 :]]
    ways = [list(range(bits - 1, 0, -1)), list(range(bits - 1, 0, -1))]
    halves = [part.reshape((pieces,) + (2,) * (bits - 1) + part.shape[2:]) for part in halves]
    for _ in range(bits - 1):
        taken = [ways[0][-1], ways[1][0]]
        places = [1 + ways[way].index(taken[way]) for way in (0, 1)]
        sides = [(me >> taken[way]) & 1 for way in (0, 1)]
        got = yield tuple(
            exchanged(pick(halves[way], 1 - sides[way], places[way]), "fsdp", 1 << taken[way])
            for way in (0, 1)
        )
        halves = [pick(halves[way], sides[way], places[way]) + got[way] for way in (0, 1)]
        for way in (0, 1):
            ways[way].remove(taken[way])
    part = jnp.concatenate([halves[0], halves[1].reshape(pieces, -1, widths[0])], axis=1)
    got = yield tuple(
        lax.ppermute(
            pick(part, (place + ahead) % pieces, 0), "seq", [(i, (i + ahead) % pieces) for i in range(pieces)]
        )
        for ahead in range(1, pieces)
    )
    own = sum((block.astype(f32) for block in got), pick(part, place, 0).astype(f32))
    if len(rows) == 1:
        return [own]
    return [own[: rows[0]], own[rows[0] :].reshape(rows[1], widths[1])]


def mm(a, b):
    return lax.dot_general(a, b, (((1,), (0,)), ((), ())), preferred_element_type=f32)


def mm_nt(a, b):
    return lax.dot_general(a, b, (((1,), (1,)), ((), ())), preferred_element_type=f32)


def mm_tn(a, b):
    return lax.dot_general(a, b, (((0,), (0,)), ((), ())), preferred_element_type=f32)


def sigmoid(v):
    return 0.5 + 0.5 * jnp.tanh(0.5 * v)


def rows_at():
    return lax.broadcasted_iota(jnp.int32, (ROWS, LANES), 0)


def lanes_at():
    return lax.broadcasted_iota(jnp.int32, (ROWS, LANES), 1)


def slab(i):
    return slice(i * LANES, (i + 1) * LANES)


def wide(i):
    return slice(i * 2 * LANES, (i + 1) * 2 * LANES)


def halves(columns, heads):
    lane = lanes_at()
    high = columns.astype(bf16).astype(f32)
    rest = pltpu.roll(columns - high, heads, 1)
    return jnp.where(lane < heads, high, jnp.where(lane < 2 * heads, rest, 0.0)).astype(bf16)


def low_lanes():
    return (lanes_at() < LANES // 2).astype(f32).astype(bf16), (lanes_at() >= LANES // 2).astype(f32).astype(bf16)


def diagonal(block, low, high):
    return jnp.concatenate([block * low, block * high], axis=0)


def parts_of_step():
    return [slice(part * ROWS, (part + 1) * ROWS) for part in range(GROUP)]


def params(**more):
    return pltpu.CompilerParams(vmem_limit_bytes=VMEM, **more)


def cost(microseconds):
    return pl.CostEstimate(flops=int(microseconds * 1e9), bytes_accessed=4 * 1024 * 1024, transcendentals=0)


def whole(shape):
    return pl.BlockSpec(shape, lambda i: (0,) * len(shape))


def by_rows(width, rows=GROUP * ROWS):
    return pl.BlockSpec((rows, width), lambda i: (i, 0))


def conv_kernel(span, rows, pieces, order_ref, before_ref, own_ref, *refs):
    near_refs, far_refs = refs[:pieces], refs[pieces : 2 * pieces]
    taps_ref, bias_ref, act_ref, cin_ref, raw_ref, near_ref, far_ref, held, normed_ref = refs[2 * pieces :]
    at = pl.program_id(0)
    last = pl.num_programs(0) - 1
    near = jnp.concatenate([ref[...] for ref in near_refs], axis=0)
    far = jnp.concatenate([ref[...] for ref in far_refs], axis=0)
    near_ref[...] = near
    far_ref[...] = far
    half = near.shape[0]
    size = own_ref.shape[1] // order_ref.shape[0]

    @pl.when(at == 0)
    def _():
        for i in range(order_ref.shape[0]):
            source = pl.ds(pl.multiple_of(order_ref[i] * size, size), size)
            normed_ref[:HALO, i * size : (i + 1) * size] = before_ref[:, source]
            normed_ref[HALO:, i * size : (i + 1) * size] = own_ref[:, source]

    def projected(start, size):
        block = normed_ref[start : start + size, :]
        return mm(block[:, :half], near) + mm(block[:, half:], far)

    part = 256

    @pl.when(at == last)
    def _():
        for start in range(0, rows, part):
            raw_ref[start : start + part, :] = projected(HALO + start, part)[:, :LANES]

    @pl.when(at < last)
    def _():
        for start, size in [(0, HALO)] + [(HALO + at, part) for at in range(0, rows, part)]:
            block = projected(start, size).astype(bf16)
            cin_ref[start : start + size, :] = block
            held[start : start + size, :] = block.astype(f32)
        for start in range(0, rows, part):
            total = jnp.broadcast_to(bias_ref[0:1, :], (part, bias_ref.shape[1]))
            for k in range(span):
                first = HALO + start - (span - 1) + k
                total = total + taps_ref[k : k + 1, :] * held[first : first + part, :]
            act_ref[start : start + part, :] = (total * sigmoid(total)).astype(bf16)


def conv_forward(order, before, own, near, far, taps, bias):
    rows, width = own.shape
    channels = taps.shape[1]
    total = near[0].shape[1]
    cols = 2 * LANES
    blocks = channels // cols

    def columns(height, upto=blocks):
        return pl.BlockSpec((height, cols), lambda i: (0, jnp.minimum(i, upto)))

    return pl.pallas_call(
        functools.partial(conv_kernel, taps.shape[0], rows, len(near)),
        grid=(blocks + 1,),
        in_specs=[pl.BlockSpec(memory_space=pltpu.SMEM), whole((HALO, width)), whole((rows, width))]
        + [columns(piece.shape[0]) for piece in near + far]
        + [columns(taps.shape[0], blocks - 1), columns(1, blocks - 1)],
        out_specs=[
            columns(rows, blocks - 1),
            columns(rows + HALO, blocks - 1),
            whole((rows, LANES)),
            columns(width // 2),
            columns(width // 2),
        ],
        out_shape=[
            jax.ShapeDtypeStruct((rows, channels), bf16),
            jax.ShapeDtypeStruct((rows + HALO, channels), bf16),
            jax.ShapeDtypeStruct((rows, LANES), f32),
            jax.ShapeDtypeStruct((width // 2, total), bf16),
            jax.ShapeDtypeStruct((width // 2, total), bf16),
        ],
        scratch_shapes=[pltpu.VMEM((rows + HALO, cols), f32), pltpu.VMEM((rows + HALO, width), bf16)],
        compiler_params=params(),
        name="conv_forward",
        cost_estimate=cost(16),
    )(order, before, own, *near, *far, taps, bias)


def steps_kernel(blocks, heads, raw_ref, bias_ref, alog_ref, step_ref, cum_ref, left_ref, right_ref, rows3):
    lane = lanes_at()
    lower = (rows_at() >= lane).astype(f32)
    rates = -jnp.exp(alog_ref[...])
    rows3[...] = jnp.zeros_like(rows3)
    for b in range(blocks):
        rows = slice(b * ROWS, (b + 1) * ROWS)
        soft = raw_ref[rows, :] + bias_ref[...]
        soft = jnp.maximum(soft, 0.0) + jnp.log1p(jnp.exp(-jnp.abs(soft)))
        step = soft.astype(bf16).astype(f32)
        step_ref[rows, :] = step
        cum = jnp.dot(lower, step * rates, precision=highest, preferred_element_type=f32)
        cum_ref[rows, :] = cum
        cum = cum * LOG2E
        parts, rest = [], cum
        for _ in range(3):
            part = rest.astype(bf16).astype(f32)
            parts.append(part)
            rest = rest - part
        left = jnp.where(lane < 3 * heads + 3, 1.0, 0.0)
        for k in (2, 1, 0):
            left = jnp.where(lane < (k + 1) * heads, pltpu.roll(parts[k], k * heads, 1), left)
        left_ref[rows, :] = left.astype(bf16)
        for k in range(3):
            flipped = -parts[k].T
            for h in range(heads):
                rows3[k : k + 1, slab(h)] = flipped[h : h + 1, :]
        right_ref[b * HALO : (b + 1) * HALO, :] = rows3[...].astype(bf16)


def steps_forward(raw, bias, a_log, heads):
    rows = raw.shape[0]
    blocks = rows // ROWS
    shape = jax.ShapeDtypeStruct((rows, LANES), f32)
    return pl.pallas_call(
        functools.partial(steps_kernel, blocks, heads),
        out_shape=[
            shape,
            shape,
            jax.ShapeDtypeStruct((rows, LANES), bf16),
            jax.ShapeDtypeStruct((blocks * HALO, heads * LANES), bf16),
        ],
        scratch_shapes=[pltpu.VMEM((HALO, heads * LANES), f32)],
        compiler_params=params(),
        name="steps_forward",
        cost_estimate=cost(6),
    )(raw, bias, a_log)


def state_kernel(heads, v_ref, b_ref, step_ref, cum_ref, etot_ref, fan_ref, x_ref, f_ref, state, tails, both):
    at = pl.program_id(0)

    @pl.when(at == 0)
    def _():
        state[...] = jnp.zeros_like(state)

    for part, r in enumerate(parts_of_step()):
        cum, step = cum_ref[r, :], step_ref[r, :]
        tail = jnp.exp(cum[ROWS - 1 :, :] - cum) * step
        both[...] = mm(jnp.concatenate([halves(step, heads), halves(tail, heads)], axis=0), fan_ref[...])
        v = v_ref[r, :].astype(f32)
        x_ref[r, :] = (v * both[:ROWS, :]).astype(bf16)
        tails[...] = (v * both[ROWS:, :]).astype(bf16)
        etot = etot_ref[pl.ds(at * GROUP + part, 1), :]
        state[...] = etot * state[...] + mm_tn(b_ref[r, :], tails[...])

    @pl.when(at == pl.num_programs(0) - 1)
    def _():
        f_ref[...] = state[...].astype(bf16)


def piece_state(act, step, cum, etot, fan, heads, inner, width):
    rows = act.shape[0]
    inputs_at = inner // width
    return pl.pallas_call(
        functools.partial(state_kernel, heads),
        grid=(rows // (GROUP * ROWS),),
        in_specs=[
            by_rows(inner),
            pl.BlockSpec((GROUP * ROWS, width), lambda i: (i, inputs_at)),
            by_rows(LANES),
            by_rows(LANES),
            whole(etot.shape),
            whole(fan.shape),
        ],
        out_specs=[by_rows(inner), whole((width, inner))],
        out_shape=[
            jax.ShapeDtypeStruct((rows, inner), bf16),
            jax.ShapeDtypeStruct((width, inner), bf16),
        ],
        scratch_shapes=[
            pltpu.VMEM((width, inner), f32),
            pltpu.VMEM((ROWS, inner), bf16),
            pltpu.VMEM((2 * ROWS, inner), f32),
        ],
        compiler_params=params(),
        name="piece_state",
        cost_estimate=cost(6),
    )(act, act, step, cum, etot, fan)


def inside_kernel(pairs, x_ref, b_ref, c_ref, left_ref, right_ref, still_ref, y_ref, right):
    fixed = left_rows(right, still_ref, right_ref)
    low, high = low_lanes()
    for part, r in enumerate(parts_of_step()):
        scores = jnp.where(rows_at() >= lanes_at(), mm_nt(c_ref[r, :], b_ref[r, :]), 0.0)
        scores = jnp.concatenate([scores, scores], axis=1)
        left = left_ref[r, :]
        for i in range(pairs):
            spread = mm(left, fixed[part, :, wide(i)])
            weights = (scores * jnp.exp2(jnp.minimum(spread, 0.0))).astype(bf16)
            y_ref[r, slab(i)] = mm(weights, diagonal(x_ref[r, slab(i)], low, high))


def left_rows(right, still_ref, right_ref):
    @pl.when(pl.program_id(0) == 0)
    def _():
        for part in range(GROUP):
            right[part, :, :] = still_ref[...]

    own = still_ref.shape[0] - 2 * HALO
    for part in range(GROUP):
        right[part, own : own + HALO, :] = right_ref[part * HALO : (part + 1) * HALO, :]
    return right


def inside_forward(x, act, left, right, still, inner, width):
    rows = act.shape[0]
    inputs_at = inner // width
    return pl.pallas_call(
        functools.partial(inside_kernel, inner // LANES),
        grid=(rows // (GROUP * ROWS),),
        in_specs=[
            by_rows(inner),
            pl.BlockSpec((GROUP * ROWS, width), lambda i: (i, inputs_at)),
            pl.BlockSpec((GROUP * ROWS, width), lambda i: (i, inputs_at + 1)),
            by_rows(LANES),
            by_rows(right.shape[1], GROUP * HALO),
            whole(still.shape),
        ],
        out_specs=by_rows(inner),
        out_shape=jax.ShapeDtypeStruct((rows, inner), f32),
        scratch_shapes=[pltpu.VMEM((GROUP,) + still.shape, bf16)],
        compiler_params=params(),
        name="inside_forward",
        cost_estimate=cost(10),
    )(x, act, act, left, right, still)


def gate_kernel(
    heads,
    pairs,
    y_ref,
    v_ref,
    b_ref,
    c_ref,
    z_ref,
    gn_ref,
    step_ref,
    cum_ref,
    etot_ref,
    ebef_ref,
    skip_ref,
    gain_ref,
    start_ref,
    ones_ref,
    fan_ref,
    out_ref,
    gm_ref,
    gz_ref,
    states_ref,
    pac_ref,
    back_ref,
    ggain_ref,
    gskip_ref,
    state,
    back,
    across,
    mixer,
    gated,
    early,
    tails,
    products,
    both,
):
    at = pl.program_id(0)
    width = pairs * LANES

    @pl.when(at == 0)
    def _():
        state[...] = start_ref[...]
        back[...] = jnp.zeros_like(back)
        ggain_ref[...] = jnp.zeros_like(ggain_ref)
        gskip_ref[...] = jnp.zeros_like(gskip_ref)

    for part, r in enumerate(parts_of_step()):
        outputs = c_ref[r, :]
        entering = state[...].astype(bf16)
        states_ref[part * state.shape[0] : (part + 1) * state.shape[0], :] = entering
        across[...] = mm(outputs, entering)
        cum = cum_ref[r, :]
        grow = jnp.exp(cum)
        tail = jnp.exp(cum[ROWS - 1 :, :] - cum) * step_ref[r, :]
        both[...] = mm(jnp.concatenate([halves(grow, heads), halves(tail, heads)], axis=0), fan_ref[...])
        squares = jnp.zeros((ROWS, LANES), f32)
        meets = jnp.zeros((ROWS, LANES), f32)
        for i in range(pairs):
            s = slab(i)
            v = v_ref[r, s].astype(f32)
            ya = across[:, s] * both[:ROWS, s]
            across[:, s] = ya
            m = (y_ref[r, s] + ya + skip_ref[:, s] * v).astype(bf16)
            mixer[:, s] = m
            z = z_ref[r, s]
            product = m.astype(f32) * (z * sigmoid(z))
            gated[:, s] = product
            squares = squares + product * product
            meets = meets + gn_ref[r, s] * gain_ref[:, s] * product
            tails[:, s] = (v * both[ROWS:, s]).astype(bf16)
        scale = lax.rsqrt(jnp.sum(squares, axis=1, keepdims=True) / width + epsilon)
        pull = scale * scale * scale * (jnp.sum(meets, axis=1, keepdims=True) / width)
        for i in range(pairs):
            s = slab(i)
            v = v_ref[r, s].astype(f32)
            product = gated[:, s]
            unit = product * scale
            gain = gain_ref[:, s]
            gn = gn_ref[r, s]
            out_ref[r, s] = (unit * gain).astype(bf16)
            ggain_ref[:, s] += jnp.sum(gn * unit, axis=0, keepdims=True)
            grad = gn * gain * scale - product * pull
            z = z_ref[r, s]
            sig = sigmoid(z)
            swish = z * sig
            gm = (grad * swish).astype(bf16)
            gm_ref[r, s] = gm
            slope = sig + swish * (1.0 - sig)
            gz_ref[r, s] = (grad * mixer[:, s].astype(f32) * slope).astype(bf16)
            g = gm.astype(f32)
            gskip_ref[:, s] += jnp.sum(g * v, axis=0, keepdims=True)
            products[:, s] = (g * across[:, s]).astype(bf16)
            early[:, s] = (g * both[:ROWS, s]).astype(bf16)
        pac_ref[r, :] = mm(products[...], ones_ref[...])
        block = at * GROUP + part
        back[...] += ebef_ref[pl.ds(block, 1), :] * mm_tn(outputs, early[...])
        state[...] = etot_ref[pl.ds(block, 1), :] * state[...] + mm_tn(b_ref[r, :], tails[...])

    @pl.when(at == pl.num_programs(0) - 1)
    def _():
        back_ref[...] = back[...].astype(bf16)


def gate_both(y, act, z, gn, step, cum, etot, ebef, skip, gain, start, ones, fan, heads, inner, width):
    rows = act.shape[0]
    inputs_at = inner // width
    blocks = rows // ROWS
    return pl.pallas_call(
        functools.partial(gate_kernel, heads, inner // LANES),
        grid=(blocks // GROUP,),
        in_specs=[
            by_rows(inner),
            by_rows(inner),
            pl.BlockSpec((GROUP * ROWS, width), lambda i: (i, inputs_at)),
            pl.BlockSpec((GROUP * ROWS, width), lambda i: (i, inputs_at + 1)),
            by_rows(inner),
            by_rows(inner),
            by_rows(LANES),
            by_rows(LANES),
            whole(etot.shape),
            whole(ebef.shape),
            whole((1, inner)),
            whole((1, inner)),
            whole((width, inner)),
            whole((inner, LANES)),
            whole(fan.shape),
        ],
        out_specs=[
            by_rows(inner),
            by_rows(inner),
            by_rows(inner),
            by_rows(inner, GROUP * width),
            by_rows(LANES),
            whole((width, inner)),
            whole((1, inner)),
            whole((1, inner)),
        ],
        out_shape=[
            jax.ShapeDtypeStruct((rows, inner), bf16),
            jax.ShapeDtypeStruct((rows, inner), bf16),
            jax.ShapeDtypeStruct((rows, inner), bf16),
            jax.ShapeDtypeStruct((blocks * width, inner), bf16),
            jax.ShapeDtypeStruct((rows, LANES), f32),
            jax.ShapeDtypeStruct((width, inner), bf16),
            jax.ShapeDtypeStruct((1, inner), f32),
            jax.ShapeDtypeStruct((1, inner), f32),
        ],
        scratch_shapes=[
            pltpu.VMEM((width, inner), f32),
            pltpu.VMEM((width, inner), f32),
            pltpu.VMEM((ROWS, inner), f32),
            pltpu.VMEM((ROWS, inner), bf16),
            pltpu.VMEM((ROWS, inner), f32),
            pltpu.VMEM((ROWS, inner), bf16),
            pltpu.VMEM((ROWS, inner), bf16),
            pltpu.VMEM((ROWS, inner), bf16),
            pltpu.VMEM((2 * ROWS, inner), f32),
        ],
        compiler_params=params(),
        name="gate_both",
        cost_estimate=cost(18),
    )(y, act, act, act, z, gn, step, cum, etot, ebef, skip, gain, start, ones, fan)


def inside_back_kernel(
    pairs, x_ref, b_ref, c_ref, g_ref, left_ref, right_ref, still_ref, taken_ref,
    dx_ref, db_ref, dc_ref, pq_ref, right, moved, late,
):
    fixed = left_rows(right, still_ref, right_ref)
    lane = lanes_at()
    low, high = low_lanes()
    ones = jnp.ones((16, ROWS), bf16)
    for part, r in enumerate(parts_of_step()):
        inputs, outputs = b_ref[r, :], c_ref[r, :]
        raw_scores = mm_nt(inputs, outputs)
        scores = jnp.where(rows_at() <= lane, raw_scores, 0.0)
        strict = jnp.where(rows_at() < lane, raw_scores, 0.0)
        scores = jnp.concatenate([scores, scores], axis=1)
        strict = jnp.concatenate([strict, strict], axis=1)
        left = -left_ref[r, :]
        gathered = jnp.zeros((ROWS, 2 * LANES), f32)
        for i in range(pairs):
            spread = mm(left, fixed[part, :, wide(i)])
            decay = jnp.exp2(jnp.minimum(spread, 0.0))
            stacked = diagonal(g_ref[r, slab(i)], low, high)
            grad = mm_nt(x_ref[r, slab(i)], stacked) * decay
            gathered = gathered + grad
            moved[:, wide(i)] = (grad * strict).astype(bf16)
            dx_ref[r, slab(i)] = mm((scores * decay).astype(bf16), stacked)
        late[...] = jnp.zeros_like(late)
        for i in range(pairs):
            sums = mm(ones, moved[:, wide(i)])
            late[2 * i : 2 * i + 1, :] = sums[0:1, :LANES]
            late[2 * i + 1 : 2 * i + 2, :] = sums[0:1, LANES:]
        pq_ref[r, :] = late[...].T - mm(moved[...], taken_ref[...])
        gathered = gathered[:, :LANES] + gathered[:, LANES:]
        gathered = jnp.where(rows_at() <= lane, gathered, 0.0).astype(bf16)
        db_ref[r, :] = mm(gathered, outputs)
        dc_ref[r, :] = mm_tn(gathered, inputs)


def inside_backward(x, act, gm, left, right, still, taken, inner, width):
    rows = act.shape[0]
    inputs_at = inner // width
    return pl.pallas_call(
        functools.partial(inside_back_kernel, inner // LANES),
        grid=(rows // (GROUP * ROWS),),
        in_specs=[
            by_rows(inner),
            pl.BlockSpec((GROUP * ROWS, width), lambda i: (i, inputs_at)),
            pl.BlockSpec((GROUP * ROWS, width), lambda i: (i, inputs_at + 1)),
            by_rows(inner),
            by_rows(LANES),
            by_rows(right.shape[1], GROUP * HALO),
            whole(still.shape),
            whole(taken.shape),
        ],
        out_specs=[by_rows(inner), by_rows(width), by_rows(width), by_rows(LANES)],
        out_shape=[
            jax.ShapeDtypeStruct((rows, inner), f32),
            jax.ShapeDtypeStruct((rows, width), f32),
            jax.ShapeDtypeStruct((rows, width), f32),
            jax.ShapeDtypeStruct((rows, LANES), f32),
        ],
        scratch_shapes=[
            pltpu.VMEM((GROUP,) + still.shape, bf16),
            pltpu.VMEM((ROWS, 2 * inner), bf16),
            pltpu.VMEM((LANES, ROWS), f32),
        ],
        compiler_params=params(),
        name="inside_backward",
        cost_estimate=cost(20),
    )(x, act, act, gm, left, right, still, taken)


def finish_kernel(
    heads,
    pairs,
    blocks,
    v_ref,
    x_ref,
    b_ref,
    c_ref,
    g_ref,
    dx_ref,
    db_ref,
    dc_ref,
    pq_ref,
    pac_ref,
    states_ref,
    step_ref,
    cum_ref,
    raw_ref,
    bias_ref,
    alog_ref,
    etot_ref,
    skip_ref,
    start_ref,
    ones_ref,
    fan_ref,
    gact_ref,
    graw_ref,
    gbias_ref,
    grate_ref,
    state,
    tails,
    early,
    first,
    second,
    third,
    spread,
    three,
):
    at = pl.program_id(0)
    step_at = blocks // GROUP - 1 - at
    inner = pairs * LANES
    width = state.shape[0]

    @pl.when(at == 0)
    def _():
        state[...] = start_ref[...]
        gbias_ref[...] = jnp.zeros_like(gbias_ref)
        grate_ref[...] = jnp.zeros_like(grate_ref)

    later = (rows_at() <= lanes_at()).astype(f32)
    earlier = (rows_at() > lanes_at()).astype(f32)
    rates = jnp.exp(alog_ref[...])
    for part, r in reversed(list(enumerate(parts_of_step()))):
        inputs, outputs = b_ref[r, :], c_ref[r, :]
        leaving = state[...]
        leaving_low = leaving.astype(bf16)
        entering = states_ref[part * width : (part + 1) * width, :]
        etot = etot_ref[pl.ds(step_at * GROUP + part, 1), :]
        held = jnp.sum(leaving * entering.astype(f32), axis=0, keepdims=True) * etot
        held = mm(jnp.broadcast_to(held, (8, inner)).astype(bf16), ones_ref[...])[0:1, :]
        spread[...] = mm(inputs, leaving_low)
        cum, step = cum_ref[r, :], step_ref[r, :]
        grow = jnp.exp(cum)
        tail = jnp.exp(cum[ROWS - 1 :, :] - cum)
        three[...] = mm(
            jnp.concatenate([halves(step, heads), halves(tail, heads), halves(grow, heads)], axis=0),
            fan_ref[...],
        )
        for i in range(pairs):
            s = slab(i)
            v = v_ref[r, s].astype(f32)
            g = g_ref[r, s].astype(f32)
            steps = three[:ROWS, s]
            x = x_ref[r, s].astype(f32)
            part_tail = three[ROWS : 2 * ROWS, s]
            more = spread[:, s] * part_tail
            dx = dx_ref[r, s] + more
            first[:, s] = (x * more).astype(bf16)
            direct = v * dx
            high = direct.astype(bf16)
            second[:, s] = high
            third[:, s] = (direct - high.astype(f32)).astype(bf16)
            gact_ref[r, s] = (steps * dx + skip_ref[:, s] * g).astype(bf16)
            tails[:, s] = (x * part_tail).astype(bf16)
            early[:, s] = (g * three[2 * ROWS :, s]).astype(bf16)
        gact_ref[r, inner : inner + width] = (db_ref[r, :] + mm_nt(tails[...], leaving_low)).astype(bf16)
        gact_ref[r, inner + width :] = (dc_ref[r, :] + mm_nt(early[...], entering)).astype(bf16)
        gdecay = (
            jnp.dot(later, pq_ref[r, :] + pac_ref[r, :], precision=highest, preferred_element_type=f32)
            + jnp.dot(
                earlier, mm(first[...], ones_ref[...]), precision=highest, preferred_element_type=f32
            )
            + held
        )
        gstep = mm(second[...], ones_ref[...]) + mm(third[...], ones_ref[...]) - rates * gdecay
        graw = gstep.astype(bf16).astype(f32) * sigmoid(raw_ref[r, :] + bias_ref[...])
        graw_ref[r, :] = graw.astype(bf16)
        gbias_ref[...] += jnp.sum(graw, axis=0, keepdims=True)
        grate_ref[...] += jnp.sum(step * gdecay, axis=0, keepdims=True)
        state[...] = etot * leaving + mm_tn(outputs, early[...])


def mixer_finish(
    act, x, gm, dx, db, dc, pq, pac, states, step, cum, raw, bias, a_log, etot, skip, start, ones, fan, heads, inner, width
):
    rows = act.shape[0]
    blocks = rows // ROWS
    inputs_at = inner // width
    channels = act.shape[1]

    def backwards(columns, height=GROUP * ROWS, column_at=0):
        return pl.BlockSpec((height, columns), lambda i: (blocks // GROUP - 1 - i, column_at))

    return pl.pallas_call(
        functools.partial(finish_kernel, heads, inner // LANES, blocks),
        grid=(blocks // GROUP,),
        in_specs=[
            backwards(inner),
            backwards(inner),
            backwards(width, column_at=inputs_at),
            backwards(width, column_at=inputs_at + 1),
            backwards(inner),
            backwards(inner),
            backwards(width),
            backwards(width),
            backwards(LANES),
            backwards(LANES),
            backwards(inner, GROUP * width),
            backwards(LANES),
            backwards(LANES),
            backwards(LANES),
            whole((1, LANES)),
            whole((1, LANES)),
            whole(etot.shape),
            whole((1, inner)),
            whole((width, inner)),
            whole((inner, LANES)),
            whole(fan.shape),
        ],
        out_specs=[backwards(channels), backwards(LANES), whole((1, LANES)), whole((1, LANES))],
        out_shape=[
            jax.ShapeDtypeStruct((rows, channels), bf16),
            jax.ShapeDtypeStruct((rows, LANES), bf16),
            jax.ShapeDtypeStruct((1, LANES), f32),
            jax.ShapeDtypeStruct((1, LANES), f32),
        ],
        scratch_shapes=[
            pltpu.VMEM((width, inner), f32),
            pltpu.VMEM((ROWS, inner), bf16),
            pltpu.VMEM((ROWS, inner), bf16),
            pltpu.VMEM((ROWS, inner), bf16),
            pltpu.VMEM((ROWS, inner), bf16),
            pltpu.VMEM((ROWS, inner), bf16),
            pltpu.VMEM((ROWS, inner), f32),
            pltpu.VMEM((3 * ROWS, inner), f32),
        ],
        compiler_params=params(),
        name="mixer_finish",
        cost_estimate=cost(16),
    )(act, x, act, act, gm, dx, db, dc, pq, pac, states, step, cum, raw, bias, a_log, etot, skip, start, ones, fan)


def conv_back_kernel(
    span, rows, blocks, cin_ref, gact_ref, graw_ref, taps_ref, bias_ref, next_ref,
    gproj_ref, gtaps_ref, gbias_ref, held, grads,
):
    part = 256
    at = pl.program_id(0)

    @pl.when(at == blocks)
    def _():
        gproj_ref[...] = graw_ref[...]

    @pl.when(at < blocks)
    def _():
        held[...] = cin_ref[...].astype(f32)
        grads[rows : rows + 8, :] = next_ref[...]
        gbias = jnp.zeros((1, LANES), f32)
        gtaps = [jnp.zeros((1, LANES), f32)] * span
        for start in range(0, rows, part):
            total = jnp.broadcast_to(bias_ref[0:1, :], (part, LANES))
            seen = []
            for k in range(span):
                first = HALO + start - (span - 1) + k
                seen.append(held[first : first + part, :])
                total = total + taps_ref[k : k + 1, :] * seen[k]
            sig = sigmoid(total)
            grad = gact_ref[start : start + part, :].astype(f32) * (sig * (1.0 + total * (1.0 - sig)))
            grads[start : start + part, :] = grad
            gbias = gbias + jnp.sum(grad, axis=0, keepdims=True)
            for k in range(span):
                gtaps[k] = gtaps[k] + jnp.sum(seen[k] * grad, axis=0, keepdims=True)
        gbias_ref[...] = gbias
        for k in range(span):
            gtaps_ref[k : k + 1, :] = gtaps[k]
        for start in range(0, rows, part):
            total = jnp.zeros((part, LANES), f32)
            for k in range(span):
                first = start + span - 1 - k
                total = total + taps_ref[k : k + 1, :] * grads[first : first + part, :]
            gproj_ref[start : start + part, :] = total.astype(bf16)


def conv_backward(cin, gact, graw, taps, bias, nexts, begin, blocks, extra):
    rows = gact.shape[0]
    span = taps.shape[0]

    def columns(height, offset=begin):
        return pl.BlockSpec((height, LANES), lambda i: (0, offset + jnp.minimum(i, blocks - 1)))

    return pl.pallas_call(
        functools.partial(conv_back_kernel, span, rows, blocks),
        grid=(blocks + extra,),
        in_specs=[
            columns(rows + HALO),
            columns(rows),
            whole((rows, LANES)),
            columns(span),
            columns(1),
            columns(8),
        ],
        out_specs=[
            pl.BlockSpec((rows, LANES), lambda i: (0, i)),
            columns(span, 0),
            columns(1, 0),
        ],
        out_shape=[
            jax.ShapeDtypeStruct((rows, (blocks + extra) * LANES), bf16),
            jax.ShapeDtypeStruct((span, blocks * LANES), f32),
            jax.ShapeDtypeStruct((1, blocks * LANES), f32),
        ],
        scratch_shapes=[pltpu.VMEM((rows + HALO, LANES), f32), pltpu.VMEM((rows + HALO, LANES), f32)],
        compiler_params=params(),
        name="conv_backward",
        cost_estimate=cost(10),
    )(cin, gact, graw, taps, bias, nexts)


def local(
    tokens,
    norm_gain,
    in_weight,
    conv_weight,
    conv_bias,
    dt_bias,
    a_log,
    skip_gain,
    gate_gain,
    out_weight,
    cotangent,
):
    tokens, incoming = tokens[0], cotangent[0]
    rows, model = tokens.shape
    heads = a_log.shape[0]
    span, channels = conv_weight.shape
    inner = gate_gain.shape[0]
    width = (channels - inner) // 2
    head_width = inner // heads
    blocks = rows // ROWS
    pad = LANES - heads

    order = gathered_order()
    conv_flight = Flight(gather(jnp.pad(in_weight[:, inner:], ((0, 0), (0, pad)))))
    before = shifted(tokens[rows - HALO :], "seq", 1)

    def first_norm(block):
        block = block.astype(f32)
        scale = lax.rsqrt(jnp.mean(block * block, axis=1, keepdims=True) + epsilon)
        return (block * scale * norm_gain).astype(bf16), scale

    own, own_scale = first_norm(tokens)
    gate_part, out_weight, own = conv_flight.step(in_weight[:, :inner], out_weight, own)
    w_gate = lax.all_gather(gate_part, "fsdp", axis=0, tiled=True)
    w_out = lax.all_gather(out_weight, "fsdp", axis=0, tiled=True)
    conv_near, conv_far = conv_flight.finish()
    act, cin, raw, conv_near, conv_far = conv_forward(
        jnp.stack([jnp.int32(at) for at in order]), first_norm(before)[0], own, conv_near, conv_far,
        conv_weight, conv_bias[None],
    )
    bias_row = jnp.pad(dt_bias, (0, pad))[None]
    alog_row = jnp.pad(a_log, (0, pad))[None]
    step, cum, left, right = steps_forward(raw, bias_row, alog_row, heads)

    totals = cum.reshape(blocks, ROWS, LANES)[:, -1, :heads]
    befores = jnp.cumsum(totals, axis=0) - totals
    etot = jnp.repeat(jnp.exp(totals), head_width, axis=1)
    ebef = jnp.repeat(jnp.exp(befores), head_width, axis=1)
    skip = jnp.repeat(skip_gain, head_width)[None]
    def fanned(count, each):
        row, column = np.arange(LANES)[:, None], np.arange(count)[None]
        return ((row < 3 * heads) & (row % heads == column // each)).astype(ml_dtypes.bfloat16)

    def gathering(count, each):
        return (np.arange(count)[:, None] // each == np.arange(LANES)[None]).astype(ml_dtypes.bfloat16)

    fan = fanned(inner, head_width)
    still = fanned(heads * LANES, LANES)
    ones = gathering(inner, head_width)
    taken = gathering(heads * LANES, LANES)
    whole_decay = jnp.repeat(jnp.exp(jnp.sum(totals, axis=0)), head_width)[None]

    x, leaves = piece_state(act, step, cum, etot, fan, heads, inner, width)
    ahead = Flight(handed_on(leaves, whole_decay, 1))
    y = inside_forward(x, act, left, right, still, inner, width)
    y = ahead.step(y)
    z = mm(own, w_gate)
    z = ahead.step(z)
    gn = mm_nt(incoming, w_out)
    gn = ahead.step(gn)
    start = ahead.finish()
    out_in, gm, gz, states, pac, back, ggain, gskip = gate_both(
        y, act, z, gn, step, cum, etot, ebef, skip, gate_gain[None], start, ones, fan, heads, inner, width
    )

    behind = Flight(handed_on(back, whole_decay, -1))
    part_out = mm_tn(out_in, incoming).astype(bf16)
    part_gate = mm_tn(own, gz).astype(bf16)
    pulled_gate = mm_nt(gz, w_gate)
    part_out, part_gate, pulled_gate = behind.step(part_out, part_gate, pulled_gate)
    sums = Flight(sum_scatter([part_out, part_gate]))
    gm = behind.step(gm)
    gm = sums.step(gm)
    dx, db, dc, pq = inside_backward(x, act, gm, left, right, still, taken, inner, width)
    dx = behind.step(dx)
    dx = sums.step(dx)
    back_start = behind.finish()
    gact, graw, gdt, grate = mixer_finish(
        act, x, gm, dx, db, dc, pq, pac, states, step, cum, raw, bias_row, alog_row, etot, skip,
        back_start, ones, fan, heads, inner, width,
    )
    top = conv_bias + jnp.zeros((8, channels), f32)
    for k in range(span):
        first = HALO - (span - 1) + k
        top = top + conv_weight[k] * cin[first : first + 8].astype(f32)
    sig = sigmoid(top)
    nexts = shifted(gact[:8].astype(f32) * (sig * (1.0 + top * (1.0 - sig))), "seq", -1)
    gproj, gtaps, gcbias = conv_backward(
        cin, gact, graw, conv_weight, conv_bias[None], nexts, 0, channels // LANES, 1
    )
    gproj = sums.step(gproj)
    part_conv = mm_tn(own, gproj).astype(bf16)
    conv_sums = Flight(sum_scatter([part_conv]))
    pulled_near = mm_nt(gproj, conv_near)
    pulled_near = conv_sums.step(pulled_near)
    pulled_far = mm_nt(gproj, conv_far)
    pulled_conv = jnp.concatenate([pulled_near, pulled_far], axis=1)
    places = [sum(jnp.where(at == block, i, 0) for i, at in enumerate(order)) for block in range(len(order))]
    grad_normed = pulled_gate + in_order(pulled_conv, places)
    unit = tokens.astype(f32) * own_scale
    pulled = grad_normed * norm_gain
    mean_pull = jnp.mean(pulled * unit, axis=1, keepdims=True)
    grad_tokens = incoming.astype(f32) + own_scale * (pulled - unit * mean_pull)
    grad_norm_gain = jnp.sum(grad_normed * unit, axis=0)
    small = [
        grad_norm_gain,
        gtaps.reshape(-1),
        gcbias[0],
        gdt[0, :heads],
        grate[0, :heads] * -jnp.exp(a_log),
        jnp.sum(gskip.reshape(heads, head_width), axis=1),
        ggain[0],
    ]
    small_sums = Flight(sum_all(jnp.concatenate(small)))
    small_sums.step()
    small_sums.flying = (conv_sums.step(*small_sums.flying),)
    small_sums.step()
    mixed = (tokens.astype(f32) + mm(out_in, w_out)).astype(bf16)
    mixed = conv_sums.step(mixed)
    mixed = sums.step(mixed)
    grad_out_weight, grad_gate_weight = sums.finish()
    (grad_conv_part,) = conv_sums.finish()
    summed = small_sums.finish()

    grad_in_weight = jnp.concatenate(
        [grad_gate_weight, grad_conv_part[:, : channels + heads]], axis=1
    )
    sizes = [part.shape[0] for part in small]
    split, at = [], 0
    for size in sizes:
        split.append(summed[at : at + size])
        at += size
    return (
        mixed[None],
        grad_tokens[None],
        grad_in_weight,
        grad_out_weight,
        split[0],
        split[1].reshape(span, channels),
        *split[2:],
    )


def solution(mesh):
    tokens = P("fsdp", "seq", None)
    sharded = P("fsdp", None)
    spread = P(("seq", "fsdp"), None)
    return jax.shard_map(
        local,
        mesh=mesh,
        in_specs=(tokens, P(), sharded, P(), P(), P(), P(), P(), P(), sharded, tokens),
        out_specs=(tokens, tokens, spread, spread, P(), P(), P(), P(), P(), P(), P()),
        check_vma=False,
    )
```

```python
import functools

import jax
import jax.numpy as jnp
import ml_dtypes
import numpy as np
from jax import lax
from jax.experimental import pallas as pl
from jax.experimental.pallas import tpu as pltpu
from jax.sharding import PartitionSpec as P

ROWS = 128
GROUP = 2
LANES = 128
HALO = 16
VMEM = 48 * 1024 * 1024
LOG2E = 1.4426950408889634
epsilon = 1e-05
bf16 = jnp.bfloat16
f32 = jnp.float32
highest = lax.Precision.HIGHEST


def shifted(block, axis, distance):
    size = lax.axis_size(axis)
    route = [(i - distance, i) for i in range(size) if 0 <= i - distance < size]
    return lax.ppermute(block, axis, route)


def exchanged(block, axis, bit):
    return lax.ppermute(block, axis, [(i, i ^ bit) for i in range(lax.axis_size(axis))])


def pick(block, at, axis):
    return lax.dynamic_index_in_dim(block, at, axis, keepdims=False)


class Flight:
    def __init__(self, steps):
        self.steps, self.value, self.flying = steps, None, None
        self.advance(None)

    def advance(self, arrived):
        try:
            self.flying = self.steps.send(arrived)
        except StopIteration as end:
            self.flying, self.value = None, end.value

    def step(self, *others):
        if self.flying is not None:
            count = len(self.flying)
            tied = lax.optimization_barrier((*self.flying, *others))
            others = tied[count:]
            self.advance(tuple(tied[:count]))
        return others[0] if len(others) == 1 else others

    def finish(self):
        while self.flying is not None:
            self.advance(self.flying)
        return self.value


def gather(weight):
    rows = weight.shape[0]
    if lax.axis_size("fsdp") != 8 or rows % 32:
        full = lax.all_gather(weight, "fsdp", axis=0, tiled=True)
        return [full[: full.shape[0] // 2]], [full[full.shape[0] // 2 :]]
    first, last = weight[: rows // 2], weight[rows // 2 :]

    def crossed(block):
        return exchanged(block, "fsdp", 1)

    first_y, last_x = exchanged(first, "fsdp", 4), exchanged(last, "fsdp", 2)
    first_x, last_y = exchanged(first, "fsdp", 2), exchanged(last, "fsdp", 4)
    far = [crossed(weight)]
    first_xy, last_xy = exchanged(first_y, "fsdp", 2), exchanged(last_x, "fsdp", 4)
    far += [crossed(block) for block in (first_x, last_x, first_y, last_y)]
    first_xy, last_xy = yield first_xy, last_xy
    far += [crossed(first_xy), crossed(last_xy)]
    return [weight, first_x, last_x, first_y, last_y, first_xy, last_xy], far


def gathered_order():
    group = lax.axis_size("fsdp")
    if group != 8:
        return list(range(group))
    me = lax.axis_index("fsdp")
    return [me ^ distance for distance in (0, 2, 4, 6, 1, 3, 5, 7)]


def in_order(block, order):
    size = block.shape[1] // len(order)
    return jnp.concatenate(
        [lax.dynamic_slice_in_dim(block, at * size, size, axis=1) for at in order], axis=1
    )


def handed_on(state, decay, distance):
    entering = jnp.zeros(state.shape, f32)
    state = state.astype(f32)
    for _ in range(lax.axis_size("seq") - 1):
        leaving = (state + decay * entering).astype(bf16)
        (arrived,) = yield (shifted(leaving, "seq", distance),)
        entering = arrived.astype(f32)
    return entering


def sum_all(vector):
    for axis in ("fsdp", "seq"):
        size = lax.axis_size(axis)
        if size & (size - 1):
            vector = lax.psum(vector, axis)
            continue
        for bit in range(size.bit_length() - 1):
            (other,) = yield (exchanged(vector, axis, 1 << bit),)
            vector = vector + other
    return vector


def sum_scatter(parts):
    pieces, group = lax.axis_size("seq"), lax.axis_size("fsdp")
    bits = group.bit_length() - 1
    rows = [part.shape[0] // (pieces * group) for part in parts]
    widths = [part.shape[1] for part in parts]
    fits = len(parts) == 2 and (rows[1] * widths[1]) % widths[0] == 0 or len(parts) == 1 and rows[0] % 2 == 0
    if group != 1 << bits or bits < 1 or not fits:
        return [
            lax.psum_scatter(part.astype(f32), ("seq", "fsdp"), scatter_dimension=0, tiled=True)
            for part in parts
        ]
    me, place = lax.axis_index("fsdp"), lax.axis_index("seq")
    parts = [part.reshape(pieces, group // 2, 2, -1, part.shape[1]) for part in parts]
    mine = me & 1
    got = yield tuple(exchanged(pick(part, 1 - mine, 2), "fsdp", 1) for part in parts)
    halves = [pick(part, mine, 2) + other for part, other in zip(parts, got)]
    if len(halves) == 1:
        halves = [halves[0][:, :, : rows[0] // 2], halves[0][:, :, rows[0] // 2 :]]
    ways = [list(range(bits - 1, 0, -1)), list(range(bits - 1, 0, -1))]
    halves = [part.reshape((pieces,) + (2,) * (bits - 1) + part.shape[2:]) for part in halves]
    for _ in range(bits - 1):
        taken = [ways[0][-1], ways[1][0]]
        places = [1 + ways[way].index(taken[way]) for way in (0, 1)]
        sides = [(me >> taken[way]) & 1 for way in (0, 1)]
        got = yield tuple(
            exchanged(pick(halves[way], 1 - sides[way], places[way]), "fsdp", 1 << taken[way])
            for way in (0, 1)
        )
        halves = [pick(halves[way], sides[way], places[way]) + got[way] for way in (0, 1)]
        for way in (0, 1):
            ways[way].remove(taken[way])
    part = jnp.concatenate([halves[0], halves[1].reshape(pieces, -1, widths[0])], axis=1)
    got = yield tuple(
        lax.ppermute(
            pick(part, (place + ahead) % pieces, 0), "seq", [(i, (i + ahead) % pieces) for i in range(pieces)]
        )
        for ahead in range(1, pieces)
    )
    own = sum((block.astype(f32) for block in got), pick(part, place, 0).astype(f32))
    if len(rows) == 1:
        return [own]
    return [own[: rows[0]], own[rows[0] :].reshape(rows[1], widths[1])]


def mm(a, b):
    return lax.dot_general(a, b, (((1,), (0,)), ((), ())), preferred_element_type=f32)


def mm_nt(a, b):
    return lax.dot_general(a, b, (((1,), (1,)), ((), ())), preferred_element_type=f32)


def mm_tn(a, b):
    return lax.dot_general(a, b, (((0,), (0,)), ((), ())), preferred_element_type=f32)


def sigmoid(v):
    return 0.5 + 0.5 * jnp.tanh(0.5 * v)


def rows_at():
    return lax.broadcasted_iota(jnp.int32, (ROWS, LANES), 0)


def lanes_at():
    return lax.broadcasted_iota(jnp.int32, (ROWS, LANES), 1)


def slab(i):
    return slice(i * LANES, (i + 1) * LANES)


def wide(i):
    return slice(i * 2 * LANES, (i + 1) * 2 * LANES)


def halves(columns, heads):
    lane = lanes_at()
    high = columns.astype(bf16).astype(f32)
    rest = pltpu.roll(columns - high, heads, 1)
    return jnp.where(lane < heads, high, jnp.where(lane < 2 * heads, rest, 0.0)).astype(bf16)


def low_lanes():
    return (lanes_at() < LANES // 2).astype(f32).astype(bf16), (lanes_at() >= LANES // 2).astype(f32).astype(bf16)


def diagonal(block, low, high):
    return jnp.concatenate([block * low, block * high], axis=0)


def parts_of_step():
    return [slice(part * ROWS, (part + 1) * ROWS) for part in range(GROUP)]


def params(**more):
    return pltpu.CompilerParams(vmem_limit_bytes=VMEM, **more)


def cost(microseconds):
    return pl.CostEstimate(flops=int(microseconds * 1e9), bytes_accessed=4 * 1024 * 1024, transcendentals=0)


def whole(shape):
    return pl.BlockSpec(shape, lambda i: (0,) * len(shape))


def by_rows(width, rows=GROUP * ROWS):
    return pl.BlockSpec((rows, width), lambda i: (i, 0))


def conv_kernel(span, rows, pieces, order_ref, before_ref, own_ref, *refs):
    near_refs, far_refs = refs[:pieces], refs[pieces : 2 * pieces]
    taps_ref, bias_ref, act_ref, cin_ref, raw_ref, near_ref, far_ref, held, normed_ref = refs[2 * pieces :]
    at = pl.program_id(0)
    last = pl.num_programs(0) - 1
    near = jnp.concatenate([ref[...] for ref in near_refs], axis=0)
    far = jnp.concatenate([ref[...] for ref in far_refs], axis=0)
    near_ref[...] = near
    far_ref[...] = far
    half = near.shape[0]
    size = own_ref.shape[1] // order_ref.shape[0]

    @pl.when(at == 0)
    def _():
        for i in range(order_ref.shape[0]):
            source = pl.ds(pl.multiple_of(order_ref[i] * size, size), size)
            normed_ref[:HALO, i * size : (i + 1) * size] = before_ref[:, source]
            normed_ref[HALO:, i * size : (i + 1) * size] = own_ref[:, source]

    def projected(start, size):
        block = normed_ref[start : start + size, :]
        return mm(block[:, :half], near) + mm(block[:, half:], far)

    part = 256

    @pl.when(at == last)
    def _():
        for start in range(0, rows, rows // 2):
            raw_ref[start : start + rows // 2, :] = projected(HALO + start, rows // 2)[:, :LANES]

    @pl.when(at < last)
    def _():
        for start, size in [(0, HALO + rows)]:
            block = projected(start, size).astype(bf16)
            cin_ref[start : start + size, :] = block
            held[start : start + size, :] = block.astype(f32)
        for start in range(0, rows, part):
            total = jnp.broadcast_to(bias_ref[0:1, :], (part, bias_ref.shape[1]))
            for k in range(span):
                first = HALO + start - (span - 1) + k
                total = total + taps_ref[k : k + 1, :] * held[first : first + part, :]
            act_ref[start : start + part, :] = (total * sigmoid(total)).astype(bf16)


def conv_forward(order, before, own, near, far, taps, bias):
    rows, width = own.shape
    channels = taps.shape[1]
    total = near[0].shape[1]
    cols = 2 * LANES
    blocks = channels // cols

    def columns(height, upto=blocks):
        return pl.BlockSpec((height, cols), lambda i: (0, jnp.minimum(i, upto)))

    return pl.pallas_call(
        functools.partial(conv_kernel, taps.shape[0], rows, len(near)),
        grid=(blocks + 1,),
        in_specs=[pl.BlockSpec(memory_space=pltpu.SMEM), whole((HALO, width)), whole((rows, width))]
        + [columns(piece.shape[0]) for piece in near + far]
        + [columns(taps.shape[0], blocks - 1), columns(1, blocks - 1)],
        out_specs=[
            columns(rows, blocks - 1),
            columns(rows + HALO, blocks - 1),
            whole((rows, LANES)),
            columns(width // 2),
            columns(width // 2),
        ],
        out_shape=[
            jax.ShapeDtypeStruct((rows, channels), bf16),
            jax.ShapeDtypeStruct((rows + HALO, channels), bf16),
            jax.ShapeDtypeStruct((rows, LANES), f32),
            jax.ShapeDtypeStruct((width // 2, total), bf16),
            jax.ShapeDtypeStruct((width // 2, total), bf16),
        ],
        scratch_shapes=[pltpu.VMEM((rows + HALO, cols), f32), pltpu.VMEM((rows + HALO, width), bf16)],
        compiler_params=params(),
        name="conv_forward",
        cost_estimate=cost(16),
    )(order, before, own, *near, *far, taps, bias)


def steps_kernel(blocks, heads, raw_ref, bias_ref, alog_ref, step_ref, cum_ref, left_ref, right_ref, rows3):
    lane = lanes_at()
    lower = (rows_at() >= lane).astype(f32)
    rates = -jnp.exp(alog_ref[...])
    rows3[...] = jnp.zeros_like(rows3)
    for b in range(blocks):
        rows = slice(b * ROWS, (b + 1) * ROWS)
        soft = raw_ref[rows, :] + bias_ref[...]
        soft = jnp.maximum(soft, 0.0) + jnp.log1p(jnp.exp(-jnp.abs(soft)))
        step = soft.astype(bf16).astype(f32)
        step_ref[rows, :] = step
        cum = jnp.dot(lower, step * rates, precision=highest, preferred_element_type=f32)
        cum_ref[rows, :] = cum
        cum = cum * LOG2E
        parts, rest = [], cum
        for _ in range(3):
            part = rest.astype(bf16).astype(f32)
            parts.append(part)
            rest = rest - part
        left = jnp.where(lane < 3 * heads + 3, 1.0, 0.0)
        for k in (2, 1, 0):
            left = jnp.where(lane < (k + 1) * heads, pltpu.roll(parts[k], k * heads, 1), left)
        left_ref[rows, :] = left.astype(bf16)
        for k in range(3):
            flipped = -parts[k].T
            for h in range(heads):
                rows3[k : k + 1, slab(h)] = flipped[h : h + 1, :]
        right_ref[b * HALO : (b + 1) * HALO, :] = rows3[...].astype(bf16)


def steps_forward(raw, bias, a_log, heads):
    rows = raw.shape[0]
    blocks = rows // ROWS
    shape = jax.ShapeDtypeStruct((rows, LANES), f32)
    return pl.pallas_call(
        functools.partial(steps_kernel, blocks, heads),
        out_shape=[
            shape,
            shape,
            jax.ShapeDtypeStruct((rows, LANES), bf16),
            jax.ShapeDtypeStruct((blocks * HALO, heads * LANES), bf16),
        ],
        scratch_shapes=[pltpu.VMEM((HALO, heads * LANES), f32)],
        compiler_params=params(),
        name="steps_forward",
        cost_estimate=cost(6),
    )(raw, bias, a_log)


def state_kernel(heads, v_ref, b_ref, step_ref, cum_ref, etot_ref, fan_ref, x_ref, f_ref, state, tails, both):
    at = pl.program_id(0)

    @pl.when(at == 0)
    def _():
        state[...] = jnp.zeros_like(state)

    for part, r in enumerate(parts_of_step()):
        cum, step = cum_ref[r, :], step_ref[r, :]
        tail = jnp.exp(cum[ROWS - 1 :, :] - cum) * step
        both[...] = mm(jnp.concatenate([halves(step, heads), halves(tail, heads)], axis=0), fan_ref[...])
        v = v_ref[r, :].astype(f32)
        x_ref[r, :] = (v * both[:ROWS, :]).astype(bf16)
        tails[...] = (v * both[ROWS:, :]).astype(bf16)
        etot = etot_ref[pl.ds(at * GROUP + part, 1), :]
        state[...] = etot * state[...] + mm_tn(b_ref[r, :], tails[...])

    @pl.when(at == pl.num_programs(0) - 1)
    def _():
        f_ref[...] = state[...].astype(bf16)


def piece_state(act, step, cum, etot, fan, heads, inner, width):
    rows = act.shape[0]
    inputs_at = inner // width
    return pl.pallas_call(
        functools.partial(state_kernel, heads),
        grid=(rows // (GROUP * ROWS),),
        in_specs=[
            by_rows(inner),
            pl.BlockSpec((GROUP * ROWS, width), lambda i: (i, inputs_at)),
            by_rows(LANES),
            by_rows(LANES),
            whole(etot.shape),
            whole(fan.shape),
        ],
        out_specs=[by_rows(inner), whole((width, inner))],
        out_shape=[
            jax.ShapeDtypeStruct((rows, inner), bf16),
            jax.ShapeDtypeStruct((width, inner), bf16),
        ],
        scratch_shapes=[
            pltpu.VMEM((width, inner), f32),
            pltpu.VMEM((ROWS, inner), bf16),
            pltpu.VMEM((2 * ROWS, inner), f32),
        ],
        compiler_params=params(),
        name="piece_state",
        cost_estimate=cost(6),
    )(act, act, step, cum, etot, fan)


def inside_kernel(pairs, x_ref, b_ref, c_ref, left_ref, right_ref, still_ref, y_ref, right):
    fixed = left_rows(right, still_ref, right_ref)
    low, high = low_lanes()
    for part, r in enumerate(parts_of_step()):
        scores = jnp.where(rows_at() >= lanes_at(), mm_nt(c_ref[r, :], b_ref[r, :]), 0.0)
        scores = jnp.concatenate([scores, scores], axis=1)
        left = left_ref[r, :]
        for i in range(pairs):
            spread = mm(left, fixed[part, :, wide(i)])
            weights = (scores * jnp.exp2(jnp.minimum(spread, 0.0))).astype(bf16)
            y_ref[r, slab(i)] = mm(weights, diagonal(x_ref[r, slab(i)], low, high))


def left_rows(right, still_ref, right_ref):
    @pl.when(pl.program_id(0) == 0)
    def _():
        for part in range(GROUP):
            right[part, :, :] = still_ref[...]

    own = still_ref.shape[0] - 2 * HALO
    for part in range(GROUP):
        right[part, own : own + HALO, :] = right_ref[part * HALO : (part + 1) * HALO, :]
    return right


def inside_forward(x, act, left, right, still, inner, width):
    rows = act.shape[0]
    inputs_at = inner // width
    return pl.pallas_call(
        functools.partial(inside_kernel, inner // LANES),
        grid=(rows // (GROUP * ROWS),),
        in_specs=[
            by_rows(inner),
            pl.BlockSpec((GROUP * ROWS, width), lambda i: (i, inputs_at)),
            pl.BlockSpec((GROUP * ROWS, width), lambda i: (i, inputs_at + 1)),
            by_rows(LANES),
            by_rows(right.shape[1], GROUP * HALO),
            whole(still.shape),
        ],
        out_specs=by_rows(inner),
        out_shape=jax.ShapeDtypeStruct((rows, inner), f32),
        scratch_shapes=[pltpu.VMEM((GROUP,) + still.shape, bf16)],
        compiler_params=params(),
        name="inside_forward",
        cost_estimate=cost(10),
    )(x, act, act, left, right, still)


def gate_kernel(
    heads,
    pairs,
    y_ref,
    v_ref,
    b_ref,
    c_ref,
    z_ref,
    gn_ref,
    step_ref,
    cum_ref,
    etot_ref,
    ebef_ref,
    skip_ref,
    gain_ref,
    start_ref,
    ones_ref,
    fan_ref,
    out_ref,
    gm_ref,
    gz_ref,
    states_ref,
    pac_ref,
    back_ref,
    ggain_ref,
    gskip_ref,
    state,
    back,
    across,
    mixer,
    gated,
    early,
    tails,
    products,
    both,
):
    at = pl.program_id(0)
    width = pairs * LANES

    @pl.when(at == 0)
    def _():
        state[...] = start_ref[...]
        back[...] = jnp.zeros_like(back)
        ggain_ref[...] = jnp.zeros_like(ggain_ref)
        gskip_ref[...] = jnp.zeros_like(gskip_ref)

    for part, r in enumerate(parts_of_step()):
        outputs = c_ref[r, :]
        entering = state[...].astype(bf16)
        states_ref[part * state.shape[0] : (part + 1) * state.shape[0], :] = entering
        across[...] = mm(outputs, entering)
        cum = cum_ref[r, :]
        grow = jnp.exp(cum)
        tail = jnp.exp(cum[ROWS - 1 :, :] - cum) * step_ref[r, :]
        both[...] = mm(jnp.concatenate([halves(grow, heads), halves(tail, heads)], axis=0), fan_ref[...])
        squares = jnp.zeros((ROWS, LANES), f32)
        meets = jnp.zeros((ROWS, LANES), f32)
        for i in range(pairs):
            s = slab(i)
            v = v_ref[r, s].astype(f32)
            ya = across[:, s] * both[:ROWS, s]
            across[:, s] = ya
            m = (y_ref[r, s] + ya + skip_ref[:, s] * v).astype(bf16)
            mixer[:, s] = m
            z = z_ref[r, s]
            product = m.astype(f32) * (z * sigmoid(z))
            gated[:, s] = product
            squares = squares + product * product
            meets = meets + gn_ref[r, s] * gain_ref[:, s] * product
            tails[:, s] = (v * both[ROWS:, s]).astype(bf16)
        scale = lax.rsqrt(jnp.sum(squares, axis=1, keepdims=True) / width + epsilon)
        pull = scale * scale * scale * (jnp.sum(meets, axis=1, keepdims=True) / width)
        for i in range(pairs):
            s = slab(i)
            v = v_ref[r, s].astype(f32)
            product = gated[:, s]
            unit = product * scale
            gain = gain_ref[:, s]
            gn = gn_ref[r, s]
            out_ref[r, s] = (unit * gain).astype(bf16)
            ggain_ref[:, s] += jnp.sum(gn * unit, axis=0, keepdims=True)
            grad = gn * gain * scale - product * pull
            z = z_ref[r, s]
            sig = sigmoid(z)
            swish = z * sig
            gm = (grad * swish).astype(bf16)
            gm_ref[r, s] = gm
            slope = sig + swish * (1.0 - sig)
            gz_ref[r, s] = (grad * mixer[:, s].astype(f32) * slope).astype(bf16)
            g = gm.astype(f32)
            gskip_ref[:, s] += jnp.sum(g * v, axis=0, keepdims=True)
            products[:, s] = (g * across[:, s]).astype(bf16)
            early[:, s] = (g * both[:ROWS, s]).astype(bf16)
        pac_ref[r, :] = mm(products[...], ones_ref[...])
        block = at * GROUP + part
        back[...] += ebef_ref[pl.ds(block, 1), :] * mm_tn(outputs, early[...])
        state[...] = etot_ref[pl.ds(block, 1), :] * state[...] + mm_tn(b_ref[r, :], tails[...])

    @pl.when(at == pl.num_programs(0) - 1)
    def _():
        back_ref[...] = back[...].astype(bf16)


def gate_both(y, act, z, gn, step, cum, etot, ebef, skip, gain, start, ones, fan, heads, inner, width):
    rows = act.shape[0]
    inputs_at = inner // width
    blocks = rows // ROWS
    return pl.pallas_call(
        functools.partial(gate_kernel, heads, inner // LANES),
        grid=(blocks // GROUP,),
        in_specs=[
            by_rows(inner),
            by_rows(inner),
            pl.BlockSpec((GROUP * ROWS, width), lambda i: (i, inputs_at)),
            pl.BlockSpec((GROUP * ROWS, width), lambda i: (i, inputs_at + 1)),
            by_rows(inner),
            by_rows(inner),
            by_rows(LANES),
            by_rows(LANES),
            whole(etot.shape),
            whole(ebef.shape),
            whole((1, inner)),
            whole((1, inner)),
            whole((width, inner)),
            whole((inner, LANES)),
            whole(fan.shape),
        ],
        out_specs=[
            by_rows(inner),
            by_rows(inner),
            by_rows(inner),
            by_rows(inner, GROUP * width),
            by_rows(LANES),
            whole((width, inner)),
            whole((1, inner)),
            whole((1, inner)),
        ],
        out_shape=[
            jax.ShapeDtypeStruct((rows, inner), bf16),
            jax.ShapeDtypeStruct((rows, inner), bf16),
            jax.ShapeDtypeStruct((rows, inner), bf16),
            jax.ShapeDtypeStruct((blocks * width, inner), bf16),
            jax.ShapeDtypeStruct((rows, LANES), f32),
            jax.ShapeDtypeStruct((width, inner), bf16),
            jax.ShapeDtypeStruct((1, inner), f32),
            jax.ShapeDtypeStruct((1, inner), f32),
        ],
        scratch_shapes=[
            pltpu.VMEM((width, inner), f32),
            pltpu.VMEM((width, inner), f32),
            pltpu.VMEM((ROWS, inner), f32),
            pltpu.VMEM((ROWS, inner), bf16),
            pltpu.VMEM((ROWS, inner), f32),
            pltpu.VMEM((ROWS, inner), bf16),
            pltpu.VMEM((ROWS, inner), bf16),
            pltpu.VMEM((ROWS, inner), bf16),
            pltpu.VMEM((2 * ROWS, inner), f32),
        ],
        compiler_params=params(),
        name="gate_both",
        cost_estimate=cost(18),
    )(y, act, act, act, z, gn, step, cum, etot, ebef, skip, gain, start, ones, fan)


def inside_back_kernel(
    pairs, x_ref, b_ref, c_ref, g_ref, left_ref, right_ref, still_ref, taken_ref,
    dx_ref, db_ref, dc_ref, pq_ref, right, moved, late,
):
    fixed = left_rows(right, still_ref, right_ref)
    lane = lanes_at()
    low, high = low_lanes()
    ones = jnp.ones((16, ROWS), bf16)
    for part, r in enumerate(parts_of_step()):
        inputs, outputs = b_ref[r, :], c_ref[r, :]
        raw_scores = mm_nt(inputs, outputs)
        scores = jnp.where(rows_at() <= lane, raw_scores, 0.0)
        strict = jnp.where(rows_at() < lane, raw_scores, 0.0)
        scores = jnp.concatenate([scores, scores], axis=1)
        strict = jnp.concatenate([strict, strict], axis=1)
        left = -left_ref[r, :]
        gathered = jnp.zeros((ROWS, 2 * LANES), f32)
        for i in range(pairs):
            spread = mm(left, fixed[part, :, wide(i)])
            decay = jnp.exp2(jnp.minimum(spread, 0.0))
            stacked = diagonal(g_ref[r, slab(i)], low, high)
            grad = mm_nt(x_ref[r, slab(i)], stacked) * decay
            gathered = gathered + grad
            moved[:, wide(i)] = (grad * strict).astype(bf16)
            dx_ref[r, slab(i)] = mm((scores * decay).astype(bf16), stacked)
        late[...] = jnp.zeros_like(late)
        for i in range(pairs):
            sums = mm(ones, moved[:, wide(i)])
            late[2 * i : 2 * i + 1, :] = sums[0:1, :LANES]
            late[2 * i + 1 : 2 * i + 2, :] = sums[0:1, LANES:]
        pq_ref[r, :] = late[...].T - mm(moved[...], taken_ref[...])
        gathered = gathered[:, :LANES] + gathered[:, LANES:]
        gathered = jnp.where(rows_at() <= lane, gathered, 0.0).astype(bf16)
        db_ref[r, :] = mm(gathered, outputs)
        dc_ref[r, :] = mm_tn(gathered, inputs)


def inside_backward(x, act, gm, left, right, still, taken, inner, width):
    rows = act.shape[0]
    inputs_at = inner // width
    return pl.pallas_call(
        functools.partial(inside_back_kernel, inner // LANES),
        grid=(rows // (GROUP * ROWS),),
        in_specs=[
            by_rows(inner),
            pl.BlockSpec((GROUP * ROWS, width), lambda i: (i, inputs_at)),
            pl.BlockSpec((GROUP * ROWS, width), lambda i: (i, inputs_at + 1)),
            by_rows(inner),
            by_rows(LANES),
            by_rows(right.shape[1], GROUP * HALO),
            whole(still.shape),
            whole(taken.shape),
        ],
        out_specs=[by_rows(inner), by_rows(width), by_rows(width), by_rows(LANES)],
        out_shape=[
            jax.ShapeDtypeStruct((rows, inner), f32),
            jax.ShapeDtypeStruct((rows, width), f32),
            jax.ShapeDtypeStruct((rows, width), f32),
            jax.ShapeDtypeStruct((rows, LANES), f32),
        ],
        scratch_shapes=[
            pltpu.VMEM((GROUP,) + still.shape, bf16),
            pltpu.VMEM((ROWS, 2 * inner), bf16),
            pltpu.VMEM((LANES, ROWS), f32),
        ],
        compiler_params=params(),
        name="inside_backward",
        cost_estimate=cost(20),
    )(x, act, act, gm, left, right, still, taken)


def finish_kernel(
    heads,
    pairs,
    blocks,
    v_ref,
    x_ref,
    b_ref,
    c_ref,
    g_ref,
    dx_ref,
    db_ref,
    dc_ref,
    pq_ref,
    pac_ref,
    states_ref,
    step_ref,
    cum_ref,
    raw_ref,
    bias_ref,
    alog_ref,
    etot_ref,
    skip_ref,
    start_ref,
    ones_ref,
    fan_ref,
    gact_ref,
    graw_ref,
    gbias_ref,
    grate_ref,
    state,
    tails,
    early,
    first,
    second,
    third,
    spread,
    three,
):
    at = pl.program_id(0)
    step_at = blocks // GROUP - 1 - at
    inner = pairs * LANES
    width = state.shape[0]

    @pl.when(at == 0)
    def _():
        state[...] = start_ref[...]
        gbias_ref[...] = jnp.zeros_like(gbias_ref)
        grate_ref[...] = jnp.zeros_like(grate_ref)

    later = (rows_at() <= lanes_at()).astype(f32)
    earlier = (rows_at() > lanes_at()).astype(f32)
    rates = jnp.exp(alog_ref[...])
    for part, r in reversed(list(enumerate(parts_of_step()))):
        inputs, outputs = b_ref[r, :], c_ref[r, :]
        leaving = state[...]
        leaving_low = leaving.astype(bf16)
        entering = states_ref[part * width : (part + 1) * width, :]
        etot = etot_ref[pl.ds(step_at * GROUP + part, 1), :]
        held = jnp.sum(leaving * entering.astype(f32), axis=0, keepdims=True) * etot
        held = mm(jnp.broadcast_to(held, (8, inner)).astype(bf16), ones_ref[...])[0:1, :]
        spread[...] = mm(inputs, leaving_low)
        cum, step = cum_ref[r, :], step_ref[r, :]
        grow = jnp.exp(cum)
        tail = jnp.exp(cum[ROWS - 1 :, :] - cum)
        three[...] = mm(
            jnp.concatenate([halves(step, heads), halves(tail, heads), halves(grow, heads)], axis=0),
            fan_ref[...],
        )
        for i in range(pairs):
            s = slab(i)
            v = v_ref[r, s].astype(f32)
            g = g_ref[r, s].astype(f32)
            steps = three[:ROWS, s]
            x = x_ref[r, s].astype(f32)
            part_tail = three[ROWS : 2 * ROWS, s]
            more = spread[:, s] * part_tail
            dx = dx_ref[r, s] + more
            first[:, s] = (x * more).astype(bf16)
            direct = v * dx
            high = direct.astype(bf16)
            second[:, s] = high
            third[:, s] = (direct - high.astype(f32)).astype(bf16)
            gact_ref[r, s] = (steps * dx + skip_ref[:, s] * g).astype(bf16)
            tails[:, s] = (x * part_tail).astype(bf16)
            early[:, s] = (g * three[2 * ROWS :, s]).astype(bf16)
        gact_ref[r, inner : inner + width] = (db_ref[r, :] + mm_nt(tails[...], leaving_low)).astype(bf16)
        gact_ref[r, inner + width :] = (dc_ref[r, :] + mm_nt(early[...], entering)).astype(bf16)
        gdecay = (
            jnp.dot(later, pq_ref[r, :] + pac_ref[r, :], precision=highest, preferred_element_type=f32)
            + jnp.dot(
                earlier, mm(first[...], ones_ref[...]), precision=highest, preferred_element_type=f32
            )
            + held
        )
        gstep = mm(second[...], ones_ref[...]) + mm(third[...], ones_ref[...]) - rates * gdecay
        graw = gstep.astype(bf16).astype(f32) * sigmoid(raw_ref[r, :] + bias_ref[...])
        graw_ref[r, :] = graw.astype(bf16)
        gbias_ref[...] += jnp.sum(graw, axis=0, keepdims=True)
        grate_ref[...] += jnp.sum(step * gdecay, axis=0, keepdims=True)
        state[...] = etot * leaving + mm_tn(outputs, early[...])


def mixer_finish(
    act, x, gm, dx, db, dc, pq, pac, states, step, cum, raw, bias, a_log, etot, skip, start, ones, fan, heads, inner, width
):
    rows = act.shape[0]
    blocks = rows // ROWS
    inputs_at = inner // width
    channels = act.shape[1]

    def backwards(columns, height=GROUP * ROWS, column_at=0):
        return pl.BlockSpec((height, columns), lambda i: (blocks // GROUP - 1 - i, column_at))

    return pl.pallas_call(
        functools.partial(finish_kernel, heads, inner // LANES, blocks),
        grid=(blocks // GROUP,),
        in_specs=[
            backwards(inner),
            backwards(inner),
            backwards(width, column_at=inputs_at),
            backwards(width, column_at=inputs_at + 1),
            backwards(inner),
            backwards(inner),
            backwards(width),
            backwards(width),
            backwards(LANES),
            backwards(LANES),
            backwards(inner, GROUP * width),
            backwards(LANES),
            backwards(LANES),
            backwards(LANES),
            whole((1, LANES)),
            whole((1, LANES)),
            whole(etot.shape),
            whole((1, inner)),
            whole((width, inner)),
            whole((inner, LANES)),
            whole(fan.shape),
        ],
        out_specs=[backwards(channels), backwards(LANES), whole((1, LANES)), whole((1, LANES))],
        out_shape=[
            jax.ShapeDtypeStruct((rows, channels), bf16),
            jax.ShapeDtypeStruct((rows, LANES), bf16),
            jax.ShapeDtypeStruct((1, LANES), f32),
            jax.ShapeDtypeStruct((1, LANES), f32),
        ],
        scratch_shapes=[
            pltpu.VMEM((width, inner), f32),
            pltpu.VMEM((ROWS, inner), bf16),
            pltpu.VMEM((ROWS, inner), bf16),
            pltpu.VMEM((ROWS, inner), bf16),
            pltpu.VMEM((ROWS, inner), bf16),
            pltpu.VMEM((ROWS, inner), bf16),
            pltpu.VMEM((ROWS, inner), f32),
            pltpu.VMEM((3 * ROWS, inner), f32),
        ],
        compiler_params=params(),
        name="mixer_finish",
        cost_estimate=cost(16),
    )(act, x, act, act, gm, dx, db, dc, pq, pac, states, step, cum, raw, bias, a_log, etot, skip, start, ones, fan)


def conv_back_kernel(
    span, rows, blocks, cin_ref, gact_ref, graw_ref, taps_ref, bias_ref, next_ref,
    gproj_ref, gtaps_ref, gbias_ref, held, grads,
):
    part = 256
    at = pl.program_id(0)

    @pl.when(at == blocks)
    def _():
        gproj_ref[...] = graw_ref[...]

    @pl.when(at < blocks)
    def _():
        held[...] = cin_ref[...].astype(f32)
        grads[rows : rows + 8, :] = next_ref[...]
        gbias = jnp.zeros((1, LANES), f32)
        gtaps = [jnp.zeros((1, LANES), f32)] * span
        for start in range(0, rows, part):
            total = jnp.broadcast_to(bias_ref[0:1, :], (part, LANES))
            seen = []
            for k in range(span):
                first = HALO + start - (span - 1) + k
                seen.append(held[first : first + part, :])
                total = total + taps_ref[k : k + 1, :] * seen[k]
            sig = sigmoid(total)
            grad = gact_ref[start : start + part, :].astype(f32) * (sig * (1.0 + total * (1.0 - sig)))
            grads[start : start + part, :] = grad
            gbias = gbias + jnp.sum(grad, axis=0, keepdims=True)
            for k in range(span):
                gtaps[k] = gtaps[k] + jnp.sum(seen[k] * grad, axis=0, keepdims=True)
        gbias_ref[...] = gbias
        for k in range(span):
            gtaps_ref[k : k + 1, :] = gtaps[k]
        for start in range(0, rows, part):
            total = jnp.zeros((part, LANES), f32)
            for k in range(span):
                first = start + span - 1 - k
                total = total + taps_ref[k : k + 1, :] * grads[first : first + part, :]
            gproj_ref[start : start + part, :] = total.astype(bf16)


def conv_backward(cin, gact, graw, taps, bias, nexts, begin, blocks, extra):
    rows = gact.shape[0]
    span = taps.shape[0]

    def columns(height, offset=begin):
        return pl.BlockSpec((height, LANES), lambda i: (0, offset + jnp.minimum(i, blocks - 1)))

    return pl.pallas_call(
        functools.partial(conv_back_kernel, span, rows, blocks),
        grid=(blocks + extra,),
        in_specs=[
            columns(rows + HALO),
            columns(rows),
            whole((rows, LANES)),
            columns(span),
            columns(1),
            columns(8),
        ],
        out_specs=[
            pl.BlockSpec((rows, LANES), lambda i: (0, i)),
            columns(span, 0),
            columns(1, 0),
        ],
        out_shape=[
            jax.ShapeDtypeStruct((rows, (blocks + extra) * LANES), bf16),
            jax.ShapeDtypeStruct((span, blocks * LANES), f32),
            jax.ShapeDtypeStruct((1, blocks * LANES), f32),
        ],
        scratch_shapes=[pltpu.VMEM((rows + HALO, LANES), f32), pltpu.VMEM((rows + HALO, LANES), f32)],
        compiler_params=params(),
        name="conv_backward",
        cost_estimate=cost(10),
    )(cin, gact, graw, taps, bias, nexts)


def local(
    tokens,
    norm_gain,
    in_weight,
    conv_weight,
    conv_bias,
    dt_bias,
    a_log,
    skip_gain,
    gate_gain,
    out_weight,
    cotangent,
):
    tokens, incoming = tokens[0], cotangent[0]
    rows, model = tokens.shape
    heads = a_log.shape[0]
    span, channels = conv_weight.shape
    inner = gate_gain.shape[0]
    width = (channels - inner) // 2
    head_width = inner // heads
    blocks = rows // ROWS
    pad = LANES - heads

    order = gathered_order()
    conv_flight = Flight(gather(jnp.pad(in_weight[:, inner:], ((0, 0), (0, pad)))))
    before = shifted(tokens[rows - HALO :], "seq", 1)

    def first_norm(block):
        block = block.astype(f32)
        scale = lax.rsqrt(jnp.mean(block * block, axis=1, keepdims=True) + epsilon)
        return (block * scale * norm_gain).astype(bf16), scale

    own, own_scale = first_norm(tokens)
    gate_part, out_weight = conv_flight.step(in_weight[:, :inner], out_weight)
    w_gate = lax.all_gather(gate_part, "fsdp", axis=0, tiled=True)
    w_out = lax.all_gather(out_weight, "fsdp", axis=0, tiled=True)
    conv_near, conv_far = conv_flight.finish()
    act, cin, raw, conv_near, conv_far = conv_forward(
        jnp.stack([jnp.int32(at) for at in order]), first_norm(before)[0], own, conv_near, conv_far,
        conv_weight, conv_bias[None],
    )
    bias_row = jnp.pad(dt_bias, (0, pad))[None]
    alog_row = jnp.pad(a_log, (0, pad))[None]
    step, cum, left, right = steps_forward(raw, bias_row, alog_row, heads)

    totals = cum.reshape(blocks, ROWS, LANES)[:, -1, :heads]
    befores = jnp.cumsum(totals, axis=0) - totals
    etot = jnp.repeat(jnp.exp(totals), head_width, axis=1)
    ebef = jnp.repeat(jnp.exp(befores), head_width, axis=1)
    skip = jnp.repeat(skip_gain, head_width)[None]
    def fanned(count, each):
        row, column = np.arange(LANES)[:, None], np.arange(count)[None]
        return ((row < 3 * heads) & (row % heads == column // each)).astype(ml_dtypes.bfloat16)

    def gathering(count, each):
        return (np.arange(count)[:, None] // each == np.arange(LANES)[None]).astype(ml_dtypes.bfloat16)

    fan = fanned(inner, head_width)
    still = fanned(heads * LANES, LANES)
    ones = gathering(inner, head_width)
    taken = gathering(heads * LANES, LANES)
    whole_decay = jnp.repeat(jnp.exp(jnp.sum(totals, axis=0)), head_width)[None]

    x, leaves = piece_state(act, step, cum, etot, fan, heads, inner, width)
    ahead = Flight(handed_on(leaves, whole_decay, 1))
    y = inside_forward(x, act, left, right, still, inner, width)
    y = ahead.step(y)
    z = mm(own, w_gate)
    z = ahead.step(z)
    gn = mm_nt(incoming, w_out)
    gn = ahead.step(gn)
    start = ahead.finish()
    out_in, gm, gz, states, pac, back, ggain, gskip = gate_both(
        y, act, z, gn, step, cum, etot, ebef, skip, gate_gain[None], start, ones, fan, heads, inner, width
    )

    behind = Flight(handed_on(back, whole_decay, -1))
    part_out = mm_tn(out_in, incoming).astype(bf16)
    part_gate = mm_tn(own, gz).astype(bf16)
    pulled_gate = mm_nt(gz, w_gate)
    part_out, part_gate, pulled_gate = behind.step(part_out, part_gate, pulled_gate)
    sums = Flight(sum_scatter([part_out, part_gate]))
    gm = sums.step(gm)
    gm = behind.step(gm)
    dx, db, dc, pq = inside_backward(x, act, gm, left, right, still, taken, inner, width)
    dx = behind.step(dx)
    dx = sums.step(dx)
    back_start = behind.finish()
    gact, graw, gdt, grate = mixer_finish(
        act, x, gm, dx, db, dc, pq, pac, states, step, cum, raw, bias_row, alog_row, etot, skip,
        back_start, ones, fan, heads, inner, width,
    )
    top = conv_bias + jnp.zeros((8, channels), f32)
    for k in range(span):
        first = HALO - (span - 1) + k
        top = top + conv_weight[k] * cin[first : first + 8].astype(f32)
    sig = sigmoid(top)
    nexts = shifted(gact[:8].astype(f32) * (sig * (1.0 + top * (1.0 - sig))), "seq", -1)
    gproj, gtaps, gcbias = conv_backward(
        cin, gact, graw, conv_weight, conv_bias[None], nexts, 0, channels // LANES, 1
    )
    gproj = sums.step(gproj)
    part_conv = mm_tn(own, gproj).astype(bf16)
    conv_sums = Flight(sum_scatter([part_conv]))
    pulled_near = mm_nt(gproj, conv_near)
    pulled_near = conv_sums.step(pulled_near)
    pulled_far = mm_nt(gproj, conv_far)
    pulled_conv = jnp.concatenate([pulled_near, pulled_far], axis=1)
    places = [sum(jnp.where(at == block, i, 0) for i, at in enumerate(order)) for block in range(len(order))]
    grad_normed = pulled_gate + in_order(pulled_conv, places)
    unit = tokens.astype(f32) * own_scale
    pulled = grad_normed * norm_gain
    mean_pull = jnp.mean(pulled * unit, axis=1, keepdims=True)
    grad_tokens = incoming.astype(f32) + own_scale * (pulled - unit * mean_pull)
    grad_norm_gain = jnp.sum(grad_normed * unit, axis=0)
    small = [
        grad_norm_gain,
        gtaps.reshape(-1),
        gcbias[0],
        gdt[0, :heads],
        grate[0, :heads] * -jnp.exp(a_log),
        jnp.sum(gskip.reshape(heads, head_width), axis=1),
        ggain[0],
    ]
    small_sums = Flight(sum_all(jnp.concatenate(small)))
    small_sums.step()
    small_sums.flying = (conv_sums.step(*small_sums.flying),)
    small_sums.step()
    mixed = (tokens.astype(f32) + mm(out_in, w_out)).astype(bf16)
    mixed = conv_sums.step(mixed)
    mixed = sums.step(mixed)
    grad_out_weight, grad_gate_weight = sums.finish()
    (grad_conv_part,) = conv_sums.finish()
    summed = small_sums.finish()

    grad_in_weight = jnp.concatenate(
        [grad_gate_weight, grad_conv_part[:, : channels + heads]], axis=1
    )
    sizes = [part.shape[0] for part in small]
    split, at = [], 0
    for size in sizes:
        split.append(summed[at : at + size])
        at += size
    return (
        mixed[None],
        grad_tokens[None],
        grad_in_weight,
        grad_out_weight,
        split[0],
        split[1].reshape(span, channels),
        *split[2:],
    )


def solution(mesh):
    tokens = P("fsdp", "seq", None)
    sharded = P("fsdp", None)
    spread = P(("seq", "fsdp"), None)
    return jax.shard_map(
        local,
        mesh=mesh,
        in_specs=(tokens, P(), sharded, P(), P(), P(), P(), P(), P(), sharded, tokens),
        out_specs=(tokens, tokens, spread, spread, P(), P(), P(), P(), P(), P(), P()),
        check_vma=False,
    )
```
